32 devices in a mesh: fsdp: 8 (over z, y), tp: 4 (over x, core).
Axes of the slice: x: 2, y: 2, z: 4, core: 2. Of those that a mesh axis runs over, the one named last changes fastest.
Arguments:
- tokens: bfloat16 [8192, 1024], P(('fsdp', 'tp')), may hold values from -6 to 6
- segment_ids: int32 [8192], P('fsdp'), may hold values from 0 to 127, as said below
- cotangent: bfloat16 [8192, 1024], P(('fsdp', 'tp')), may hold values from -6 to 6
- norm_gain: float32 [1024], P(('fsdp', 'tp')), may hold values from 0.5 to 1.5
- w_z: float32 [1024, 1536], P('fsdp', 'tp'), may hold values from -0.09375 to 0.09375, as said below
- w_x: float32 [1024, 1536], P('fsdp', 'tp'), may hold values from -0.09375 to 0.09375, as said below
- w_bc: float32 [1024, 256], P(('fsdp', 'tp')), may hold values from -0.09375 to 0.09375, as said below
- w_dt: float32 [1024, 24], P('fsdp', 'tp'), may hold values from -0.09375 to 0.09375, as said below
- conv_x: float32 [1536, 4], P('tp'), may hold values from -3 to 3
- conv_bias_x: float32 [1536], P('tp'), may hold values from -1.75 to 1.75
- conv_bc: float32 [256, 4], P(('fsdp', 'tp')), may hold values from -3 to 3
- conv_bias_bc: float32 [256], P(('fsdp', 'tp')), may hold values from -1.75 to 1.75
- dt_bias: float32 [24], P('tp'), may hold values from -6 to -2
- a_log: float32 [24], P('tp'), may hold values from 0 to 2.75
- d_skip: float32 [24], P('tp'), may hold values from 0.5 to 1.5
- mixer_gain: float32 [1536], P('tp'), may hold values from 0.5 to 1.5
- w_mixer_out: float32 [1536, 1024], P('tp', 'fsdp'), may hold values from -0.15625 to 0.15625
- w_query: float32 [1024, 512], P('fsdp', 'tp'), may hold values from -0.09375 to 0.09375, as said below
- w_keyval: float32 [1024, 256], P(('fsdp', 'tp')), may hold values from -0.09375 to 0.09375, as said below
- w_attn_out: float32 [512, 1024], P('tp', 'fsdp'), may hold values from -0.75 to 0.75
- ffn_gain: float32 [1024], P(('fsdp', 'tp')), may hold values from 0.5 to 1.5
- w_gate: float32 [1024, 2048], P('fsdp', 'tp'), may hold values from -0.1875 to 0.1875
- w_up: float32 [1024, 2048], P('fsdp', 'tp'), may hold values from -0.1875 to 0.1875
- w_down: float32 [2048, 1024], P('tp', 'fsdp'), may hold values from -0.125 to 0.125
Outputs:
- layer_out: bfloat16 [8192, 1024], P(('fsdp', 'tp'))
- grad_tokens: float32 [8192, 1024], P(('fsdp', 'tp'))
- grad_norm_gain: float32 [1024], P(('fsdp', 'tp'))
- grad_w_z: float32 [1024, 1536], P('fsdp', 'tp')
- grad_w_x: float32 [1024, 1536], P('fsdp', 'tp')
- grad_w_bc: float32 [1024, 256], P(('fsdp', 'tp'))
- grad_w_dt: float32 [1024, 24], P('fsdp', 'tp')
- grad_conv_x: float32 [1536, 4], P('tp')
- grad_conv_bias_x: float32 [1536], P('tp')
- grad_conv_bc: float32 [256, 4], P(('fsdp', 'tp'))
- grad_conv_bias_bc: float32 [256], P(('fsdp', 'tp'))
- grad_dt_bias: float32 [24], P('tp')
- grad_a_log: float32 [24], P('tp')
- grad_d_skip: float32 [24], P('tp')
- grad_mixer_gain: float32 [1536], P('tp')
- grad_w_mixer_out: float32 [1536, 1024], P('tp', 'fsdp')
- grad_w_query: float32 [1024, 512], P('fsdp', 'tp')
- grad_w_keyval: float32 [1024, 256], P(('fsdp', 'tp'))
- grad_w_attn_out: float32 [512, 1024], P('tp', 'fsdp')
- grad_ffn_gain: float32 [1024], P(('fsdp', 'tp'))
- grad_w_gate: float32 [1024, 2048], P('fsdp', 'tp')
- grad_w_up: float32 [1024, 2048], P('fsdp', 'tp')
- grad_w_down: float32 [2048, 1024], P('tp', 'fsdp')
The draws below stay inside these ranges and needn't reach their ends.
Inputs may be any that keep to these rules, and one draw needn't show every extreme that they name: `segment_ids`: within each sequence of 1024 tokens the ids start at 0 and rise by 0 or 1 from one token to the next; they rise only at positions that are multiples of 8 within the sequence. `w_z`: independent entries of deviation 1024^-0.5. `w_x`: independent entries of deviation 1024^-0.5. `w_bc`: independent entries of deviation 1024^-0.5. `w_dt`: independent entries of deviation 1024^-0.5. `w_query`: independent entries of deviation 1024^-0.5. `w_keyval`: independent entries of deviation 1024^-0.5.
All inputs are finite; a program needn't handle non-finite values.
Results may differ from the reference program's by a relative error of at most 0.025.
Values may be sent and summed in bfloat16 or wider, within the bound.
No kernel may reach another device: no remote copies, remote signals or barrier semaphores. Data moves between devices by JAX's collectives and lax.ppermute only.
A program may use at most 192 MiB of HBM per device.

```python
import jax
import jax.numpy as jnp
from jax import lax

D = 1024
MAMBA_HEADS = 24
MAMBA_HEAD = 64
STATE = 128
CONV = 4
HEADS = 8
KV_HEADS = 2
HEAD = 64
FF = 2048
SEQ = 1024
SEQS = 1
DS = 1536
TOKENS = 8192
N_FSDP = 8
N_TP = 4


def draw_segment_ids(key, part):
    key = jax.random.fold_in(key, 7)
    seq_total = TOKENS // SEQ
    block_count = SEQ // 8
    rate_key, mark_key, pick_key = jax.random.split(key, 3)
    levels = jax.random.randint(rate_key, (seq_total, 1), 0, 4)
    picked = jax.random.randint(pick_key, (), 0, seq_total)
    levels = jnp.where(jnp.arange(seq_total)[:, None] == picked, 0, levels)
    spans = jnp.left_shift(1, 2 * levels)
    mark_draws = jax.random.randint(mark_key, (seq_total, block_count), 0, 1 << 20)
    block_start = (mark_draws % spans == 0) & (jnp.arange(block_count)[None, :] > 0)
    places = jnp.arange(SEQ)
    starts = block_start[:, places // 8] & (places % 8 == 0)[None, :]
    return jnp.cumsum(starts.astype(jnp.int32), axis=1).reshape(TOKENS).astype(jnp.int32)


def drawn_matrix(key, rows_count, cols_count, fan_count):
    deviation = float(fan_count) ** (-0.5)
    return jax.random.truncated_normal(key, -3.0, 3.0, (rows_count, cols_count), jnp.float32) * deviation


def draw_w_z(key, part):
    key = jax.random.fold_in(key, 11)
    return drawn_matrix(key, D, DS, D)


def draw_w_x(key, part):
    key = jax.random.fold_in(key, 13)
    return drawn_matrix(key, D, DS, D)


def draw_w_bc(key, part):
    key = jax.random.fold_in(key, 17)
    return drawn_matrix(key, D, 2 * STATE, D)


def draw_w_dt(key, part):
    key = jax.random.fold_in(key, 19)
    return drawn_matrix(key, D, MAMBA_HEADS, D)


def draw_w_query(key, part):
    key = jax.random.fold_in(key, 23)
    return drawn_matrix(key, D, HEADS * HEAD, D)


def draw_w_keyval(key, part):
    key = jax.random.fold_in(key, 29)
    return drawn_matrix(key, D, 2 * KV_HEADS * HEAD, D)


def steps_of(key, shape, cuts, smallest, high):
    loudness, own = 1.0, jax.random.fold_in(key, 6)
    for dim, shards_of in cuts:
        draws = jnp.exp(jax.random.uniform(jax.random.fold_in(own, dim), (shards_of,), jnp.float32, smallest / len(cuts), high / len(cuts)))
        loudness = loudness * jnp.repeat(draws, shape[dim] // shards_of).reshape([-1 if axis == dim else 1 for axis in range(len(shape))])
    return loudness


def scatter_about(key, extent, scale, most, cuts=(), kind=jnp.bfloat16):
    values = scale * jax.random.normal(key, extent, jnp.float32)
    if cuts:
        values = values * steps_of(key, extent, cuts, -0.22, 0.18)
    return jnp.clip(values, -most, most).astype(kind)


def setup_inputs(seed: int = 0) -> dict:
    splits = jax.random.split(jax.random.key(seed), 25)
    tokens = scatter_about(splits[0], (TOKENS, D), 1.0, 6.0, ((0, 32),))
    segment_ids = draw_segment_ids(jax.random.fold_in(splits[24], 71), 0)
    cotangent = scatter_about(splits[2], (TOKENS, D), 1.0, 6.0, ((0, 32),))
    norm_gain = jnp.clip(1.0 + 0.1 * jax.random.normal(splits[3], (D,), jnp.float32), 0.5, 1.5)
    w_z = draw_w_z(jax.random.fold_in(splits[24], 71), 0)
    w_x = draw_w_x(jax.random.fold_in(splits[24], 71), 0)
    w_bc = draw_w_bc(jax.random.fold_in(splits[24], 71), 0)
    w_dt = draw_w_dt(jax.random.fold_in(splits[24], 71), 0)
    conv_x = scatter_about(splits[8], (DS, CONV), CONV ** -0.5, 3.0, ((0, 4),), jnp.float32)
    conv_bias_x = scatter_about(splits[9], (DS,), 0.3, 1.75, ((0, 4),), jnp.float32)
    conv_bc = scatter_about(splits[10], (2 * STATE, CONV), CONV ** -0.5, 3.0, ((0, 32),), jnp.float32)
    conv_bias_bc = scatter_about(splits[11], (2 * STATE,), 0.3, 1.75, ((0, 32),), jnp.float32)
    dt_bias = jnp.clip(-6.0 + 4.0 * jax.random.uniform(splits[12], (MAMBA_HEADS,), jnp.float32) ** steps_of(splits[12], (MAMBA_HEADS,), ((0, 4),), -0.2, 0.2), -6.0, -2.0)
    a_log = jnp.clip(2.75 * jax.random.uniform(splits[13], (MAMBA_HEADS,), jnp.float32) ** steps_of(splits[13], (MAMBA_HEADS,), ((0, 4),), -0.2, 0.2), 0.0, 2.75)
    d_skip = jnp.clip(0.5 + 1.0 * jax.random.uniform(splits[14], (MAMBA_HEADS,), jnp.float32) ** steps_of(splits[14], (MAMBA_HEADS,), ((0, 4),), -0.2, 0.2), 0.5, 1.5)
    mixer_gain = jnp.clip(1.0 + 0.1 * jax.random.normal(splits[15], (DS,), jnp.float32), 0.5, 1.5)
    w_mixer_out = scatter_about(splits[16], (DS, D), DS ** -0.5, 0.15625, ((0, 4), (1, 8)), jnp.float32)
    w_query = draw_w_query(jax.random.fold_in(splits[24], 71), 0)
    w_keyval = draw_w_keyval(jax.random.fold_in(splits[24], 71), 0)
    w_attn_out = scatter_about(splits[19], (HEADS * HEAD, D), HEAD ** -0.5, 0.75, ((0, 4), (1, 8)), jnp.float32)
    ffn_gain = jnp.clip(1.0 + 0.1 * jax.random.normal(splits[20], (D,), jnp.float32), 0.5, 1.5)
    w_gate = scatter_about(splits[21], (D, FF), D ** -0.5, 0.1875, ((0, 8), (1, 4)), jnp.float32)
    w_up = scatter_about(splits[22], (D, FF), D ** -0.5, 0.1875, ((0, 8), (1, 4)), jnp.float32)
    w_down = scatter_about(splits[23], (FF, D), FF ** -0.5, 0.125, ((0, 4), (1, 8)), jnp.float32)
    return dict(tokens=tokens, segment_ids=segment_ids, cotangent=cotangent, norm_gain=norm_gain, w_z=w_z, w_x=w_x, w_bc=w_bc, w_dt=w_dt, conv_x=conv_x, conv_bias_x=conv_bias_x, conv_bc=conv_bc, conv_bias_bc=conv_bias_bc, dt_bias=dt_bias, a_log=a_log, d_skip=d_skip, mixer_gain=mixer_gain, w_mixer_out=w_mixer_out, w_query=w_query, w_keyval=w_keyval, w_attn_out=w_attn_out, ffn_gain=ffn_gain, w_gate=w_gate, w_up=w_up, w_down=w_down)


EPS = 1e-06
ROPE_BASE = 10000.0
NEG_FILL = -1e+30
PRECISE = lax.Precision.HIGHEST

@jax.custom_vjp
def low(v):
    return lax.optimization_barrier(v.astype(jnp.bfloat16)).astype(jnp.float32)

@jax.custom_vjp
def low_back(v):
    return v

def low_keep(v):
    return (low(v), None)

def low_pass(kept, grad):
    return (grad,)

def back_keep(v):
    return (v, None)

def back_low(kept, grad):
    return (low(grad),)
low.defvjp(low_keep, low_pass)
low_back.defvjp(back_keep, back_low)

def matmul(left_side, right_side):
    return jnp.dot(left_side, right_side, precision=PRECISE, preferred_element_type=jnp.float32)

def rms_scale(rows_in, gain_vec):
    inverse = lax.rsqrt(lax.optimization_barrier(jnp.mean(rows_in * rows_in, axis=-1, keepdims=True)) + EPS)
    return rows_in * inverse * gain_vec

def sequence_tables(seg_ids):
    length = seg_ids.shape[0]
    places = jnp.arange(length, dtype=jnp.int32)
    before = jnp.roll(seg_ids, 1)
    starts = jnp.where((places == 0) | (seg_ids != before), places, 0)
    position = places - lax.cummax(starts, axis=0)
    half_dim = HEAD // 2
    frequency = jnp.exp(-jnp.log(ROPE_BASE) * jnp.arange(half_dim, dtype=jnp.float32) / half_dim)
    angles = position.astype(jnp.float32)[:, None] * frequency[None, :]
    cosine = jnp.cos(angles)[:, None, :]
    sine_vals = jnp.sin(angles)[:, None, :]
    causal = (seg_ids[:, None] == seg_ids[None, :]) & (places[:, None] >= places[None, :])
    conv_keep = [((places >= lag_step) & (seg_ids == jnp.roll(seg_ids, lag_step)))[:, None] for lag_step in range(1, CONV)]
    return (cosine, sine_vals, causal, conv_keep)

def rotate(values, cosine, sine_vals):
    half_dim = values.shape[-1] // 2
    first_half = values[..., :half_dim]
    second_half = values[..., half_dim:]
    return jnp.concatenate([first_half * cosine - second_half * sine_vals, second_half * cosine + first_half * sine_vals], axis=-1)

def causal_conv(values, kernel, offset, conv_keep):
    kernel_len = kernel.shape[1]
    summed = values * kernel[:, kernel_len - 1] + offset
    for lag_step in range(1, kernel_len):
        shifted = jnp.concatenate([jnp.zeros((lag_step, values.shape[1]), values.dtype), values[:-lag_step]], axis=0)
        summed = summed + jnp.where(conv_keep[lag_step - 1], shifted, 0.0) * kernel[:, kernel_len - 1 - lag_step]
    return summed

def decay_table(log_rates, causal):
    running = jnp.cumsum(log_rates, axis=0).T
    spread = jnp.where(causal[None], running[:, :, None] - running[:, None, :], 0.0)
    return jnp.where(causal[None], jnp.exp(spread), 0.0)

def prepare(conv_in, state_in, step_in, kernel_x, offset_x, kernel_bc, offset_bc, step_bias, rate_log, conv_keep, causal):
    mixer_in = jax.nn.silu(causal_conv(conv_in, kernel_x, offset_x, conv_keep))
    state_act = jax.nn.silu(causal_conv(state_in, kernel_bc, offset_bc, conv_keep))
    step_size = jax.nn.softplus(step_in + step_bias)
    return (mixer_in, state_act, step_size, decay_table(-step_size * jnp.exp(rate_log), causal))

def finish(scan_out, mixed_vals, skip_vec, gate_in, gain_vec):
    seq_len, head_count, head_dim = scan_out.shape
    combined = scan_out + skip_vec[None, :, None] * mixed_vals
    gated_vals = combined * jax.nn.silu(gate_in).reshape(seq_len, head_count, head_dim)
    inverse = lax.rsqrt(lax.optimization_barrier(jnp.mean(gated_vals * gated_vals, axis=(1, 2), keepdims=True)) + EPS)
    return (gated_vals * inverse * gain_vec.reshape(head_count, head_dim)).reshape(seq_len, head_count * head_dim)

def token_mixing(normed, seg_ids, params):
    norm_gain, w_z, w_x, w_bc, w_dt, conv_x, conv_bias_x, conv_bc, conv_bias_bc, dt_bias, a_log, d_skip, mixer_gain, w_mixer_out, w_query, w_keyval, w_attn_out, ffn_gain, w_gate, w_up, w_down = params
    cosine, sine_vals, causal, conv_keep = sequence_tables(seg_ids)
    seq_len = normed.shape[0]
    channels = DS // N_TP
    mamba_local = MAMBA_HEADS // N_TP
    query_local = HEADS // N_TP
    group_size = HEADS // KV_HEADS
    kernel_bc = low(conv_bc)
    offset_bc = low(conv_bias_bc)
    summed = jnp.zeros((seq_len, D), jnp.float32)
    for member in range(N_TP):
        chan_cols = slice(member * channels, (member + 1) * channels)
        head_cols = slice(member * mamba_local, (member + 1) * mamba_local)
        query_cols = slice(member * query_local * HEAD, (member + 1) * query_local * HEAD)
        kv_head = member * query_local // group_size
        gate_in = low_back(matmul(normed, low(w_z)[:, chan_cols]))
        conv_in = low_back(matmul(normed, low(w_x)[:, chan_cols]))
        state_in = low_back(matmul(normed, low(w_bc)))
        step_in = low_back(matmul(normed, low(w_dt)[:, head_cols]))
        mixer_in, state_act, step_size, decays = prepare(conv_in, state_in, step_in, conv_x[chan_cols], conv_bias_x[chan_cols], kernel_bc, offset_bc, dt_bias[head_cols], a_log[head_cols], conv_keep, causal)
        mixed_vals = low(mixer_in).reshape(seq_len, mamba_local, MAMBA_HEAD)
        state_vals = low(state_act)
        gram_mat = low_back(matmul(state_vals[:, STATE:], state_vals[:, :STATE].T))
        weights_mat = low(gram_mat[None] * decays)
        inputs_mat = low(step_size[:, :, None] * mixed_vals)
        scan_out = low_back(jnp.einsum('hts,shp->thp', weights_mat, inputs_mat, precision=PRECISE))
        mamba_out = low(finish(scan_out, mixed_vals, d_skip[head_cols], gate_in, mixer_gain[chan_cols]))
        query_raw = low_back(matmul(normed, low(w_query)[:, query_cols])).reshape(seq_len, query_local, HEAD)
        key_raw = low_back(matmul(normed, low(w_keyval)[:, kv_head * HEAD:(kv_head + 1) * HEAD]))
        value_raw = low_back(matmul(normed, low(w_keyval)[:, (KV_HEADS + kv_head) * HEAD:(KV_HEADS + kv_head + 1) * HEAD]))
        queries = low(rotate(query_raw, cosine, sine_vals))
        keys_rot = low(rotate(key_raw[:, None, :], cosine, sine_vals))[:, 0]
        values_in = low(value_raw)
        scores = low_back(jnp.einsum('thd,sd->hts', queries, keys_rot, precision=PRECISE) * HEAD ** (-0.5))
        probs_mat = jax.nn.softmax(jnp.where(causal[None], scores, NEG_FILL), axis=-1)
        attended = jnp.einsum('hts,sd->thd', low(probs_mat), values_in, precision=PRECISE)
        attn_out = low(low_back(attended)).reshape(seq_len, query_local * HEAD)
        summed = summed + matmul(mamba_out, low(w_mixer_out)[chan_cols]) + matmul(attn_out, low(w_attn_out)[query_cols])
    return summed

def layer(tok_rows, seg_ids, params):
    norm_gain = params[0]
    ffn_gain = params[17]
    w_gate = params[18]
    w_up = params[19]
    w_down = params[20]
    normed = low(rms_scale(tok_rows, low(norm_gain)))
    seq_count = tok_rows.shape[0] // SEQ

    def one_sequence(pair_in):
        return token_mixing(pair_in[0], pair_in[1], params)
    mixed = lax.map(jax.checkpoint(one_sequence), (normed.reshape(seq_count, SEQ, D), seg_ids.reshape(seq_count, SEQ)))
    after_mix = tok_rows + low_back(mixed.reshape(seq_count * SEQ, D))
    ffn_in = low(rms_scale(after_mix, low(ffn_gain)))
    gate_out = low_back(matmul(ffn_in, low(w_gate)))
    up_out = low_back(matmul(ffn_in, low(w_up)))
    hidden = low(jax.nn.silu(gate_out) * up_out)
    return after_mix + low_back(matmul(hidden, low(w_down)))

def reference(tokens, segment_ids, cotangent, norm_gain, w_z, w_x, w_bc, w_dt, conv_x, conv_bias_x, conv_bc, conv_bias_bc, dt_bias, a_log, d_skip, mixer_gain, w_mixer_out, w_query, w_keyval, w_attn_out, ffn_gain, w_gate, w_up, w_down):
    params = (norm_gain, w_z, w_x, w_bc, w_dt, conv_x, conv_bias_x, conv_bc, conv_bias_bc, dt_bias, a_log, d_skip, mixer_gain, w_mixer_out, w_query, w_keyval, w_attn_out, ffn_gain, w_gate, w_up, w_down)
    group_rows = SEQS * SEQ
    tok_blocks = tokens.astype(jnp.float32).reshape(N_FSDP, group_rows, D)
    seg_blocks = segment_ids.reshape(N_FSDP, group_rows)
    cot_blocks = cotangent.astype(jnp.float32).reshape(N_FSDP, group_rows, D)

    def step_fn(carry_grads, block_in):
        tok_rows, seg_ids, cot_rows = block_in

        def local_layer(rows_in, param_in):
            return layer(rows_in, seg_ids, param_in)
        result, pull_back = jax.vjp(local_layer, tok_rows, params)
        grad_rows, grad_params = pull_back(cot_rows)
        return (jax.tree.map(jnp.add, carry_grads, grad_params), (result.astype(jnp.bfloat16), grad_rows))
    zero_grads = jax.tree.map(jnp.zeros_like, params)
    totals, stacked = lax.scan(step_fn, zero_grads, (tok_blocks, seg_blocks, cot_blocks))
    return (stacked[0].reshape(TOKENS, D), stacked[1].reshape(TOKENS, D), totals[0], totals[1], totals[2], totals[3], totals[4], totals[5], totals[6], totals[7], totals[8], totals[9], totals[10], totals[11], totals[12], totals[13], totals[14], totals[15], totals[16], totals[17], totals[18], totals[19], totals[20])
```

```python
import jax
import jax.numpy as jnp
from jax import lax
from jax.sharding import PartitionSpec as P

STATE = 128
CONV = 4
HEADS = 8
KV_HEADS = 2
HEAD = 64
SEQ = 1024


EPS = 1e-06
ROPE_BASE = 10000.0
NEG_FILL = -1e30


def sequence_tables(seg_ids):
    length = seg_ids.shape[0]
    places = jnp.arange(length, dtype=jnp.int32)
    before = jnp.roll(seg_ids, 1)
    starts = jnp.where((places == 0) | (seg_ids != before), places, 0)
    position = places - lax.cummax(starts, axis=0)
    half_dim = HEAD // 2
    frequency = jnp.exp(-jnp.log(ROPE_BASE) * jnp.arange(half_dim, dtype=jnp.float32) / half_dim)
    angles = position.astype(jnp.float32)[:, None] * frequency[None, :]
    cosine = jnp.cos(angles)[:, None, :]
    sine_vals = jnp.sin(angles)[:, None, :]
    causal = (seg_ids[:, None] == seg_ids[None, :]) & (places[:, None] >= places[None, :])
    conv_keep = [
        ((places >= lag_step) & (seg_ids == jnp.roll(seg_ids, lag_step)))[:, None]
        for lag_step in range(1, CONV)
    ]
    return (cosine, sine_vals, causal, conv_keep)


def rotate(values, cosine, sine_vals):
    half_dim = values.shape[-1] // 2
    first_half = values[..., :half_dim]
    second_half = values[..., half_dim:]
    return jnp.concatenate(
        [
            first_half * cosine - second_half * sine_vals,
            second_half * cosine + first_half * sine_vals,
        ],
        axis=-1,
    )


def causal_conv(values, kernel, offset, conv_keep):
    kernel_len = kernel.shape[1]
    summed = values * kernel[:, kernel_len - 1] + offset
    for lag_step in range(1, kernel_len):
        shifted = jnp.concatenate(
            [jnp.zeros((lag_step, values.shape[1]), values.dtype), values[:-lag_step]], axis=0
        )
        summed = (
            summed
            + jnp.where(conv_keep[lag_step - 1], shifted, 0.0)
            * kernel[:, kernel_len - 1 - lag_step]
        )
    return summed


def decay_table(log_rates, causal):
    running = jnp.cumsum(log_rates, axis=0).T
    spread = jnp.where(causal[None], running[:, :, None] - running[:, None, :], 0.0)
    return jnp.where(causal[None], jnp.exp(spread), 0.0)


def prepare(
    conv_in,
    state_in,
    step_in,
    kernel_x,
    offset_x,
    kernel_bc,
    offset_bc,
    step_bias,
    rate_log,
    conv_keep,
    causal,
):
    mixer_in = jax.nn.silu(causal_conv(conv_in, kernel_x, offset_x, conv_keep))
    state_act = jax.nn.silu(causal_conv(state_in, kernel_bc, offset_bc, conv_keep))
    step_size = jax.nn.softplus(step_in + step_bias)
    return (mixer_in, state_act, step_size, decay_table(-step_size * jnp.exp(rate_log), causal))


def finish(scan_out, mixed_vals, skip_vec, gate_in, gain_vec):
    seq_len, head_count, head_dim = scan_out.shape
    combined = scan_out + skip_vec[None, :, None] * mixed_vals
    gated_vals = combined * jax.nn.silu(gate_in).reshape(seq_len, head_count, head_dim)
    inverse = lax.rsqrt(jnp.mean(gated_vals * gated_vals, axis=(1, 2), keepdims=True) + EPS)
    return (gated_vals * inverse * gain_vec.reshape(head_count, head_dim)).reshape(
        seq_len, head_count * head_dim
    )


def contract_rows(left_side, right_side):
    return lax.dot_general(
        left_side, right_side, (((0,), (0,)), ((), ())), preferred_element_type=jnp.float32
    )


def contract_cols(left_side, right_side):
    return lax.dot_general(
        left_side, right_side, (((1,), (1,)), ((), ())), preferred_element_type=jnp.float32
    )


def split_cols(matrix, widths):
    pieces = []
    begin_at = 0
    for part_width in widths:
        pieces.append(matrix[:, begin_at : begin_at + part_width])
        begin_at = begin_at + part_width
    return pieces


def flip(values, axis, mask):
    size = lax.axis_size(axis)
    return lax.ppermute(values, axis, [(i, i ^ mask) for i in range(size)])


def ring(values, step):
    return lax.ppermute(values, "fsdp", [(i, (i + 2 * step) % 8) for i in range(8)])


def staged():
    return lax.axis_size("fsdp") == 8


def place_bits():
    index = lax.axis_index("tp")
    return index // 2, index % 2


def gather_rows(rows_in):
    x_at, core_at = place_bits()
    far = flip(rows_in, "tp", 2)
    near = flip(rows_in, "tp", 1)
    cross = flip(far, "tp", 1)
    mine = jnp.where(core_at == 0, jnp.stack([rows_in, near]), jnp.stack([near, rows_in]))
    theirs = jnp.where(core_at == 0, jnp.stack([far, cross]), jnp.stack([cross, far]))
    whole = jnp.where(x_at == 0, jnp.stack([mine, theirs]), jnp.stack([theirs, mine]))
    return whole.reshape(4 * rows_in.shape[0], rows_in.shape[1])


def reduce_rows(rows_in):
    x_at, core_at = place_bits()
    parts = rows_in.reshape(2, 2, rows_in.shape[0] // 4, rows_in.shape[1])
    keep = jnp.where(core_at == 0, parts[:, 0], parts[:, 1])
    give = jnp.where(core_at == 0, parts[:, 1], parts[:, 0]).astype(jnp.bfloat16)
    half = keep + flip(give, "tp", 1).astype(jnp.float32)
    keep = jnp.where(x_at == 0, half[0], half[1])
    give = jnp.where(x_at == 0, half[1], half[0]).astype(jnp.bfloat16)
    return keep + flip(give, "tp", 2).astype(jnp.float32)


def fsdp_place():
    index = lax.axis_index("fsdp")
    return index // 2, index % 2


def to_rel(values, axis):
    if not staged():
        return values
    z_at, y_at = fsdp_place()
    shape = values.shape
    block = shape[axis] // 8
    split = shape[:axis] + (4, 2, block) + shape[axis + 1 :]
    parts = values.reshape(split)
    parts = jnp.where(y_at == 0, parts, jnp.flip(parts, axis + 1))
    parts = jnp.concatenate([parts, parts], axis)
    return lax.dynamic_slice_in_dim(parts, z_at, 4, axis).reshape(shape)


def from_rel(values, axis):
    if not staged():
        return values
    z_at, y_at = fsdp_place()
    shape = values.shape
    block = shape[axis] // 8
    split = shape[:axis] + (4, 2, block) + shape[axis + 1 :]
    parts = values.reshape(split)
    parts = jnp.where(y_at == 0, parts, jnp.flip(parts, axis + 1))
    parts = jnp.concatenate([parts, parts], axis)
    return lax.dynamic_slice_in_dim(parts, 4 - z_at, 4, axis).reshape(shape)


def gather_fsdp(shard):
    if not staged():
        return lax.all_gather(shard, "fsdp", axis=0, tiled=True)
    rows = shard.shape[0]
    pair = jnp.concatenate([shard, flip(shard, "fsdp", 1)], axis=0)
    below = ring(pair, 1)
    above = ring(pair, -1)
    far_a = ring(below[:rows], 1)
    far_b = ring(above[rows:], -1)
    return jnp.concatenate([pair, above, far_a, far_b, below], axis=0)


def scatter_fsdp(grads):
    if not staged():
        return lax.psum_scatter(grads, "fsdp", scatter_dimension=0, tiled=True)
    half_type = jnp.bfloat16
    rows = grads.shape[0] // 8
    parts = grads.reshape(4, 2, rows, grads.shape[1])
    wire = parts.astype(half_type)
    up_far = ring(wire[2, 0], 1)
    down_far = ring(wire[2, 1], -1)
    up_near = ring(wire[1, 1], 1)
    down_near = ring(wire[3, 0], -1)
    full = jnp.float32
    up_sum = ring((parts[1, 0] + up_far.astype(full)).astype(half_type), 1)
    down_sum = ring((parts[3, 1] + down_far.astype(full)).astype(half_type), -1)
    own = parts[0, 0] + up_sum.astype(full) + down_near.astype(full)
    other = parts[0, 1] + up_near.astype(full) + down_sum.astype(full)
    return own + flip(other.astype(half_type), "fsdp", 1).astype(full)


def sum_fsdp(values):
    if not staged():
        return lax.psum(values, "fsdp")
    for mask in (1, 2, 6):
        values = values + flip(values, "fsdp", mask)
    return values


def sum_tp(values):
    for mask in (1, 2):
        values = values + flip(values, "tp", mask)
    return values


def rms_parts(rows_in):
    inverse = lax.rsqrt(jnp.mean(rows_in * rows_in, axis=-1, keepdims=True) + EPS)
    return (rows_in * inverse, inverse)


def rms_back(d_out, normed, inverse, gain_vec):
    scaled = d_out * gain_vec
    d_rows = inverse * (scaled - normed * jnp.mean(scaled * normed, axis=-1, keepdims=True))
    return (d_rows, jnp.sum(d_out * normed, axis=0))


def ssd_core(mixer_in, state_act, step_size, decays):
    seq_len = mixer_in.shape[0]
    head_count = step_size.shape[1]
    mixed_vals = mixer_in.astype(jnp.bfloat16).reshape(seq_len, head_count, -1)
    state_vals = state_act.astype(jnp.bfloat16)
    basis_b = state_vals[:, :STATE]
    basis_c = state_vals[:, STATE:]
    gram_mat = contract_cols(basis_c, basis_b)
    weights_mat = (gram_mat[None] * decays).astype(jnp.bfloat16)
    mixed_f32 = mixed_vals.astype(jnp.float32)
    inputs_mat = (step_size[:, :, None] * mixed_f32).astype(jnp.bfloat16)
    scan_out = jnp.einsum(
        "hts,shp->thp", weights_mat, inputs_mat, preferred_element_type=jnp.float32
    )
    return (mixed_f32, basis_b, basis_c, gram_mat, weights_mat, inputs_mat, scan_out)


def attend_scores(queries, keys_rot, causal):
    products = jnp.einsum(
        "thd,sd->hts", queries, keys_rot, preferred_element_type=jnp.float32
    ) * HEAD ** (-0.5)
    return jnp.where(causal[None], products, NEG_FILL)


def sum_first(stacked):
    return jnp.sum(stacked, axis=0)


def shards(
    tokens,
    segment_ids,
    cotangent,
    norm_gain,
    w_z,
    w_x,
    w_bc,
    w_dt,
    conv_x,
    conv_bias_x,
    conv_bc,
    conv_bias_bc,
    dt_bias,
    a_log,
    d_skip,
    mixer_gain,
    w_mixer_out,
    w_query,
    w_keyval,
    w_attn_out,
    ffn_gain,
    w_gate,
    w_up,
    w_down,
):
    half_type = jnp.bfloat16
    full_type = jnp.float32
    row_count = w_bc.shape[0]
    gain_rows = norm_gain.shape[0]
    conv_rows = conv_bc.shape[0]
    small_in = jnp.concatenate([norm_gain, ffn_gain, conv_bc.reshape(-1), conv_bias_bc])
    small_size = small_in.shape[0]
    shared_cols = w_bc.shape[1] + w_keyval.shape[1]
    small_in = jnp.pad(small_in.reshape(1, -1), ((0, 15), (0, shared_cols - small_size)))
    shared_in = jnp.concatenate(
        [jnp.concatenate([w_bc, w_keyval], axis=1), small_in], axis=0
    ).astype(half_type)
    shared_all = gather_rows(shared_in).reshape(4, row_count + 16, shared_in.shape[1])
    small_rows = gather_fsdp(shared_all[:, row_count, :128])
    small_all = small_rows.reshape(-1, 128)
    gain_one, gain_two = (
        small_all[:, at : at + gain_rows].reshape(-1).astype(full_type) for at in (0, gain_rows)
    )
    conv_all = from_rel(small_all, 0)[:, 2 * gain_rows : small_size].astype(full_type)
    kernel_bc = conv_all[:, : conv_rows * CONV].reshape(-1, CONV)
    offset_bc = conv_all[:, conv_rows * CONV :].reshape(-1)
    bc_rows = shared_all[:, :row_count].reshape(4 * row_count, shared_in.shape[1])
    channels = w_z.shape[1]
    query_width = w_query.shape[1]
    query_local = query_width // HEAD
    hidden_local = w_gate.shape[1]
    head_index = lax.axis_index("tp") * query_local // (HEADS // KV_HEADS)
    keyval_rows = bc_rows[:, 2 * STATE :]
    key_rows = jnp.where(head_index == 0, keyval_rows[:, :HEAD], keyval_rows[:, HEAD : 2 * HEAD])
    value_rows = jnp.where(
        head_index == 0, keyval_rows[:, 2 * HEAD : 3 * HEAD], keyval_rows[:, 3 * HEAD :]
    )
    step_heads = w_dt.shape[1]
    step_rows = jnp.pad(w_dt.astype(half_type), ((0, 0), (0, 128 - step_heads)))
    widths = [channels, channels, 2 * STATE, query_width, HEAD, HEAD]

    def mix_forward(seq_in):
        proj_seq, step_seq, seg_ids = seq_in
        seq_len = proj_seq.shape[0]
        cosine, sine_vals, causal, conv_keep = sequence_tables(seg_ids)
        gate_in, conv_in, state_in, query_raw, key_raw, value_raw = split_cols(proj_seq, widths)
        mixer_in, state_act, step_size, decays = prepare(
            conv_in,
            state_in,
            step_seq,
            conv_x,
            conv_bias_x,
            kernel_bc,
            offset_bc,
            dt_bias,
            a_log,
            conv_keep,
            causal,
        )
        core_out = ssd_core(mixer_in, state_act, step_size, decays)
        mamba_out = finish(core_out[6], core_out[0], d_skip, gate_in, mixer_gain).astype(half_type)
        queries = rotate(query_raw.reshape(seq_len, query_local, HEAD), cosine, sine_vals).astype(
            half_type
        )
        keys_rot = rotate(key_raw.reshape(seq_len, 1, HEAD), cosine, sine_vals)[:, 0].astype(
            half_type
        )
        values_in = value_raw.astype(half_type)
        scores = attend_scores(queries, keys_rot, causal)
        row_max = jnp.max(scores, axis=-1, keepdims=True)
        log_total = row_max + jnp.log(jnp.sum(jnp.exp(scores - row_max), axis=-1, keepdims=True))
        probs_mat = jnp.exp(scores - log_total).astype(half_type)
        attended = jnp.einsum("hts,sd->thd", probs_mat, values_in, preferred_element_type=full_type)
        return (
            mamba_out,
            attended.reshape(seq_len, query_width).astype(half_type),
            log_total[:, :, 0],
        )

    def mix_backward(seq_in):
        proj_seq, step_seq, seg_ids, log_seq, d_cat_seq = seq_in
        seq_len = proj_seq.shape[0]
        cosine, sine_vals, causal, conv_keep = sequence_tables(seg_ids)
        gate_in, conv_in, state_in, query_raw, key_raw, value_raw = split_cols(proj_seq, widths)

        def prep_local(
            conv_part, state_part, step_part, kern_x, offs_x, kern_bc, offs_bc, bias_step, log_rate
        ):
            return prepare(
                conv_part,
                state_part,
                step_part,
                kern_x,
                offs_x,
                kern_bc,
                offs_bc,
                bias_step,
                log_rate,
                conv_keep,
                causal,
            )

        prepared, pull_prep = jax.vjp(
            prep_local,
            conv_in,
            state_in,
            step_seq,
            conv_x,
            conv_bias_x,
            kernel_bc,
            offset_bc,
            dt_bias,
            a_log,
        )
        mixer_in, state_act, step_size, decays = prepared
        mixed_f32, basis_b, basis_c, gram_mat, weights_mat, inputs_mat, scan_out = ssd_core(
            mixer_in, state_act, step_size, decays
        )
        d_mamba = d_cat_seq[:, :channels]
        d_attn = d_cat_seq[:, channels:]
        finished, pull_fin = jax.vjp(finish, scan_out, mixed_f32, d_skip, gate_in, mixer_gain)
        d_scan, d_mixed_skip, grad_skip, d_gate_in, grad_gain = pull_fin(d_mamba)
        d_scan_half = d_scan.astype(half_type)
        d_inputs = jnp.einsum(
            "hts,thp->shp", weights_mat, d_scan_half, preferred_element_type=full_type
        )
        d_weights = jnp.einsum(
            "thp,shp->hts", d_scan_half, inputs_mat, preferred_element_type=full_type
        )
        d_gram = jnp.sum(d_weights * decays, axis=0).astype(half_type)
        d_decays = d_weights * gram_mat[None]
        d_basis_c = jnp.dot(d_gram, basis_b, preferred_element_type=full_type)
        d_basis_b = contract_rows(d_gram, basis_c)
        d_mixed = (d_mixed_skip + d_inputs * step_size[:, :, None]).reshape(seq_len, channels)
        d_step_size = jnp.sum(d_inputs * mixed_f32, axis=-1)
        prep_grads = pull_prep(
            (d_mixed, jnp.concatenate([d_basis_b, d_basis_c], axis=1), d_step_size, d_decays)
        )
        (
            d_conv_in,
            d_state_in,
            d_step_in,
            grad_kx,
            grad_bx,
            grad_kbc,
            grad_bbc,
            grad_sbias,
            grad_rlog,
        ) = prep_grads

        def rope_pair(query_part, key_part):
            return (rotate(query_part, cosine, sine_vals), rotate(key_part, cosine, sine_vals))

        rotated, pull_rope = jax.vjp(
            rope_pair,
            query_raw.reshape(seq_len, query_local, HEAD),
            key_raw.reshape(seq_len, 1, HEAD),
        )
        queries = rotated[0].astype(half_type)
        keys_rot = rotated[1][:, 0].astype(half_type)
        values_in = value_raw.astype(half_type)
        scores = attend_scores(queries, keys_rot, causal)
        probs_full = jnp.exp(scores - log_seq[:, :, None])
        d_attended = d_attn.reshape(seq_len, query_local, HEAD).astype(half_type)
        d_values = jnp.einsum(
            "hts,thd->sd",
            probs_full.astype(half_type),
            d_attended,
            preferred_element_type=full_type,
        )
        d_probs = jnp.einsum("thd,sd->hts", d_attended, values_in, preferred_element_type=full_type)
        d_scores = (
            probs_full * (d_probs - jnp.sum(probs_full * d_probs, axis=-1, keepdims=True))
        ).astype(half_type)
        d_queries = jnp.einsum(
            "hts,sd->thd", d_scores, keys_rot, preferred_element_type=full_type
        ) * HEAD ** (-0.5)
        d_keys = jnp.einsum(
            "hts,thd->sd", d_scores, queries, preferred_element_type=full_type
        ) * HEAD ** (-0.5)
        d_query_raw, d_key_raw = pull_rope((d_queries, d_keys[:, None, :]))
        d_proj = jnp.concatenate(
            [
                d_gate_in,
                d_conv_in,
                d_state_in,
                d_query_raw.reshape(seq_len, query_width),
                d_key_raw.reshape(seq_len, HEAD),
                d_values,
            ],
            axis=1,
        ).astype(half_type)
        return (
            d_proj,
            d_step_in.astype(half_type),
            (grad_kx, grad_bx, grad_kbc, grad_bbc, grad_sbias, grad_rlog, grad_skip, grad_gain),
        )

    proj_weight = gather_fsdp(
        jnp.concatenate(
            [
                w_z.astype(half_type),
                w_x.astype(half_type),
                bc_rows[:, : 2 * STATE],
                w_query.astype(half_type),
                key_rows,
                value_rows,
                step_rows,
            ],
            axis=1,
        )
    )
    out_weight = gather_fsdp(
        jnp.concatenate([w_mixer_out.astype(half_type).T, w_attn_out.astype(half_type).T], axis=1)
    )
    ffn_weight = gather_fsdp(
        jnp.concatenate(
            [w_gate.astype(half_type), w_up.astype(half_type), w_down.astype(half_type).T], axis=1
        )
    )
    gate_up_weight = ffn_weight[:, : 2 * hidden_local]
    down_weight = ffn_weight[:, 2 * hidden_local :]
    group_rows = segment_ids.shape[0]
    seq_count = group_rows // SEQ
    tok_rows = to_rel(tokens, 1).astype(full_type)
    cot_rows = to_rel(cotangent, 1)
    normed_one, inverse_one = rms_parts(tok_rows)
    first_in = gather_rows((normed_one * gain_one).astype(half_type))
    projected = jnp.dot(first_in, proj_weight, preferred_element_type=full_type)
    step_raw = projected[:, sum(widths) : sum(widths) + step_heads]
    projected = projected[:, : sum(widths)]
    seg_seqs = segment_ids.reshape(seq_count, SEQ)
    proj_seqs = projected.reshape(seq_count, SEQ, projected.shape[1])
    step_seqs = step_raw.reshape(seq_count, SEQ, step_raw.shape[1])
    mamba_all, attn_all, log_totals = lax.map(mix_forward, (proj_seqs, step_seqs, seg_seqs))
    mixed_cat = jnp.concatenate(
        [mamba_all.reshape(group_rows, channels), attn_all.reshape(group_rows, query_width)], axis=1
    )
    after_mix = tok_rows + reduce_rows(
        contract_cols(mixed_cat, out_weight)
    )
    normed_two, inverse_two = rms_parts(after_mix)
    second_in = gather_rows((normed_two * gain_two).astype(half_type))
    gate_up = jnp.dot(second_in, gate_up_weight, preferred_element_type=full_type)
    gate_out = gate_up[:, :hidden_local]
    up_out = gate_up[:, hidden_local:]
    hidden = (jax.nn.silu(gate_out) * up_out).astype(half_type)
    output = after_mix + reduce_rows(contract_cols(hidden, down_weight))
    cot_all = gather_rows(cot_rows)
    d_hidden = jnp.dot(cot_all, down_weight, preferred_element_type=full_type)
    grad_down = contract_rows(cot_all, hidden)
    gate_sig = jax.nn.sigmoid(gate_out)
    d_gate = d_hidden * up_out * gate_sig * (1.0 + gate_out * (1.0 - gate_sig))
    d_up = d_hidden * (gate_out * gate_sig)
    d_gate_up = jnp.concatenate([d_gate, d_up], axis=1).astype(half_type)
    grad_gate_up = contract_rows(second_in, d_gate_up)
    ffn_sum = scatter_fsdp(jnp.concatenate([grad_gate_up, grad_down], axis=1))
    d_second = reduce_rows(contract_cols(d_gate_up, gate_up_weight))
    d_norm_two, grad_gain_two = rms_back(d_second, normed_two, inverse_two, gain_two)
    d_after = cot_rows.astype(full_type) + d_norm_two
    d_mix_all = gather_rows(d_after.astype(half_type))
    d_cat = jnp.dot(d_mix_all, out_weight, preferred_element_type=full_type)
    out_sum = scatter_fsdp(contract_rows(d_mix_all, mixed_cat))
    d_projs, d_steps, small_parts = lax.map(
        mix_backward,
        (proj_seqs, step_seqs, seg_seqs, log_totals, d_cat.reshape(seq_count, SEQ, d_cat.shape[1])),
    )
    small_sums = [sum_first(stacked) for stacked in small_parts]
    d_proj_all = d_projs.reshape(group_rows, d_projs.shape[2])
    d_step_all = d_steps.reshape(group_rows, d_steps.shape[2])
    d_wide = jnp.concatenate(
        [d_proj_all, jnp.pad(d_step_all, ((0, 0), (0, 128 - step_heads)))], axis=1
    )
    proj_sum = scatter_fsdp(contract_rows(first_in, d_wide))
    d_first = reduce_rows(contract_cols(d_wide, proj_weight))
    d_norm_one, grad_gain_one = rms_back(d_first, normed_one, inverse_one, gain_one)
    grad_tokens = from_rel(d_after + d_norm_one, 1)
    sum_z, sum_x, sum_bc, sum_query, sum_key, sum_value, sum_step = split_cols(
        proj_sum, widths + [step_heads]
    )

    x_at, core_at = place_bits()
    shared_rows = jnp.concatenate([sum_bc, sum_key, sum_value], axis=1)
    shared_rows = shared_rows.reshape(2, 2, row_count, shared_rows.shape[1])
    keep = jnp.where(core_at == 0, shared_rows[:, 0], shared_rows[:, 1])
    give = jnp.where(core_at == 0, shared_rows[:, 1], shared_rows[:, 0])
    chip_rows = keep + flip(give, "tp", 1)
    keep = jnp.where(x_at == 0, chip_rows[0], chip_rows[1])
    give = jnp.where(x_at == 0, chip_rows[1], chip_rows[0])
    came = flip(give, "tp", 2)
    grad_bc = keep[:, : 2 * STATE] + came[:, : 2 * STATE]
    key_mine, value_mine = split_cols(keep[:, 2 * STATE :], [HEAD, HEAD])
    key_came, value_came = split_cols(came[:, 2 * STATE :], [HEAD, HEAD])
    grad_keyval = jnp.where(
        x_at == 0,
        jnp.concatenate([key_mine, key_came, value_mine, value_came], axis=1),
        jnp.concatenate([key_came, key_mine, value_came, value_mine], axis=1),
    )

    gains = jnp.stack([from_rel(grad_gain_one, 0), from_rel(grad_gain_two, 0)])
    common = jnp.concatenate([gains.reshape(-1), small_sums[2].reshape(-1), small_sums[3]])
    common_size = common.shape[0]
    parts = [small_sums[0], small_sums[1], small_sums[4], small_sums[5], small_sums[6], small_sums[7]]
    flat = jnp.concatenate([sum_tp(common)] + [part.reshape(-1) for part in parts])
    flat = jnp.pad(flat, (0, -flat.shape[0] % 1024)).reshape(-1, 128)
    flat = sum_fsdp(flat).reshape(-1)
    vector_sums = []
    begin_at = common_size
    for part in parts:
        vector_sums.append(flat[begin_at : begin_at + part.size].reshape(part.shape))
        begin_at = begin_at + part.size
    device = lax.axis_index("fsdp") * 4 + lax.axis_index("tp")
    width = grad_gain_one.shape[0]
    sum_gain_one = lax.dynamic_slice_in_dim(flat[:width], device * gain_rows, gain_rows)
    sum_gain_two = lax.dynamic_slice_in_dim(flat[width : 2 * width], device * gain_rows, gain_rows)
    conv_flat = flat[2 * width : 2 * width + 2 * STATE * CONV].reshape(2 * STATE, CONV)
    bias_flat = flat[2 * width + 2 * STATE * CONV : common_size]
    sum_conv = lax.dynamic_slice_in_dim(conv_flat, device * conv_rows, conv_rows)
    sum_bias = lax.dynamic_slice_in_dim(bias_flat, device * conv_rows, conv_rows)
    sum_gate, sum_up, sum_down = split_cols(ffn_sum, [hidden_local, hidden_local, hidden_local])
    return (
        from_rel(output.astype(half_type), 1),
        grad_tokens,
        sum_gain_one,
        sum_z,
        sum_x,
        grad_bc,
        sum_step,
        vector_sums[0],
        vector_sums[1],
        sum_conv,
        sum_bias,
        vector_sums[2],
        vector_sums[3],
        vector_sums[4],
        vector_sums[5],
        out_sum[:, :channels].T,
        sum_query,
        grad_keyval,
        out_sum[:, channels:].T,
        sum_gain_two,
        sum_gate,
        sum_up,
        sum_down.T,
    )


def solution(mesh):
    placed = (
        P(("fsdp", "tp"), None),
        P("fsdp"),
        P(("fsdp", "tp"), None),
        P(("fsdp", "tp")),
        P("fsdp", "tp"),
        P("fsdp", "tp"),
        P(("fsdp", "tp"), None),
        P("fsdp", "tp"),
        P("tp", None),
        P("tp"),
        P(("fsdp", "tp"), None),
        P(("fsdp", "tp")),
        P("tp"),
        P("tp"),
        P("tp"),
        P("tp"),
        P("tp", "fsdp"),
        P("fsdp", "tp"),
        P(("fsdp", "tp"), None),
        P("tp", "fsdp"),
        P(("fsdp", "tp")),
        P("fsdp", "tp"),
        P("fsdp", "tp"),
        P("tp", "fsdp"),
    )
    return jax.shard_map(
        shards,
        mesh=mesh,
        in_specs=placed,
        out_specs=(
            P(("fsdp", "tp"), None),
            P(("fsdp", "tp"), None),
            P(("fsdp", "tp")),
            P("fsdp", "tp"),
            P("fsdp", "tp"),
            P(("fsdp", "tp"), None),
            P("fsdp", "tp"),
            P("tp", None),
            P("tp"),
            P(("fsdp", "tp"), None),
            P(("fsdp", "tp")),
            P("tp"),
            P("tp"),
            P("tp"),
            P("tp"),
            P("tp", "fsdp"),
            P("fsdp", "tp"),
            P(("fsdp", "tp"), None),
            P("tp", "fsdp"),
            P(("fsdp", "tp")),
            P("fsdp", "tp"),
            P("fsdp", "tp"),
            P("tp", "fsdp"),
        ),
        check_vma=False,
    )
```

```python
import functools

import jax
import jax.numpy as jnp
from jax import lax
from jax.experimental import pallas as pl
from jax.experimental.pallas import tpu as pltpu
from jax.sharding import PartitionSpec as P

STATE = 128
CONV = 4
HEADS = 8
KV_HEADS = 2
HEAD = 64

EPS = 1e-06
ROPE_BASE = 10000.0
NEG_FILL = -1e30


def contract_rows(left_side, right_side):
    return lax.dot_general(
        left_side, right_side, (((0,), (0,)), ((), ())), preferred_element_type=jnp.float32
    )


def contract_cols(left_side, right_side):
    return lax.dot_general(
        left_side, right_side, (((1,), (1,)), ((), ())), preferred_element_type=jnp.float32
    )


def split_cols(matrix, widths):
    pieces = []
    begin_at = 0
    for part_width in widths:
        pieces.append(matrix[:, begin_at : begin_at + part_width])
        begin_at = begin_at + part_width
    return pieces


def flip(values, axis, mask):
    size = lax.axis_size(axis)
    return lax.ppermute(values, axis, [(i, i ^ mask) for i in range(size)])


def ring(values, step):
    return lax.ppermute(values, "fsdp", [(i, (i + 2 * step) % 8) for i in range(8)])


def staged():
    return lax.axis_size("fsdp") == 8


def place_bits():
    index = lax.axis_index("tp")
    return index // 2, index % 2


def gather_pieces(rows_in):
    far = flip(rows_in, "tp", 2)
    near = flip(rows_in, "tp", 1)
    cross = flip(far, "tp", 1)
    return rows_in, far, near, cross


def reduce_pieces(keep, give):
    half = keep.shape[0] // 2
    near = flip(give, "tp", 1)
    passed = (keep[half:] + near[half:].astype(jnp.float32)).astype(jnp.bfloat16)
    far = flip(passed, "tp", 2)
    return keep, near, far


def fsdp_place():
    index = lax.axis_index("fsdp")
    return index // 2, index % 2


class Scatter:
    def __init__(self, grads):
        self.grads = grads
        self.rows = grads[0].shape[0] // 8
        self.carried = None
        if staged():
            self.came = self.exchange(3)

    def part(self, dy, dz):
        rows = slice((dy * 4 + dz) * self.rows, (dy * 4 + dz + 1) * self.rows)
        if len(self.grads) == 1:
            return self.grads[0][rows]
        return jnp.concatenate([grad[rows] for grad in self.grads], axis=1)

    def exchange(self, dz):
        return flip(self.part(1, dz), "fsdp", 1)

    def summed(self, dz):
        total = self.part(0, dz).astype(jnp.float32) + self.came.astype(jnp.float32)
        return total if self.carried is None else total + self.carried.astype(jnp.float32)

    def step(self, dz):
        if not staged():
            return ()
        self.carried = ring(self.summed(dz).astype(jnp.bfloat16), 1)
        self.came = self.exchange(dz - 1)
        return self.carried, self.came

    def total(self):
        if not staged():
            return lax.psum_scatter(
                jnp.concatenate(self.grads, axis=1), "fsdp", scatter_dimension=0, tiled=True
            ).astype(jnp.float32)
        return self.summed(0)


class Gather:
    def __init__(self, shard):
        self.shard = shard
        if staged():
            self.along, self.across = [shard], [flip(shard, "fsdp", 1)]

    def step(self):
        if not staged():
            return ()
        came = ring(self.along[-1], 1)
        self.along.append(came)
        self.across.append(flip(came, "fsdp", 1))
        return came, self.across[-1]

    def parts(self):
        if not staged():
            return [lax.all_gather(self.shard, "fsdp", axis=0, tiled=True)]
        return [blocks[-dz % 4] for blocks in (self.along, self.across) for dz in range(4)]


def sum_fsdp(values):
    if not staged():
        return lax.psum(values, "fsdp")
    for mask in (1, 2, 6):
        values = values + flip(values, "fsdp", mask)
    return values


def sum_tp(values):
    for mask in (1, 2):
        values = values + flip(values, "tp", mask)
    return values


def feature_order():
    if not staged():
        return jnp.arange(8, dtype=jnp.int32)
    z_at, y_at = fsdp_place()
    steps = jnp.arange(8, dtype=jnp.int32)
    return (z_at + steps % 4) % 4 * 2 + (y_at ^ (steps // 4))


CHUNK = 32


def row_chunks(rows, body, carry=0):
    def step(k, carry):
        return body(pl.ds(pl.multiple_of(k * CHUNK, CHUNK), CHUNK), carry)

    return lax.fori_loop(0, rows // CHUNK, step, carry)


def front_body(order_ref, tok_ref, cot_ref, both_ref, tok_rel):
    rows_all, width = tok_ref.shape
    block = width // 8

    def chunk(rows, carry):
        below = pl.ds(pl.multiple_of(rows.start + rows_all, CHUNK), CHUNK)
        for b in range(8):
            there = pl.ds(pl.multiple_of(order_ref[b] * block, block), block)
            here = slice(b * block, b * block + block)
            tok_rel[rows, here] = tok_ref[rows, there]
            both_ref[below, here] = cot_ref[rows, there]
        values = tok_rel[rows].astype(jnp.float32)
        normed = values * lax.rsqrt(jnp.mean(values * values, axis=-1, keepdims=True) + EPS)
        both_ref[rows] = normed.astype(jnp.bfloat16)
        return carry

    row_chunks(rows_all, chunk)


def summed_rows(rows, keep_ref, near_ref, far_ref):
    return (
        keep_ref[rows] + near_ref[rows].astype(jnp.float32) + far_ref[rows].astype(jnp.float32)
    )


def mixed_body(_, tok_ref, keep_ref, near_ref, far_ref, gain_ref, after_ref, second_ref):
    def chunk(rows, carry):
        after = tok_ref[rows].astype(jnp.float32) + summed_rows(rows, keep_ref, near_ref, far_ref)
        after_ref[rows] = after
        normed = after * lax.rsqrt(jnp.mean(after * after, axis=-1, keepdims=True) + EPS)
        second_ref[rows] = (normed * gain_ref[...]).astype(jnp.bfloat16)
        return carry

    row_chunks(tok_ref.shape[0], chunk)


def output_body(order_ref, after_ref, keep_ref, near_ref, far_ref, out_ref):
    block = after_ref.shape[1] // 8

    def chunk(rows, carry):
        values = after_ref[rows] + summed_rows(rows, keep_ref, near_ref, far_ref)
        values = values.astype(jnp.bfloat16)
        for b in range(8):
            there = pl.ds(pl.multiple_of(order_ref[b] * block, block), block)
            out_ref[rows, there] = values[:, b * block : b * block + block]
        return carry

    row_chunks(after_ref.shape[0], chunk)


def norm_back(values, d_out, gain):
    inverse = lax.rsqrt(jnp.mean(values * values, axis=-1, keepdims=True) + EPS)
    normed = values * inverse
    scaled = d_out * gain
    return inverse * (scaled - normed * jnp.mean(scaled * normed, axis=-1, keepdims=True))


def after_back_body(
    _, after_ref, cot_ref, keep_ref, near_ref, far_ref, gain_ref, d_after_ref, d_mix_ref
):
    def chunk(rows, carry):
        d_second = summed_rows(rows, keep_ref, near_ref, far_ref)
        lower = pl.ds(pl.multiple_of(rows.start + after_ref.shape[0], CHUNK), CHUNK)
        d_after = cot_ref[lower].astype(jnp.float32) + norm_back(
            after_ref[rows], d_second, gain_ref[...]
        )
        d_after_ref[rows] = d_after
        d_mix_ref[rows] = d_after.astype(jnp.bfloat16)
        return carry

    row_chunks(after_ref.shape[0], chunk)


def token_back_body(
    order_ref, tok_ref, d_after_ref, keep_ref, near_ref, far_ref, gain_ref, out_ref
):
    block = tok_ref.shape[1] // 8

    def chunk(rows, carry):
        d_first = summed_rows(rows, keep_ref, near_ref, far_ref)
        values = d_after_ref[rows] + norm_back(
            tok_ref[rows].astype(jnp.float32), d_first, gain_ref[...]
        )
        for b in range(8):
            there = pl.ds(pl.multiple_of(order_ref[b] * block, block), block)
            out_ref[rows, there] = values[:, b * block : b * block + block]
        return carry

    row_chunks(tok_ref.shape[0], chunk)


def piece_at(block, at):
    apart = block ^ at
    return (apart & 1) * 2 + (apart >> 1)


def head_lanes(columns, first, lanes):
    rows = columns.shape[0]
    even = jnp.broadcast_to(columns[:, first : first + 1], (rows, 128))
    odd = jnp.broadcast_to(columns[:, first + 1 : first + 2], (rows, 128))
    return jnp.where(lanes < HEAD, even, odd)


def lane_ids(rows, cols):
    return lax.broadcasted_iota(jnp.int32, (rows, cols), 1)


def row_ids(rows, cols):
    return lax.broadcasted_iota(jnp.int32, (rows, cols), 0)


def dot_nt(left_side, right_side, **kw):
    return lax.dot_general(
        left_side, right_side, (((1,), (1,)), ((), ())), preferred_element_type=jnp.float32, **kw
    )


def dot_nn(left_side, right_side):
    return jnp.dot(left_side, right_side, preferred_element_type=jnp.float32)


def dot_tn(left_side, right_side):
    return lax.dot_general(
        left_side, right_side, (((0,), (0,)), ((), ())), preferred_element_type=jnp.float32
    )


def conv_window(window, taps, offset, keep):
    rows = window.shape[0] - 8
    summed = window[8:] * taps[CONV - 1 : CONV] + offset
    for lag in range(1, CONV):
        summed = summed + window[8 - lag : 8 - lag + rows] * keep[:, lag : lag + 1] * (
            taps[CONV - 1 - lag : CONV - lag]
        )
    return summed


def log_one_plus(values):
    ratio = values / (2.0 + values)
    square = ratio * ratio
    series = jnp.full_like(values, 1.0 / 15.0)
    for odd in (13, 11, 9, 7, 5, 3, 1):
        series = series * square + 1.0 / odd
    return 2.0 * ratio * series


def scan_lanes(values, reverse):
    length = values.shape[1]
    lanes = lane_ids(*values.shape)
    step = 1
    while step < length:
        if reverse:
            moved = jnp.where(lanes < length - step, pltpu.roll(values, length - step, 1), 0.0)
        else:
            moved = jnp.where(lanes >= step, pltpu.roll(values, step, 1), 0.0)
        values = values + moved
        step = step * 2
    return values


def pair_mask(seg_col, seg_row, at_t, at_s):
    size = seg_col.shape[0]
    rows = row_ids(size, size) + at_t * size
    cols = lane_ids(size, size) + at_s * size
    return (seg_col == seg_row) & (rows >= cols)


def swap_halves(values, lanes):
    half = HEAD // 2
    return jnp.where(
        lanes % HEAD < half, pltpu.roll(values, 128 - half, 1), pltpu.roll(values, half, 1)
    )


def ssd_forward_body(
    heads,
    at_ref,
    proj_ref,
    segc_ref,
    segr_ref,
    keep_ref,
    taps_ref,
    tapb_ref,
    rate_ref,
    scan_ref,
    xpre_ref,
    bpre_ref,
    basis_ref,
    inputs_ref,
    rows_ref,
    cols_ref,
    xpad,
    bpad,
    dtr,
):
    blocks, size = proj_ref.shape[0], proj_ref.shape[1]
    channels = xpre_ref.shape[1]
    states = bpre_ref.shape[1]
    tail = proj_ref.shape[2] - states - 128
    at = at_ref[0]
    xpad[0:8] = jnp.zeros((8, channels), jnp.float32)
    bpad[0:8] = jnp.zeros((8, states), jnp.float32)

    def load(a, carry):
        rows = pl.ds(pl.multiple_of(a * size + 8, 8), size)
        block = piece_at(a, at)
        xpad[rows] = proj_ref[block, :, :channels]
        bpad[rows] = proj_ref[block, :, tail : tail + states]
        steps = proj_ref[block, :, tail + states :]
        dtr[:, pl.ds(pl.multiple_of(a * size, size), size)] = steps.T[0:8]
        return carry

    lax.fori_loop(0, blocks, load, 0)
    raw = dtr[...] + rate_ref[:, 0:1]
    step_size = jnp.maximum(raw, 0.0) + log_one_plus(jnp.exp(-jnp.abs(raw)))
    log_rate = -step_size * jnp.exp(rate_ref[:, 1:2])
    cum = scan_lanes(log_rate, False)
    length = raw.shape[1]
    rows_ref[0:8] = step_size
    rows_ref[8:16] = cum
    rows_ref[16:24] = raw
    cols_ref[...] = jnp.concatenate(
        [step_size, cum, jnp.zeros((112, length), jnp.float32)], axis=0
    ).T
    lanes = lane_ids(size, 128)

    def prepare_block(a, carry):
        window = pl.ds(pl.multiple_of(a * size, size), size + 8)
        rows = pl.ds(pl.multiple_of(a * size, size), size)
        keep = keep_ref[rows]
        columns = cols_ref[rows]
        bpre = conv_window(bpad[window], tapb_ref[0:4], tapb_ref[4:5], keep)
        bpre_ref[rows] = bpre
        basis_ref[rows] = (bpre * jax.nn.sigmoid(bpre)).astype(jnp.bfloat16)
        for pair in range(channels // 128):
            span = slice(pair * 128, pair * 128 + 128)
            xpre = conv_window(xpad[window, span], taps_ref[0:4, span], taps_ref[4:5, span], keep)
            xpre_ref[rows, span] = xpre
            mixed = (xpre * jax.nn.sigmoid(xpre)).astype(jnp.bfloat16).astype(jnp.float32)
            steps = head_lanes(columns, 2 * pair, lanes)
            inputs_ref[rows, span] = (steps * mixed).astype(jnp.bfloat16)
        return carry

    lax.fori_loop(0, blocks, prepare_block, 0)
    state = states // 2

    def row_block(i, carry):
        rows_t = pl.ds(pl.multiple_of(i * size, size), size)
        basis_c = basis_ref[rows_t, state:]
        seg_t = segc_ref[rows_t]
        columns = cols_ref[rows_t]

        def pair_block(j, totals):
            rows_s = pl.ds(pl.multiple_of(j * size, size), size)
            allowed = pair_mask(seg_t, segr_ref[:, rows_s], i, j)
            gram = jnp.where(allowed, dot_nt(basis_c, basis_ref[rows_s, :state]), 0.0)
            cum_s = rows_ref[8:16, rows_s]
            fresh = []
            for pair in range(heads // 2):
                values = inputs_ref[rows_s, pair * 128 : pair * 128 + 128]
                outs = []
                for h in (2 * pair, 2 * pair + 1):
                    spread = columns[:, 8 + h : 9 + h] - cum_s[h : h + 1]
                    weights = (gram * jnp.exp(jnp.minimum(spread, 0.0))).astype(jnp.bfloat16)
                    outs.append(dot_nn(weights, values))
                fresh.append(totals[pair] + jnp.where(lanes < HEAD, outs[0], outs[1]))
            return tuple(fresh)

        zero = jnp.zeros((size, 128), jnp.float32)
        totals = lax.fori_loop(0, i + 1, pair_block, (zero,) * (heads // 2))
        for pair in range(heads // 2):
            scan_ref[rows_t, pair * 128 : pair * 128 + 128] = totals[pair]
        return carry

    lax.fori_loop(0, blocks, row_block, 0)


def attend_forward_body(
    count,
    at_ref,
    first_ref,
    proj_ref,
    scan_ref,
    xpre_ref,
    segc_ref,
    segr_ref,
    cos_ref,
    sin_ref,
    gain_ref,
    *refs,
):
    parts = refs[:count]
    cat_ref, gate_ref, query_ref, keyk_ref, valv_ref, logs_ref, inv_ref, weight_ref = refs[count:]
    stack_rows(parts, weight_ref)
    blocks, size = proj_ref.shape[0], proj_ref.shape[1]
    channels = scan_ref.shape[1]
    at = at_ref[0]
    lanes = lane_ids(size, 128)
    half_type = jnp.bfloat16

    def finish_block(a, carry):
        rows = pl.ds(pl.multiple_of(a * size, size), size)
        block = piece_at(a, at)
        xpre = xpre_ref[rows]
        mixed = (xpre * jax.nn.sigmoid(xpre)).astype(half_type).astype(jnp.float32)
        mine = dot_nn(first_ref[block], weight_ref[:, : channels + 128])
        gate, query = mine[:, :channels], mine[:, channels:]
        gate_ref[block] = gate
        gated = (scan_ref[rows] + gain_ref[1:2] * mixed) * (gate * jax.nn.sigmoid(gate))
        inverse = lax.rsqrt(jnp.mean(gated * gated, axis=-1, keepdims=True) + EPS)
        inv_ref[rows] = jnp.broadcast_to(inverse, (size, 128))
        cat_ref[block, :, :channels] = (gated * inverse * gain_ref[0:1]).astype(half_type)
        cosine, sine = cos_ref[rows], sin_ref[rows]
        query_ref[rows] = (query * cosine + swap_halves(query, lanes) * sine).astype(half_type)
        keyval = proj_ref[block, :, channels : channels + 128]
        keyval = keyval * jnp.where(lanes < HEAD, cosine, 1.0) + swap_halves(
            keyval, lanes
        ) * jnp.where(lanes < HEAD, sine, 0.0)
        moved = pltpu.roll(keyval, HEAD, 1)
        keyk_ref[rows] = jnp.where(lanes < HEAD, keyval, moved).astype(half_type)
        valv_ref[rows] = jnp.where(lanes < HEAD, moved, keyval).astype(half_type)
        return carry

    lax.fori_loop(0, blocks, finish_block, 0)
    for i in range(blocks):
        width = (i + 1) * size
        rows = slice(i * size, width)
        query = query_ref[rows]
        places = row_ids(size, width) + i * size
        allowed = (segc_ref[rows] == segr_ref[:, :width]) & (places >= lane_ids(size, width))
        outs, logs = [], []
        for h in range(2):
            mine = (lanes < HEAD) if h == 0 else (lanes >= HEAD)
            masked = jnp.where(mine, query, jnp.zeros_like(query))
            scores = dot_nt(masked, keyk_ref[:width]) * HEAD ** (-0.5)
            scores = jnp.where(allowed, scores, NEG_FILL)
            top = jnp.max(scores, axis=-1, keepdims=True)
            powers = jnp.exp(scores - top)
            total = jnp.sum(powers, axis=-1, keepdims=True)
            outs.append(dot_nn(powers.astype(half_type), valv_ref[:width]) / total)
            logs.append(top + jnp.log(total))
        cat_ref[piece_at(i, at), :, channels:] = jnp.where(lanes < HEAD, outs[0], outs[1]).astype(half_type)
        logs_ref[rows] = jnp.where(lanes < HEAD, logs[0], logs[1])


def attend_backward_body(
    at_ref,
    gate_ref,
    mine_ref,
    far_ref,
    near_ref,
    cross_ref,
    weight_ref,
    scan_ref,
    xpre_ref,
    segc_ref,
    segr_ref,
    cos_ref,
    sin_ref,
    gain_ref,
    query_ref,
    keyk_ref,
    valv_ref,
    logs_ref,
    inv_ref,
    dproj_ref,
    dcomb_ref,
    small_ref,
    dmix_ref,
    dkey,
    dval,
    dcat_ref,
):
    wide = dcat_ref.shape[2]
    for p, piece in enumerate((mine_ref, far_ref, near_ref, cross_ref)):
        dmix_ref[p] = piece[...]
        dcat_ref[p] = dot_nn(piece[...], weight_ref[:, weight_ref.shape[1] - wide :])
    blocks, size = gate_ref.shape[0], gate_ref.shape[1]
    channels = scan_ref.shape[1]
    at = at_ref[0]
    lanes = lane_ids(size, 128)
    half_type = jnp.bfloat16

    def finish_block(a, carry):
        grad_gain, grad_skip = carry
        rows = pl.ds(pl.multiple_of(a * size, size), size)
        block = piece_at(a, at)
        xpre = xpre_ref[rows]
        mixed = (xpre * jax.nn.sigmoid(xpre)).astype(half_type).astype(jnp.float32)
        gate = gate_ref[block]
        sig = jax.nn.sigmoid(gate)
        act = gate * sig
        combined = scan_ref[rows] + gain_ref[1:2] * mixed
        inverse = inv_ref[rows, 0:1]
        normed = combined * act * inverse
        d_out = dcat_ref[block, :, :channels]
        grad_gain = grad_gain + jnp.sum(d_out * normed, axis=0, keepdims=True)
        scaled = d_out * gain_ref[0:1]
        d_gated = inverse * (scaled - normed * jnp.mean(scaled * normed, axis=-1, keepdims=True))
        d_comb = d_gated * act
        dcomb_ref[rows] = d_comb
        grad_skip = grad_skip + jnp.sum(d_comb * mixed, axis=0, keepdims=True)
        d_gate = d_gated * combined * sig * (1.0 + gate * (1.0 - sig))
        dproj_ref[block, :, :channels] = d_gate.astype(half_type)
        return grad_gain, grad_skip

    zero = jnp.zeros((1, channels), jnp.float32)
    grad_gain, grad_skip = lax.fori_loop(0, blocks, finish_block, (zero, zero))
    small_ref[...] = jnp.concatenate(
        [grad_gain, grad_skip, jnp.zeros((6, channels), jnp.float32)], axis=0
    )
    dkey[...] = jnp.zeros_like(dkey)
    dval[...] = jnp.zeros_like(dval)
    for i in range(blocks):
        width = (i + 1) * size
        rows = slice(i * size, width)
        query = query_ref[rows]
        d_att = dcat_ref[piece_at(i, at), :, channels:].astype(half_type)
        logs = logs_ref[rows]
        places = row_ids(size, width) + i * size
        allowed = (segc_ref[rows] == segr_ref[:, :width]) & (places >= lane_ids(size, width))
        outs = []
        for h in range(2):
            mine = (lanes < HEAD) if h == 0 else (lanes >= HEAD)
            masked = jnp.where(mine, query, jnp.zeros_like(query))
            d_masked = jnp.where(mine, d_att, jnp.zeros_like(d_att))
            scores = dot_nt(masked, keyk_ref[:width]) * HEAD ** (-0.5)
            scores = jnp.where(allowed, scores, NEG_FILL)
            probs = jnp.exp(scores - logs[:, h * HEAD : h * HEAD + 1])
            d_probs = dot_nt(d_masked, valv_ref[:width])
            mean = jnp.sum(probs * d_probs, axis=-1, keepdims=True)
            d_scores = (probs * (d_probs - mean)).astype(half_type)
            outs.append(dot_nn(d_scores, keyk_ref[:width]))
            dkey[:width] += dot_tn(d_scores, masked)
            dval[:width] += dot_tn(probs.astype(half_type), d_masked)
        d_query = jnp.where(lanes < HEAD, outs[0], outs[1]) * HEAD ** (-0.5)
        cosine, sine = cos_ref[rows], sin_ref[rows]
        d_query = d_query * cosine - swap_halves(d_query, lanes) * sine
        dproj_ref[piece_at(i, at), :, channels : channels + 128] = d_query.astype(half_type)

    def key_block(a, carry):
        rows = pl.ds(pl.multiple_of(a * size, size), size)
        d_key, d_val = dkey[rows], dval[rows]
        d_key = (d_key + pltpu.roll(d_key, HEAD, 1)) * HEAD ** (-0.5)
        d_val = d_val + pltpu.roll(d_val, HEAD, 1)
        d_key = d_key * cos_ref[rows] - swap_halves(d_key, lanes) * sin_ref[rows]
        dproj_ref[piece_at(a, at), :, channels + 128 :] = jnp.where(lanes < HEAD, d_key, d_val).astype(
            half_type
        )
        return carry

    lax.fori_loop(0, blocks, key_block, 0)


def silu_slope(values):
    sig = jax.nn.sigmoid(values)
    return sig * (1.0 + values * (1.0 - sig))


def conv_back(d_window, keep_window, taps):
    rows = d_window.shape[0] - 8
    summed = d_window[:rows] * taps[CONV - 1 : CONV]
    for lag in range(1, CONV):
        moved = d_window * keep_window[:, lag : lag + 1]
        summed = summed + moved[lag : lag + rows] * taps[CONV - 1 - lag : CONV - lag]
    return summed


def conv_grads(d_pre, window, keep):
    rows = d_pre.shape[0]
    sums = []
    for tap in range(CONV):
        lag = CONV - 1 - tap
        moved = window[8 - lag : 8 - lag + rows]
        if lag:
            moved = moved * keep[:, lag : lag + 1]
        sums.append(jnp.sum(d_pre * moved, axis=0, keepdims=True))
    sums.append(jnp.sum(d_pre, axis=0, keepdims=True))
    sums.append(jnp.zeros((8 - len(sums), d_pre.shape[1]), jnp.float32))
    return jnp.concatenate(sums, axis=0)


def ssd_backward_body(
    heads,
    at_ref,
    proj_ref,
    dcomb_ref,
    scan_ref,
    segc_ref,
    segr_ref,
    keep_ref,
    taps_ref,
    tapb_ref,
    rate_ref,
    gain_ref,
    xpre_ref,
    bpre_ref,
    basis_ref,
    inputs_ref,
    rows_ref,
    cols_ref,
    dproj_ref,
    gradx_ref,
    gradb_ref,
    grads_ref,
    xpad,
    bpad,
    dpx,
    dpb,
    dsc,
    dst,
    cbt,
    mixt,
    dint,
    dbt,
    dcb,
    qrow,
):
    blocks, size = proj_ref.shape[0], proj_ref.shape[1]
    channels = xpre_ref.shape[1]
    states = bpre_ref.shape[1]
    state = states // 2
    tail = proj_ref.shape[2] - states - 128
    length = blocks * size
    at = at_ref[0]
    half_type = jnp.bfloat16
    lanes = lane_ids(size, 128)
    xpad[0:8] = jnp.zeros((8, channels), jnp.float32)
    bpad[0:8] = jnp.zeros((8, states), jnp.float32)
    dpx[length : length + 8] = jnp.zeros((8, channels), jnp.float32)
    dpb[length : length + 8] = jnp.zeros((8, states), jnp.float32)
    dint[...] = jnp.zeros_like(dint)
    dbt[...] = jnp.zeros_like(dbt)
    head_of = jnp.where(
        lane_ids(8, channels) // HEAD == row_ids(8, channels), 1.0, 0.0
    ).astype(jnp.float32)

    def load(a, carry):
        rows = pl.ds(pl.multiple_of(a * size, size), size)
        padded = pl.ds(pl.multiple_of(a * size + 8, 8), size)
        block = piece_at(a, at)
        xpad[padded] = proj_ref[block, :, :channels]
        bpad[padded] = proj_ref[block, :, tail : tail + states]
        d_scan = dcomb_ref[rows].astype(half_type)
        dsc[rows] = d_scan
        d_full = d_scan.astype(jnp.float32)
        dst[:, rows] = d_full.T.astype(half_type)
        cbt[:, rows] = basis_ref[rows, state:].astype(jnp.float32).T.astype(half_type)
        xpre = xpre_ref[rows]
        mixed = (xpre * jax.nn.sigmoid(xpre)).astype(half_type).astype(jnp.float32)
        mixt[:, rows] = mixed.T
        qrow[:, rows] = dot_nt(head_of, d_full * scan_ref[rows], precision=lax.Precision.HIGHEST)
        return carry

    lax.fori_loop(0, blocks, load, 0)

    def row_block(i, carry):
        rows_t = pl.ds(pl.multiple_of(i * size, size), size)
        basis_c = basis_ref[rows_t, state:]
        seg_t = segc_ref[rows_t]
        columns = cols_ref[rows_t]

        def pair_block(j, total):
            rows_s = pl.ds(pl.multiple_of(j * size, size), size)
            allowed = pair_mask(seg_t, segr_ref[:, rows_s], i, j)
            gram = jnp.where(allowed, dot_nt(basis_c, basis_ref[rows_s, :state]), 0.0)
            cum_s = rows_ref[8:16, rows_s]
            d_gram = jnp.zeros((size, size), jnp.float32)
            for pair in range(heads // 2):
                span = slice(pair * 128, pair * 128 + 128)
                values = inputs_ref[rows_s, span]
                d_scan = dsc[rows_t, span]
                for h in (2 * pair, 2 * pair + 1):
                    mine = (lanes < HEAD) if h % 2 == 0 else (lanes >= HEAD)
                    spread = columns[:, 8 + h : 9 + h] - cum_s[h : h + 1]
                    decay = jnp.exp(jnp.minimum(spread, 0.0))
                    weights = (gram * decay).astype(half_type)
                    d_weights = dot_nt(jnp.where(mine, d_scan, jnp.zeros_like(d_scan)), values)
                    d_gram = d_gram + d_weights * decay
                    chans = slice(h * HEAD, h * HEAD + HEAD)
                    dint[chans, rows_s] += dot_nn(dst[chans, rows_t], weights)
            d_gram = jnp.where(allowed, d_gram, 0.0).astype(half_type)
            dbt[:, rows_s] += dot_nn(cbt[:, rows_t], d_gram)
            return total + dot_nn(d_gram, basis_ref[rows_s, :state])

        dcb[rows_t] = lax.fori_loop(0, i + 1, pair_block, jnp.zeros((size, state), jnp.float32))
        return carry

    lax.fori_loop(0, blocks, row_block, 0)

    step_size = rows_ref[0:8]
    raw = rows_ref[16:24]
    d_step, col_part = [], []
    for h in range(heads):
        chans = slice(h * HEAD, h * HEAD + HEAD)
        d_inputs = dint[chans]
        mixed = mixt[chans]
        scaled = step_size[h : h + 1] * mixed
        d_step.append(jnp.sum(d_inputs * mixed, axis=0, keepdims=True))
        inputs = scaled.astype(half_type).astype(jnp.float32)
        col_part.append(jnp.sum(d_inputs * inputs, axis=0, keepdims=True))
        dint[chans] = d_inputs * step_size[h : h + 1]
    blank = jnp.zeros((8 - heads, length), jnp.float32)
    d_step = jnp.concatenate(d_step + [blank], axis=0)
    d_cum = qrow[...] - jnp.concatenate(col_part + [blank], axis=0)
    d_log = scan_lanes(d_cum, True)
    rate = jnp.exp(rate_ref[:, 1:2])
    grad_rate = jnp.sum(d_log * (-step_size * rate), axis=1, keepdims=True)
    d_raw = (d_step - d_log * rate) * jax.nn.sigmoid(raw)
    d_raw = jnp.where(row_ids(8, length) < heads, d_raw, 0.0)
    grad_bias = jnp.sum(d_raw, axis=1, keepdims=True)
    lanes8 = lane_ids(8, 128)
    grads_ref[...] = jnp.where(lanes8 == 0, grad_bias, jnp.where(lanes8 == 1, grad_rate, 0.0))
    qrow[...] = d_raw

    def grad_block(a, carry):
        rows = pl.ds(pl.multiple_of(a * size, size), size)
        d_mixed = dint[:, rows].T + dcomb_ref[rows] * gain_ref[1:2]
        dpx[rows] = d_mixed * silu_slope(xpre_ref[rows])
        d_basis = jnp.concatenate([dbt[:, rows].T, dcb[rows]], axis=1)
        dpb[rows] = d_basis * silu_slope(bpre_ref[rows])
        return carry

    lax.fori_loop(0, blocks, grad_block, 0)

    def conv_block(a, carry):
        grad_x, grad_b = carry
        rows = pl.ds(pl.multiple_of(a * size, size), size)
        window = pl.ds(pl.multiple_of(a * size, size), size + 8)
        block = piece_at(a, at)
        keep_window = keep_ref[window]
        keep = keep_window[:size]
        d_wide = dpx[window]
        dproj_ref[block, :, :channels] = conv_back(d_wide, keep_window, taps_ref[...]).astype(
            half_type
        )
        grad_x = grad_x + conv_grads(d_wide[:size], xpad[window], keep)
        d_wide = dpb[window]
        dproj_ref[block, :, channels : channels + states] = conv_back(
            d_wide, keep_window, tapb_ref[...]
        ).astype(half_type)
        grad_b = grad_b + conv_grads(d_wide[:size], bpad[window], keep)
        d_steps = jnp.concatenate([qrow[:, rows], jnp.zeros((120, size), jnp.float32)], axis=0)
        dproj_ref[block, :, channels + states :] = d_steps.T.astype(half_type)
        return grad_x, grad_b

    grad_x, grad_b = lax.fori_loop(
        0,
        blocks,
        conv_block,
        (jnp.zeros((8, channels), jnp.float32), jnp.zeros((8, states), jnp.float32)),
    )
    gradx_ref[...] = grad_x
    gradb_ref[...] = grad_b


def stack_rows(pieces, out_ref):
    begin_at = 0
    for piece in pieces:
        out_ref[begin_at : begin_at + piece.shape[0]] = piece[...]
        begin_at = begin_at + piece.shape[0]


def project_body(count, order_ref, *refs):
    pieces, parts = refs[:4], refs[4 : 4 + count]
    first_ref, proj_ref, weight_ref, small_ref, taps_ref = refs[4 + count :]
    width = weight_ref.shape[0]
    rows = proj_ref.shape[1]
    states = taps_ref.shape[1]
    stack_rows(parts, weight_ref)
    small = weight_ref[:, weight_ref.shape[1] - 128 :].astype(jnp.float32).T[8:16]
    small_ref[...] = small
    gain = small[0:1]
    for p, piece in enumerate(pieces):
        first = (piece[:rows].astype(jnp.float32) * gain).astype(jnp.bfloat16)
        first_ref[p] = first
        proj_ref[p] = dot_nn(first, weight_ref[...])
    feature = row_ids(width, states)
    block = width // 8
    place = feature % block
    for b in range(8):
        place = place + jnp.where(feature // block == b, order_ref[b] * block, 0)
    channel = lane_ids(width, states)
    taps = []
    for k in range(CONV + 1):
        picked = jnp.where(place == channel * CONV + k % CONV, 1.0, 0.0).astype(jnp.bfloat16)
        found = dot_nn(small.astype(jnp.bfloat16), picked)
        taps.append(found[2:3] if k < CONV else found[3:4])
    taps.append(jnp.zeros((8 - len(taps), states), jnp.float32))
    taps_ref[...] = jnp.concatenate(taps, axis=0)


def product_body(_, values_ref, weight_ref, keep_ref, give_ref):
    rows = values_ref.shape[1]
    columns = slice(weight_ref.shape[1] - values_ref.shape[2], None)
    for p in (3, 1, 2, 0):
        result = dot_nt(values_ref[p], weight_ref[:, columns])
        if p < 2:
            keep_ref[p * rows : p * rows + rows] = result
        else:
            give_ref[p * rows - 2 * rows : p * rows - rows] = result.astype(jnp.bfloat16)


def first_back_body(_, attn_ref, scan_ref, late_ref, weight_ref, keep_ref, give_ref):
    rows = attn_ref.shape[1]
    wide = attn_ref.shape[2] - 128
    channels = wide - 128
    for p in (3, 1, 2, 0):
        result = dot_nt(attn_ref[p, :, :wide], late_ref[:, :wide])
        result = result + dot_nt(attn_ref[p, :, wide:], weight_ref[:, channels:wide])
        result = result + dot_nt(scan_ref[p, :, :channels], weight_ref[:, :channels])
        result = result + dot_nt(scan_ref[p, :, channels:], weight_ref[:, wide:])
        if p < 2:
            keep_ref[p * rows : p * rows + rows] = result
        else:
            give_ref[p * rows - 2 * rows : p * rows - rows] = result.astype(jnp.bfloat16)


def ffn_body(slots, fresh, _, *refs):
    pieces, cots = refs[0:2], refs[2:4]
    if fresh:
        parts, outs = refs[4:-7], refs[-7:]
        weight_ref = outs[6]
        stack_rows(parts, weight_ref)
    else:
        weight_ref, outs = refs[4], refs[-6:]
    second_ref, cot_ref, hidden_ref, dgu_ref, dkeep, dgive = outs[:6]
    hidden_local = hidden_ref.shape[2]
    rows = second_ref.shape[1]
    gate_up_weight = weight_ref.at[:, : 2 * hidden_local]
    down_weight = weight_ref.at[:, 2 * hidden_local :]
    for p, piece, cots_ref in zip(slots, pieces, cots):
        values, cot = piece[...], cots_ref[rows:]
        second_ref[p] = values
        cot_ref[p] = cot
        gate_up = dot_nn(values, gate_up_weight[...])
        d_hidden = dot_nn(cot, down_weight[...])
        gate, up = gate_up[:, :hidden_local], gate_up[:, hidden_local:]
        sig = jax.nn.sigmoid(gate)
        act = gate * sig
        hidden = (act * up).astype(jnp.bfloat16)
        hidden_ref[p] = hidden
        d_gate = (d_hidden * up * sig * (1.0 + gate * (1.0 - sig))).astype(jnp.bfloat16)
        d_up = (d_hidden * act).astype(jnp.bfloat16)
        dgu_ref[p, :, :hidden_local] = d_gate
        dgu_ref[p, :, hidden_local:] = d_up
        d_second = dot_nt(dgu_ref[p], gate_up_weight[...])
        if p < 2:
            dkeep[...] = d_second
        else:
            dgive[...] = d_second.astype(jnp.bfloat16)


def pack_body(turned, _, *refs):
    out_ref = refs[-1]
    begin_at = 0
    for index, ref in enumerate(refs[:-1]):
        values = ref[...]
        if index in turned:
            values = values.T
        out_ref[:, begin_at : begin_at + values.shape[1]] = values.astype(jnp.bfloat16)
        begin_at = begin_at + values.shape[1]


def shared_body(at_ref, mine_ref, near_ref, far_ref, cross_ref, step_ref, out_ref):
    at = at_ref[0]
    rows = mine_ref.shape[0]
    lanes = lane_ids(rows, 128)
    states = mine_ref.shape[1] - 384
    for j, ref in enumerate((mine_ref, near_ref, far_ref, cross_ref)):
        values = ref[...].astype(jnp.float32)
        here = pl.ds(pl.multiple_of((at ^ j) * rows, rows), rows)
        key, value = values[:, :128], values[:, 128:256]
        low = jnp.where(lanes < HEAD, key, pltpu.roll(value, HEAD, 1))
        high = jnp.where(lanes < HEAD, pltpu.roll(key, HEAD, 1), value)
        out_ref[here, :128] = jnp.where(at < 2, low, high).astype(jnp.bfloat16)
        out_ref[here, 128 : 128 + states] = values[:, 256 : 256 + states].astype(jnp.bfloat16)
        out_ref[here, 128 + states :] = (
            values[:, 256 + states :] + step_ref[here]
        ).astype(jnp.bfloat16)


def call_kernel(body, outs, scratch, *args, deps=(), micros=2, limit=32, aliases=None):
    shapes = [jax.ShapeDtypeStruct(shape, kind) for shape, kind in outs]
    count, extra = len(args), len(deps)
    whole = pl.BlockSpec(memory_space=pltpu.VMEM)

    def wrapped(*refs):
        body(*refs[:count], *refs[count + extra :])

    return pl.pallas_call(
        wrapped,
        out_shape=shapes,
        in_specs=[pl.BlockSpec(memory_space=pltpu.SMEM)]
        + [whole] * (count - 1)
        + [pl.BlockSpec(memory_space=pl.ANY)] * extra,
        out_specs=[whole] * len(shapes),
        scratch_shapes=[pltpu.VMEM(shape, kind) for shape, kind in scratch],
        input_output_aliases=aliases or {},
        compiler_params=pltpu.CompilerParams(vmem_limit_bytes=limit * 2**20),
        cost_estimate=pl.CostEstimate(
            flops=int(micros * 1e9), bytes_accessed=0, transcendentals=0
        ),
    )(*args, *deps)


def sequence_tables(seg_ids):
    length = seg_ids.shape[0]
    places = jnp.arange(length, dtype=jnp.int32)
    starts = jnp.where((places == 0) | (seg_ids != jnp.roll(seg_ids, 1)), places, 0)
    position = places - lax.cummax(starts, axis=0)
    half_dim = HEAD // 2
    frequency = jnp.exp(-jnp.log(ROPE_BASE) * jnp.arange(half_dim, dtype=jnp.float32) / half_dim)
    angles = position.astype(jnp.float32)[:, None] * frequency[None, :]
    cosine, sine = jnp.cos(angles), jnp.sin(angles)
    cosine = jnp.concatenate([cosine] * 4, axis=1)
    sine = jnp.concatenate([-sine, sine] * 2, axis=1)
    masks = [jnp.ones((length,), jnp.float32)]
    for lag in range(1, CONV):
        masks.append(
            ((places >= lag) & (seg_ids == jnp.roll(seg_ids, lag))).astype(jnp.float32)
        )
    masks = jnp.stack(masks + [jnp.zeros((length,), jnp.float32)] * (8 - CONV), axis=1)
    return cosine, sine, jnp.pad(masks, ((0, 8), (0, 0)))


def tap_rows(kernel, offset):
    taps = jnp.concatenate([kernel.T, offset[None, :]], axis=0)
    return jnp.pad(taps, ((0, 8 - taps.shape[0]), (0, 0)))


def shards(
    tokens,
    segment_ids,
    cotangent,
    norm_gain,
    w_z,
    w_x,
    w_bc,
    w_dt,
    conv_x,
    conv_bias_x,
    conv_bc,
    conv_bias_bc,
    dt_bias,
    a_log,
    d_skip,
    mixer_gain,
    w_mixer_out,
    w_query,
    w_keyval,
    w_attn_out,
    ffn_gain,
    w_gate,
    w_up,
    w_down,
):
    half_type = jnp.bfloat16
    full_type = jnp.float32
    rows, width = tokens.shape
    length = segment_ids.shape[0]
    channels = w_z.shape[1]
    heads = w_dt.shape[1]
    hidden_local = w_gate.shape[1]
    states = 2 * STATE
    blocks = length // rows

    row_count = w_bc.shape[0]
    gain_rows = norm_gain.shape[0]
    conv_rows = conv_bc.shape[0]
    at = lax.axis_index("tp").astype(jnp.int32).reshape(1)
    order = feature_order()
    x_at, core_at = place_bits()
    x_core = jnp.zeros((1,), jnp.int32)

    small = jnp.stack([norm_gain, ffn_gain, conv_bc.reshape(-1), jnp.repeat(conv_bias_bc, CONV)], 1)
    shared_in = jnp.concatenate(
        [w_keyval, w_bc, jnp.pad(small, ((0, 0), (8, 116)))], axis=1
    ).astype(half_type)
    step_wide = jnp.pad(w_dt, ((0, 0), (0, 128 - heads)))
    if staged():
        mine, far, near, cross = gather_pieces(shared_in)
        (shared_shard,) = call_kernel(
            shared_body,
            [((4 * row_count, states + 256), half_type)],
            [],
            at,
            mine,
            near,
            far,
            cross,
            step_wide,
            micros=1,
        )
    else:
        shared_all = lax.all_gather(shared_in, "tp", axis=0, tiled=True)
        key_rows, value_rows = (
            jnp.where(x_at == 0, shared_all[:, k : k + HEAD], shared_all[:, k + HEAD : k + 2 * HEAD])
            for k in (0, 128)
        )
        shared_shard = jnp.concatenate(
            [
                key_rows,
                value_rows,
                shared_all[:, 256 : 256 + states],
                shared_all[:, 256 + states :] + step_wide.astype(half_type),
            ],
            axis=1,
        )
    def pack(turned, *shards, deps=()):
        width_all = sum(shard.size for shard in shards) // w_x.shape[0]
        return call_kernel(
            functools.partial(pack_body, turned),
            [((w_x.shape[0], width_all), half_type)],
            [],
            x_core,
            *shards,
            deps=deps,
            micros=1,
        )[0]

    gather = Gather(jnp.concatenate([w_x.astype(half_type), shared_shard], axis=1))
    both_mine, tok_rows = call_kernel(
        front_body,
        [((2 * rows, width), half_type), ((rows, width), half_type)],
        [],
        order,
        tokens,
        cotangent,
        deps=[far] if staged() else [],
    )
    both = gather_pieces(both_mine)
    gather.step()
    second_step = gather.step()
    gather.step()
    late_gather = Gather(pack((2, 3), w_z, w_query, w_mixer_out, w_attn_out, deps=second_step))
    first_step = late_gather.step()
    second_step = late_gather.step()
    late_gather.step()
    ffn_gather = Gather(pack((2,), w_gate, w_up, w_down, deps=second_step))
    ffn_first = ffn_gather.step()

    cosine, sine, keep_masks = sequence_tables(segment_ids)
    seg_col, seg_row = segment_ids[:, None], segment_ids[None, :]
    taps_x = tap_rows(conv_x, conv_bias_x)
    rates = jnp.pad(jnp.stack([dt_bias, a_log], axis=1), ((0, 8 - heads), (0, 126)))
    gains = jnp.stack([mixer_gain, jnp.repeat(d_skip, channels // heads)])
    gains = jnp.pad(gains, ((0, 6), (0, 0)))

    row_half = ((rows, width), half_type)
    row_full = ((rows, width), full_type)
    parts = gather.parts()
    columns = channels + 128 + states + 128
    first_in, proj, weight, small_rows, taps_bc = call_kernel(
        functools.partial(project_body, len(parts)),
        [
            ((blocks, rows, width), half_type),
            ((blocks, rows, columns), full_type),
            ((width, columns), half_type),
            ((8, width), full_type),
            ((8, states), full_type),
        ],
        [],
        order,
        *both,
        *parts,
        micros=6,
    )
    gain_one, gain_two = small_rows[0:1], small_rows[1:2]

    scan_out, x_pre, bc_pre, basis, inputs, time_rows, time_cols = call_kernel(
        functools.partial(ssd_forward_body, heads),
        [
            ((length, channels), full_type),
            ((length, channels), full_type),
            ((length, states), full_type),
            ((length, states), half_type),
            ((length, channels), half_type),
            ((24, length), full_type),
            ((length, 128), full_type),
        ],
        [
            ((length + 8, channels), full_type),
            ((length + 8, states), full_type),
            ((8, length), full_type),
        ],
        at,
        proj,
        seg_col,
        seg_row,
        keep_masks,
        taps_x,
        taps_bc,
        rates,
        deps=[*first_step, *second_step],
        micros=11,
    )
    parts = late_gather.parts()
    head_half = ((length, 128), half_type)
    head_full = ((length, 128), full_type)
    cat, gate_in, query, keyk, valv, logs, inverse, late_weight = call_kernel(
        functools.partial(attend_forward_body, len(parts)),
        [
            ((blocks, rows, channels + 128), half_type),
            ((blocks, rows, channels), full_type),
            head_half,
            head_half,
            head_half,
            head_full,
            head_full,
            ((width, 2 * (channels + 128)), half_type),
        ],
        [],
        at,
        first_in,
        proj,
        scan_out,
        x_pre,
        seg_col,
        seg_row,
        cosine,
        sine,
        gains,
        *parts,
        deps=ffn_first,
        micros=9,
    )
    ffn_second = ffn_gather.step()

    def row_products(values, weight, deps=()):
        return call_kernel(
            product_body,
            [((2 * rows, width), full_type), ((2 * rows, width), half_type)],
            [],
            x_core,
            values,
            weight,
            deps=deps,
        )

    mix_terms = reduce_pieces(*row_products(cat, late_weight, deps=ffn_second))
    ffn_third = ffn_gather.step()
    after_mix, second_mine = call_kernel(
        mixed_body,
        [row_full, row_half],
        [],
        order,
        tok_rows,
        *mix_terms,
        gain_two,
        deps=ffn_third,
    )
    second = gather_pieces(second_mine)

    parts = ffn_gather.parts()
    filled = [
        ((blocks, rows, width), half_type),
        ((blocks, rows, width), half_type),
        ((blocks, rows, hidden_local), half_type),
        ((blocks, rows, 2 * hidden_local), half_type),
    ]
    sums = [row_full, row_half]
    *filled_in, d_keep, d_give, ffn_weight = call_kernel(
        functools.partial(ffn_body, (0, 2), True),
        filled + sums + [((width, 3 * hidden_local), half_type)],
        [],
        x_core,
        second[0],
        second[2],
        both[0],
        both[2],
        *parts,
        micros=5,
    )
    *filled_in, d_keep_x, d_give_x = call_kernel(
        functools.partial(ffn_body, (1, 3), False),
        filled + sums,
        [],
        x_core,
        second[1],
        second[3],
        both[1],
        both[3],
        ffn_weight,
        *filled_in,
        micros=5,
        aliases={6: 0, 7: 1, 8: 2, 9: 3},
    )
    second_in, cot_all, hidden, d_gate_up = (
        array.reshape(length, array.shape[2]) for array in filled_in
    )
    near = flip(d_give, "tp", 1)
    passed = d_keep_x + flip(d_give_x, "tp", 1).astype(full_type)
    d_second = d_keep, near, flip(passed.astype(half_type), "tp", 2)
    ffn_scatter = Scatter(
        [
            contract_rows(second_in, d_gate_up).astype(half_type),
            contract_rows(cot_all, hidden).astype(half_type),
        ]
    )

    d_after, d_mix = call_kernel(
        after_back_body,
        [row_full, row_half],
        [],
        order,
        after_mix,
        both_mine,
        *d_second,
        gain_two,
    )
    d_mix_all = gather_pieces(d_mix)
    ffn_steps = [ffn_scatter.step(3)]

    d_attn, d_comb, sums_mix, d_mix_whole = call_kernel(
        attend_backward_body,
        [
            ((blocks, rows, channels + 256), half_type),
            ((length, channels), full_type),
            ((8, channels), full_type),
            ((blocks, rows, width), half_type),
        ],
        [
            ((length, 128), full_type),
            ((length, 128), full_type),
            ((blocks, rows, channels + 128), full_type),
        ],
        at,
        gate_in,
        *d_mix_all,
        late_weight,
        scan_out,
        x_pre,
        seg_col,
        seg_row,
        cosine,
        sine,
        gains,
        query,
        keyk,
        valv,
        logs,
        inverse,
        deps=ffn_steps[0],
        micros=10,
    )
    ffn_steps.append(ffn_scatter.step(2))
    out_terms = reduce_pieces(*row_products(filled_in[2], ffn_weight, deps=d_mix_all[1:]))
    first_rows = first_in.reshape(length, width)
    attn_scatter = Scatter(
        [
            contract_rows(first_rows, d_attn.reshape(length, channels + 256)).astype(half_type),
            contract_rows(
                d_mix_whole.reshape(length, width), cat.reshape(length, channels + 128)
            ).astype(half_type),
        ]
    )
    d_scan, sums_x, sums_bc, sums_rate = call_kernel(
        functools.partial(ssd_backward_body, heads),
        [
            ((blocks, rows, channels + states + 128), half_type),
            ((8, channels), full_type),
            ((8, states), full_type),
            ((8, 128), full_type),
        ],
        [
            ((length + 8, channels), full_type),
            ((length + 8, states), full_type),
            ((length + 8, channels), full_type),
            ((length + 8, states), full_type),
            ((length, channels), half_type),
            ((channels, length), half_type),
            ((STATE, length), half_type),
            ((channels, length), full_type),
            ((channels, length), full_type),
            ((STATE, length), full_type),
            ((length, STATE), full_type),
            ((8, length), full_type),
        ],
        at,
        proj,
        d_comb,
        scan_out,
        seg_col,
        seg_row,
        keep_masks,
        taps_x,
        taps_bc,
        rates,
        gains,
        x_pre,
        bc_pre,
        basis,
        inputs,
        time_rows,
        time_cols,
        deps=ffn_steps[1],
        micros=18,
    )
    ffn_steps.append(ffn_scatter.step(1))
    ffn_sum = ffn_scatter.total()
    scan_scatter = Scatter(
        [
            contract_rows(
                first_rows, d_scan.reshape(length, channels + states + 128)
            ).astype(half_type)
        ]
    )
    keep, give = call_kernel(
        first_back_body,
        [((2 * rows, width), full_type), ((2 * rows, width), half_type)],
        [],
        x_core,
        d_attn,
        d_scan,
        late_weight,
        weight,
        deps=[out_terms[2]],
        micros=4,
    )
    d_first = reduce_pieces(keep, give)
    (grad_tokens,) = call_kernel(
        token_back_body,
        [row_full],
        [],
        order,
        tok_rows,
        d_after,
        *d_first,
        gain_one,
    )

    for dz in (3, 2, 1):
        attn_scatter.step(dz)
        scan_scatter.step(dz)
    attn_sum = attn_scatter.total()
    scan_sum = scan_scatter.total()
    out_sum = attn_sum[:, channels + 256 :]
    attn_sum = attn_sum[:, : channels + 256]

    (layer_out,) = call_kernel(
        output_body,
        [row_half],
        [],
        order,
        after_mix,
        *out_terms,
    )
    sum_x, sum_bc, sum_step = split_cols(scan_sum, [channels, states, heads])
    bc_rows = shared_shard[:, 128 : 128 + states]
    sum_z, sum_query, sum_keyval = split_cols(attn_sum, [channels, 128, 128])
    shared_rows = jnp.concatenate([sum_bc, sum_keyval], axis=1)
    shared_rows = shared_rows.reshape(2, 2, row_count, shared_rows.shape[1])
    keep = jnp.where(core_at == 0, shared_rows[:, 0], shared_rows[:, 1])
    give = jnp.where(core_at == 0, shared_rows[:, 1], shared_rows[:, 0])
    chip_rows = keep + flip(give, "tp", 1)
    keep = jnp.where(x_at == 0, chip_rows[0], chip_rows[1])
    give = jnp.where(x_at == 0, chip_rows[1], chip_rows[0])
    came = flip(give, "tp", 2)
    grad_bc = keep[:, :states] + came[:, :states]
    key_mine, value_mine = split_cols(keep[:, states:], [HEAD, HEAD])
    key_came, value_came = split_cols(came[:, states:], [HEAD, HEAD])
    grad_keyval = jnp.where(
        x_at == 0,
        jnp.concatenate([key_mine, key_came, value_mine, value_came], axis=1),
        jnp.concatenate([key_came, key_mine, value_came, value_mine], axis=1),
    )

    def weighted(grads, weights):
        weights = jnp.concatenate([weight.astype(half_type) for weight in weights], axis=1)
        return jnp.sum(grads * weights.astype(full_type), axis=1)

    by_row = [
        weighted(scan_sum[:, : channels + states + heads], [w_x, bc_rows[:, :states], w_dt])
        + weighted(attn_sum, [w_z, w_query, shared_shard[:, :128]]),
        weighted(ffn_sum[:, : 2 * hidden_local], [w_gate, w_up]),
    ]
    by_row = sum_tp(jnp.stack(by_row)).reshape(2, 4, gain_rows)
    by_row = lax.dynamic_index_in_dim(by_row, lax.axis_index("tp"), 1, keepdims=False)
    rounded = [gain.astype(half_type).astype(full_type) for gain in (norm_gain, ffn_gain)]
    sum_gain_one, sum_gain_two = by_row[0] / rounded[0], by_row[1] / rounded[1]

    common = sums_bc.reshape(-1)
    skips = sums_mix[1].reshape(heads, channels // heads).sum(axis=1)
    parts = [sums_x[:5].reshape(-1), sums_rate[:, :2].reshape(-1), skips, sums_mix[0]]
    flat = jnp.concatenate([sum_tp(common)] + parts)
    flat = jnp.pad(flat, (0, -flat.shape[0] % 1024)).reshape(-1, 128)
    flat = sum_fsdp(flat).reshape(-1)
    bc_sums = flat[: common.shape[0]].reshape(8, states)
    flat = flat[common.shape[0] :]
    device = lax.axis_index("fsdp") * 4 + lax.axis_index("tp")
    sum_conv = lax.dynamic_slice_in_dim(bc_sums[:4].T, device * conv_rows, conv_rows)
    sum_bias = lax.dynamic_slice_in_dim(bc_sums[4], device * conv_rows, conv_rows)
    x_sums = flat[: 5 * channels].reshape(5, channels)
    flat = flat[5 * channels :]
    rate_sums = flat[:16].reshape(8, 2)[:heads]
    skip_sums = flat[16 : 16 + heads]
    gain_sums = flat[16 + heads : 16 + heads + channels]
    sum_gate, sum_up, sum_down = split_cols(ffn_sum, [hidden_local] * 3)
    return (
        layer_out,
        grad_tokens,
        sum_gain_one,
        sum_z,
        sum_x,
        grad_bc,
        sum_step,
        x_sums[:4].T,
        x_sums[4],
        sum_conv,
        sum_bias,
        rate_sums[:, 0],
        rate_sums[:, 1],
        skip_sums,
        gain_sums,
        out_sum[:, :channels].T,
        sum_query,
        grad_keyval,
        out_sum[:, channels:].T,
        sum_gain_two,
        sum_gate,
        sum_up,
        sum_down.T,
    )


def solution(mesh):
    placed = (
        P(("fsdp", "tp"), None),
        P("fsdp"),
        P(("fsdp", "tp"), None),
        P(("fsdp", "tp")),
        P("fsdp", "tp"),
        P("fsdp", "tp"),
        P(("fsdp", "tp"), None),
        P("fsdp", "tp"),
        P("tp", None),
        P("tp"),
        P(("fsdp", "tp"), None),
        P(("fsdp", "tp")),
        P("tp"),
        P("tp"),
        P("tp"),
        P("tp"),
        P("tp", "fsdp"),
        P("fsdp", "tp"),
        P(("fsdp", "tp"), None),
        P("tp", "fsdp"),
        P(("fsdp", "tp")),
        P("fsdp", "tp"),
        P("fsdp", "tp"),
        P("tp", "fsdp"),
    )
    return jax.shard_map(
        shards,
        mesh=mesh,
        in_specs=placed,
        out_specs=(
            P(("fsdp", "tp"), None),
            P(("fsdp", "tp"), None),
            P(("fsdp", "tp")),
            P("fsdp", "tp"),
            P("fsdp", "tp"),
            P(("fsdp", "tp"), None),
            P("fsdp", "tp"),
            P("tp", None),
            P("tp"),
            P(("fsdp", "tp"), None),
            P(("fsdp", "tp")),
            P("tp"),
            P("tp"),
            P("tp"),
            P("tp"),
            P("tp", "fsdp"),
            P("fsdp", "tp"),
            P(("fsdp", "tp"), None),
            P("tp", "fsdp"),
            P(("fsdp", "tp")),
            P("fsdp", "tp"),
            P("fsdp", "tp"),
            P("tp", "fsdp"),
        ),
        check_vma=False,
    )
```

```python
import functools

import jax
import jax.numpy as jnp
from jax import lax
from jax.experimental import pallas as pl
from jax.experimental.pallas import tpu as pltpu
from jax.sharding import PartitionSpec as P

STATE = 128
CONV = 4
HEADS = 8
KV_HEADS = 2
HEAD = 64

EPS = 1e-06
ROPE_BASE = 10000.0
NEG_FILL = -1e30


def contract_rows(left_side, right_side):
    return lax.dot_general(
        left_side, right_side, (((0,), (0,)), ((), ())), preferred_element_type=jnp.float32
    )


def contract_cols(left_side, right_side):
    return lax.dot_general(
        left_side, right_side, (((1,), (1,)), ((), ())), preferred_element_type=jnp.float32
    )


def split_cols(matrix, widths):
    pieces = []
    begin_at = 0
    for part_width in widths:
        pieces.append(matrix[:, begin_at : begin_at + part_width])
        begin_at = begin_at + part_width
    return pieces


def flip(values, axis, mask):
    size = lax.axis_size(axis)
    return lax.ppermute(values, axis, [(i, i ^ mask) for i in range(size)])


def ring(values, step):
    return lax.ppermute(values, "fsdp", [(i, (i + 2 * step) % 8) for i in range(8)])


def staged():
    return lax.axis_size("fsdp") == 8


def place_bits():
    index = lax.axis_index("tp")
    return index // 2, index % 2


def gather_pieces(rows_in, late=False):
    far = flip(rows_in, "tp", 2)
    near = flip(after(rows_in, far) if late else rows_in, "tp", 1)
    cross = flip(far, "tp", 1)
    return rows_in, far, near, cross


def reduce_pieces(keep, give):
    half = keep.shape[0] // 2
    near = flip(give, "tp", 1)
    passed = (keep[half:] + near[half:].astype(jnp.float32)).astype(jnp.bfloat16)
    far = flip(passed, "tp", 2)
    return keep, near, far


def fsdp_place():
    index = lax.axis_index("fsdp")
    return index // 2, index % 2


def after(value, *deps):
    if not deps:
        return value

    def body(_, value_ref, out_ref):
        out_ref[...] = value_ref[...]

    return call_kernel(
        body, [(value.shape, value.dtype)], [], no_scalar(), value, deps=deps, micros=1, limit=8
    )[0]


def no_scalar():
    return jnp.zeros((1,), jnp.int32)


def block_of(grads, rows, dy, dz):
    at = (dy * 4 + dz) * rows
    return [grad[at : at + rows] for grad in grads]


def store_side_by_side(values, out_ref):
    begin_at = 0
    for value in values:
        out_ref[:, begin_at : begin_at + value.shape[1]] = value.astype(out_ref.dtype)
        begin_at = begin_at + value.shape[1]


def add_arrivals(values, arrivals):
    sums, begin_at = [], 0
    for value in values:
        columns = slice(begin_at, begin_at + value.shape[1])
        total = value.astype(jnp.float32)
        for arrival in arrivals:
            total = total + arrival[:, columns].astype(jnp.float32)
        sums.append(total)
        begin_at = begin_at + value.shape[1]
    return sums


def first_block_body(rows, _, *refs):
    store_side_by_side(block_of(refs[:-1], rows, 1, 3), refs[-1])


def step_body(count, rows, dz, _, *refs):
    grads, arrivals, (send_ref, next_ref) = refs[:count], refs[count:-2], refs[-2:]
    sums = add_arrivals(block_of(grads, rows, 0, dz), [ref[...] for ref in arrivals])
    store_side_by_side(sums, send_ref)
    store_side_by_side(block_of(grads, rows, 1, dz - 1), next_ref)


def total_body(count, rows, columns, weighted, _, *refs):
    grads, refs = refs[:count], refs[count:]
    outs = refs[-1 - len(columns) :]
    weights = refs[-1 - len(columns) - len(weighted) : -1 - len(columns)]
    arrivals = [ref[...] for ref in refs[: -1 - len(columns) - len(weighted)]]
    sums = add_arrivals(block_of(grads, rows, 0, 0) if rows else [grads[0][...]], arrivals)
    total = jnp.concatenate(sums, axis=1) if len(sums) > 1 else sums[0]
    by_row = jnp.zeros((total.shape[0], 1), jnp.float32)
    for begin_at, weight in zip(weighted, weights):
        values = total[:, begin_at : begin_at + weight.shape[1]]
        rounded = weight[...].astype(jnp.bfloat16).astype(jnp.float32)
        by_row = by_row + jnp.sum(values * rounded, axis=1, keepdims=True)
    for (begin_at, width, turned), out_ref in zip(columns, outs):
        values = total[:, begin_at : begin_at + width]
        out_ref[...] = values.T if turned else values
    outs[-1][...] = jnp.broadcast_to(by_row, outs[-1].shape)


class Scatter:
    def __init__(self, grads, *deps):
        self.grads = grads
        self.rows = grads[0].shape[0] // 8
        self.width = sum(grad.shape[1] for grad in grads)
        self.arrivals = []
        if staged():
            (first,) = call_kernel(
                functools.partial(first_block_body, self.rows),
                [((self.rows, self.width), jnp.bfloat16)],
                [],
                no_scalar(),
                *grads,
                deps=deps,
                micros=1,
                limit=16,
            )
            self.arrivals = [flip(first, "fsdp", 1)]

    def step(self, dz, *deps):
        if not staged():
            return ()
        block = ((self.rows, self.width), jnp.bfloat16)
        send, following = call_kernel(
            functools.partial(step_body, len(self.grads), self.rows, dz),
            [block, block],
            [],
            no_scalar(),
            *self.grads,
            *self.arrivals,
            deps=deps,
            micros=1,
            limit=16,
        )
        self.arrivals = [flip(following, "fsdp", 1), ring(send, 1)]
        return self.arrivals

    def total(self, columns, weighted, *weights):
        if staged():
            grads, rows = self.grads, self.rows
        else:
            grads = [
                lax.psum_scatter(
                    jnp.concatenate(self.grads, axis=1), "fsdp", scatter_dimension=0, tiled=True
                )
            ]
            rows = 0
        own = grads[0].shape[0] // 8 if rows else grads[0].shape[0]
        shapes = [
            ((width, own) if turned else (own, width), jnp.float32)
            for _, width, turned in columns
        ]
        return call_kernel(
            functools.partial(total_body, len(grads), rows, columns, weighted),
            shapes + [((own, 128), jnp.float32)],
            [],
            no_scalar(),
            *grads,
            *self.arrivals,
            *weights,
            micros=1,
        )


class Gather:
    def __init__(self, shard):
        self.shard = shard
        if staged():
            self.along, self.across = [shard], []

    def step(self, *deps):
        if not staged():
            return ()
        held = after(self.along[-1], *self.across[-1:], *deps)
        if len(self.along) < 4:
            self.along.append(ring(held, 1))
        self.across.append(flip(held, "fsdp", 1))
        return self.along[-1], self.across[-1]

    def parts(self):
        if not staged():
            return [lax.all_gather(self.shard, "fsdp", axis=0, tiled=True)]
        return [blocks[-dz % 4] for blocks in (self.along, self.across) for dz in range(4)]


def sum_fsdp(values):
    if not staged():
        return lax.psum(values, "fsdp")
    for mask in (1, 2, 6):
        values = values + flip(values, "fsdp", mask)
    return values


def sum_tp(values):
    for mask in (1, 2):
        values = values + flip(values, "tp", mask)
    return values


def feature_order():
    if not staged():
        return jnp.arange(8, dtype=jnp.int32)
    z_at, y_at = fsdp_place()
    steps = jnp.arange(8, dtype=jnp.int32)
    return (z_at + steps % 4) % 4 * 2 + (y_at ^ (steps // 4))


CHUNK = 32


def row_chunks(rows, body, carry=0):
    def step(k, carry):
        return body(pl.ds(pl.multiple_of(k * CHUNK, CHUNK), CHUNK), carry)

    return lax.fori_loop(0, rows // CHUNK, step, carry)


def front_body(order_ref, tok_ref, cot_ref, both_ref, tok_rel):
    rows_all, width = tok_ref.shape
    block = width // 8

    def chunk(rows, carry):
        below = pl.ds(pl.multiple_of(rows.start + rows_all, CHUNK), CHUNK)
        for b in range(8):
            there = pl.ds(pl.multiple_of(order_ref[b] * block, block), block)
            here = slice(b * block, b * block + block)
            tok_rel[rows, here] = tok_ref[rows, there]
            both_ref[below, here] = cot_ref[rows, there]
        values = tok_rel[rows].astype(jnp.float32)
        normed = values * lax.rsqrt(jnp.mean(values * values, axis=-1, keepdims=True) + EPS)
        both_ref[rows] = normed.astype(jnp.bfloat16)
        return carry

    row_chunks(rows_all, chunk)


def summed_rows(rows, keep_ref, near_ref, far_ref):
    return (
        keep_ref[rows] + near_ref[rows].astype(jnp.float32) + far_ref[rows].astype(jnp.float32)
    )


def mixed_body(_, tok_ref, keep_ref, near_ref, far_ref, gain_ref, after_ref, second_ref):
    def chunk(rows, carry):
        after = tok_ref[rows].astype(jnp.float32) + summed_rows(rows, keep_ref, near_ref, far_ref)
        after_ref[rows] = after
        normed = after * lax.rsqrt(jnp.mean(after * after, axis=-1, keepdims=True) + EPS)
        second_ref[rows] = (normed * gain_ref[...]).astype(jnp.bfloat16)
        return carry

    row_chunks(tok_ref.shape[0], chunk)


def output_body(order_ref, after_ref, keep_ref, near_ref, far_ref, out_ref):
    block = after_ref.shape[1] // 8

    def chunk(rows, carry):
        values = after_ref[rows] + summed_rows(rows, keep_ref, near_ref, far_ref)
        values = values.astype(jnp.bfloat16)
        for b in range(8):
            there = pl.ds(pl.multiple_of(order_ref[b] * block, block), block)
            out_ref[rows, there] = values[:, b * block : b * block + block]
        return carry

    row_chunks(after_ref.shape[0], chunk)


def norm_back(values, d_out, gain):
    inverse = lax.rsqrt(jnp.mean(values * values, axis=-1, keepdims=True) + EPS)
    normed = values * inverse
    scaled = d_out * gain
    return inverse * (scaled - normed * jnp.mean(scaled * normed, axis=-1, keepdims=True))


def after_back_body(
    _, after_ref, cot_ref, keep_ref, near_ref, far_ref, gain_ref, d_after_ref, d_mix_ref
):
    def chunk(rows, carry):
        d_second = summed_rows(rows, keep_ref, near_ref, far_ref)
        lower = pl.ds(pl.multiple_of(rows.start + after_ref.shape[0], CHUNK), CHUNK)
        d_after = cot_ref[lower].astype(jnp.float32) + norm_back(
            after_ref[rows], d_second, gain_ref[...]
        )
        d_after_ref[rows] = d_after
        d_mix_ref[rows] = d_after.astype(jnp.bfloat16)
        return carry

    row_chunks(after_ref.shape[0], chunk)


def token_back_body(
    order_ref, tok_ref, d_after_ref, keep_ref, near_ref, far_ref, gain_ref, out_ref
):
    block = tok_ref.shape[1] // 8

    def chunk(rows, carry):
        d_first = summed_rows(rows, keep_ref, near_ref, far_ref)
        values = d_after_ref[rows] + norm_back(
            tok_ref[rows].astype(jnp.float32), d_first, gain_ref[...]
        )
        for b in range(8):
            there = pl.ds(pl.multiple_of(order_ref[b] * block, block), block)
            out_ref[rows, there] = values[:, b * block : b * block + block]
        return carry

    row_chunks(tok_ref.shape[0], chunk)


def piece_at(block, at):
    apart = block ^ at
    return (apart & 1) * 2 + (apart >> 1)


def head_lanes(columns, first, lanes):
    rows = columns.shape[0]
    even = jnp.broadcast_to(columns[:, first : first + 1], (rows, 128))
    odd = jnp.broadcast_to(columns[:, first + 1 : first + 2], (rows, 128))
    return jnp.where(lanes < HEAD, even, odd)


def lane_ids(rows, cols):
    return lax.broadcasted_iota(jnp.int32, (rows, cols), 1)


def row_ids(rows, cols):
    return lax.broadcasted_iota(jnp.int32, (rows, cols), 0)


def dot_nt(left_side, right_side, **kw):
    return lax.dot_general(
        left_side, right_side, (((1,), (1,)), ((), ())), preferred_element_type=jnp.float32, **kw
    )


def dot_nn(left_side, right_side):
    return jnp.dot(left_side, right_side, preferred_element_type=jnp.float32)


def dot_tn(left_side, right_side):
    return lax.dot_general(
        left_side, right_side, (((0,), (0,)), ((), ())), preferred_element_type=jnp.float32
    )


def conv_window(window, taps, offset, keep):
    rows = window.shape[0] - 8
    summed = window[8:] * taps[CONV - 1 : CONV] + offset
    for lag in range(1, CONV):
        summed = summed + window[8 - lag : 8 - lag + rows] * keep[:, lag : lag + 1] * (
            taps[CONV - 1 - lag : CONV - lag]
        )
    return summed


def log_one_plus(values):
    ratio = values / (2.0 + values)
    square = ratio * ratio
    series = jnp.full_like(values, 1.0 / 15.0)
    for odd in (13, 11, 9, 7, 5, 3, 1):
        series = series * square + 1.0 / odd
    return 2.0 * ratio * series


def scan_lanes(values, reverse):
    length = values.shape[1]
    lanes = lane_ids(*values.shape)
    step = 1
    while step < length:
        if reverse:
            moved = jnp.where(lanes < length - step, pltpu.roll(values, length - step, 1), 0.0)
        else:
            moved = jnp.where(lanes >= step, pltpu.roll(values, step, 1), 0.0)
        values = values + moved
        step = step * 2
    return values


def pair_mask(seg_col, seg_row, at_t, at_s):
    size = seg_col.shape[0]
    rows = row_ids(size, size) + at_t * size
    cols = lane_ids(size, size) + at_s * size
    return (seg_col == seg_row) & (rows >= cols)


def swap_halves(values, lanes):
    half = HEAD // 2
    return jnp.where(
        lanes % HEAD < half, pltpu.roll(values, 128 - half, 1), pltpu.roll(values, half, 1)
    )


def ssd_forward_body(
    heads,
    at_ref,
    proj_ref,
    segc_ref,
    segr_ref,
    keep_ref,
    taps_ref,
    tapb_ref,
    rate_ref,
    scan_ref,
    xpre_ref,
    bpre_ref,
    basis_ref,
    inputs_ref,
    rows_ref,
    cols_ref,
    xpad,
    bpad,
    dtr,
):
    blocks, size = proj_ref.shape[0], proj_ref.shape[1]
    channels = xpre_ref.shape[1]
    states = bpre_ref.shape[1]
    tail = proj_ref.shape[2] - states - 128
    at = at_ref[0]
    xpad[0:8] = jnp.zeros((8, channels), jnp.float32)
    bpad[0:8] = jnp.zeros((8, states), jnp.float32)

    def load(a, carry):
        rows = pl.ds(pl.multiple_of(a * size + 8, 8), size)
        block = piece_at(a, at)
        xpad[rows] = proj_ref[block, :, :channels]
        bpad[rows] = proj_ref[block, :, tail : tail + states]
        steps = proj_ref[block, :, tail + states :]
        dtr[:, pl.ds(pl.multiple_of(a * size, size), size)] = steps.T[0:8]
        return carry

    lax.fori_loop(0, blocks, load, 0)
    raw = dtr[...] + rate_ref[:, 0:1]
    step_size = jnp.maximum(raw, 0.0) + log_one_plus(jnp.exp(-jnp.abs(raw)))
    log_rate = -step_size * jnp.exp(rate_ref[:, 1:2])
    cum = scan_lanes(log_rate, False)
    length = raw.shape[1]
    rows_ref[0:8] = step_size
    rows_ref[8:16] = cum
    rows_ref[16:24] = raw
    cols_ref[...] = jnp.concatenate(
        [step_size, cum, jnp.zeros((112, length), jnp.float32)], axis=0
    ).T
    lanes = lane_ids(size, 128)

    def prepare_block(a, carry):
        window = pl.ds(pl.multiple_of(a * size, size), size + 8)
        rows = pl.ds(pl.multiple_of(a * size, size), size)
        keep = keep_ref[rows]
        columns = cols_ref[rows]
        bpre = conv_window(bpad[window], tapb_ref[0:4], tapb_ref[4:5], keep)
        bpre_ref[rows] = bpre
        basis_ref[rows] = (bpre * jax.nn.sigmoid(bpre)).astype(jnp.bfloat16)
        for pair in range(channels // 128):
            span = slice(pair * 128, pair * 128 + 128)
            xpre = conv_window(xpad[window, span], taps_ref[0:4, span], taps_ref[4:5, span], keep)
            xpre_ref[rows, span] = xpre
            mixed = (xpre * jax.nn.sigmoid(xpre)).astype(jnp.bfloat16).astype(jnp.float32)
            steps = head_lanes(columns, 2 * pair, lanes)
            inputs_ref[rows, span] = (steps * mixed).astype(jnp.bfloat16)
        return carry

    lax.fori_loop(0, blocks, prepare_block, 0)
    state = states // 2

    def row_block(i, carry):
        rows_t = pl.ds(pl.multiple_of(i * size, size), size)
        basis_c = basis_ref[rows_t, state:]
        seg_t = segc_ref[rows_t]
        columns = cols_ref[rows_t]

        def pair_block(j, totals):
            rows_s = pl.ds(pl.multiple_of(j * size, size), size)
            allowed = pair_mask(seg_t, segr_ref[:, rows_s], i, j)
            gram = jnp.where(allowed, dot_nt(basis_c, basis_ref[rows_s, :state]), 0.0)
            cum_s = rows_ref[8:16, rows_s]
            fresh = []
            for pair in range(heads // 2):
                values = inputs_ref[rows_s, pair * 128 : pair * 128 + 128]
                outs = []
                for h in (2 * pair, 2 * pair + 1):
                    spread = columns[:, 8 + h : 9 + h] - cum_s[h : h + 1]
                    weights = (gram * jnp.exp(jnp.minimum(spread, 0.0))).astype(jnp.bfloat16)
                    outs.append(dot_nn(weights, values))
                fresh.append(totals[pair] + jnp.where(lanes < HEAD, outs[0], outs[1]))
            return tuple(fresh)

        zero = jnp.zeros((size, 128), jnp.float32)
        totals = lax.fori_loop(0, i + 1, pair_block, (zero,) * (heads // 2))
        for pair in range(heads // 2):
            scan_ref[rows_t, pair * 128 : pair * 128 + 128] = totals[pair]
        return carry

    lax.fori_loop(0, blocks, row_block, 0)


def attend_forward_body(
    count,
    at_ref,
    first_ref,
    proj_ref,
    scan_ref,
    xpre_ref,
    segc_ref,
    segr_ref,
    cos_ref,
    sin_ref,
    gain_ref,
    *refs,
):
    parts = refs[:count]
    cat_ref, gate_ref, query_ref, keyk_ref, valv_ref, logs_ref, inv_ref, weight_ref = refs[count:]
    stack_rows(parts, weight_ref)
    blocks, size = proj_ref.shape[0], proj_ref.shape[1]
    channels = scan_ref.shape[1]
    at = at_ref[0]
    lanes = lane_ids(size, 128)
    half_type = jnp.bfloat16

    def finish_block(a, carry):
        rows = pl.ds(pl.multiple_of(a * size, size), size)
        block = piece_at(a, at)
        xpre = xpre_ref[rows]
        mixed = (xpre * jax.nn.sigmoid(xpre)).astype(half_type).astype(jnp.float32)
        mine = dot_nn(first_ref[block], weight_ref[:, : channels + 128])
        gate, query = mine[:, :channels], mine[:, channels:]
        gate_ref[block] = gate
        gated = (scan_ref[rows] + gain_ref[1:2] * mixed) * (gate * jax.nn.sigmoid(gate))
        inverse = lax.rsqrt(jnp.mean(gated * gated, axis=-1, keepdims=True) + EPS)
        inv_ref[rows] = jnp.broadcast_to(inverse, (size, 128))
        cat_ref[block, :, :channels] = (gated * inverse * gain_ref[0:1]).astype(half_type)
        cosine, sine = cos_ref[rows], sin_ref[rows]
        query_ref[rows] = (query * cosine + swap_halves(query, lanes) * sine).astype(half_type)
        keyval = proj_ref[block, :, channels : channels + 128]
        keyval = keyval * jnp.where(lanes < HEAD, cosine, 1.0) + swap_halves(
            keyval, lanes
        ) * jnp.where(lanes < HEAD, sine, 0.0)
        moved = pltpu.roll(keyval, HEAD, 1)
        keyk_ref[rows] = jnp.where(lanes < HEAD, keyval, moved).astype(half_type)
        valv_ref[rows] = jnp.where(lanes < HEAD, moved, keyval).astype(half_type)
        return carry

    lax.fori_loop(0, blocks, finish_block, 0)
    for i in range(blocks):
        width = (i + 1) * size
        rows = slice(i * size, width)
        query = query_ref[rows]
        places = row_ids(size, width) + i * size
        allowed = (segc_ref[rows] == segr_ref[:, :width]) & (places >= lane_ids(size, width))
        outs, logs = [], []
        for h in range(2):
            mine = (lanes < HEAD) if h == 0 else (lanes >= HEAD)
            masked = jnp.where(mine, query, jnp.zeros_like(query))
            scores = dot_nt(masked, keyk_ref[:width]) * HEAD ** (-0.5)
            scores = jnp.where(allowed, scores, NEG_FILL)
            top = jnp.max(scores, axis=-1, keepdims=True)
            powers = jnp.exp(scores - top)
            total = jnp.sum(powers, axis=-1, keepdims=True)
            outs.append(dot_nn(powers.astype(half_type), valv_ref[:width]) / total)
            logs.append(top + jnp.log(total))
        cat_ref[piece_at(i, at), :, channels:] = jnp.where(lanes < HEAD, outs[0], outs[1]).astype(half_type)
        logs_ref[rows] = jnp.where(lanes < HEAD, logs[0], logs[1])


def gate_backward_body(
    at_ref,
    gate_ref,
    mine_ref,
    far_ref,
    near_ref,
    cross_ref,
    weight_ref,
    scan_ref,
    xpre_ref,
    gain_ref,
    inv_ref,
    dgate_ref,
    dcomb_ref,
    small_ref,
    dmix_ref,
    datt_ref,
):
    blocks, size = gate_ref.shape[0], gate_ref.shape[1]
    channels = scan_ref.shape[1]
    at = at_ref[0]
    half_type = jnp.bfloat16
    wide = channels + 128
    for p, piece in enumerate((mine_ref, far_ref, near_ref, cross_ref)):
        dmix_ref[p] = piece[...]

    def finish_block(a, carry):
        grad_gain, grad_skip = carry
        rows = pl.ds(pl.multiple_of(a * size, size), size)
        block = piece_at(a, at)
        d_cat = dot_nn(dmix_ref[block], weight_ref[:, weight_ref.shape[1] - wide :])
        datt_ref[rows] = d_cat[:, channels:].astype(half_type)
        xpre = xpre_ref[rows]
        mixed = (xpre * jax.nn.sigmoid(xpre)).astype(half_type).astype(jnp.float32)
        gate = gate_ref[block]
        sig = jax.nn.sigmoid(gate)
        act = gate * sig
        combined = scan_ref[rows] + gain_ref[1:2] * mixed
        inverse = inv_ref[rows, 0:1]
        normed = combined * act * inverse
        d_out = d_cat[:, :channels]
        grad_gain = grad_gain + jnp.sum(d_out * normed, axis=0, keepdims=True)
        scaled = d_out * gain_ref[0:1]
        d_gated = inverse * (scaled - normed * jnp.mean(scaled * normed, axis=-1, keepdims=True))
        d_comb = d_gated * act
        dcomb_ref[rows] = d_comb
        grad_skip = grad_skip + jnp.sum(d_comb * mixed, axis=0, keepdims=True)
        d_gate = d_gated * combined * sig * (1.0 + gate * (1.0 - sig))
        dgate_ref[block] = d_gate.astype(half_type)
        return grad_gain, grad_skip

    zero = jnp.zeros((1, channels), jnp.float32)
    grad_gain, grad_skip = lax.fori_loop(0, blocks, finish_block, (zero, zero))
    small_ref[...] = jnp.concatenate(
        [grad_gain, grad_skip, jnp.zeros((6, channels), jnp.float32)], axis=0
    )


def attend_backward_body(
    at_ref,
    datt_ref,
    segc_ref,
    segr_ref,
    cos_ref,
    sin_ref,
    query_ref,
    keyk_ref,
    valv_ref,
    logs_ref,
    dproj_ref,
    dkey,
    dval,
):
    blocks, size = dproj_ref.shape[0], dproj_ref.shape[1]
    at = at_ref[0]
    lanes = lane_ids(size, 128)
    half_type = jnp.bfloat16
    dkey[...] = jnp.zeros_like(dkey)
    dval[...] = jnp.zeros_like(dval)
    for i in range(blocks):
        width = (i + 1) * size
        rows = slice(i * size, width)
        query = query_ref[rows]
        d_att = datt_ref[rows]
        logs = logs_ref[rows]
        places = row_ids(size, width) + i * size
        allowed = (segc_ref[rows] == segr_ref[:, :width]) & (places >= lane_ids(size, width))
        outs = []
        for h in range(2):
            mine = (lanes < HEAD) if h == 0 else (lanes >= HEAD)
            masked = jnp.where(mine, query, jnp.zeros_like(query))
            d_masked = jnp.where(mine, d_att, jnp.zeros_like(d_att))
            scores = dot_nt(masked, keyk_ref[:width]) * HEAD ** (-0.5)
            scores = jnp.where(allowed, scores, NEG_FILL)
            probs = jnp.exp(scores - logs[:, h * HEAD : h * HEAD + 1])
            d_probs = dot_nt(d_masked, valv_ref[:width])
            mean = jnp.sum(probs * d_probs, axis=-1, keepdims=True)
            d_scores = (probs * (d_probs - mean)).astype(half_type)
            outs.append(dot_nn(d_scores, keyk_ref[:width]))
            dkey[:width] += dot_tn(d_scores, masked)
            dval[:width] += dot_tn(probs.astype(half_type), d_masked)
        d_query = jnp.where(lanes < HEAD, outs[0], outs[1]) * HEAD ** (-0.5)
        cosine, sine = cos_ref[rows], sin_ref[rows]
        d_query = d_query * cosine - swap_halves(d_query, lanes) * sine
        dproj_ref[piece_at(i, at), :, :128] = d_query.astype(half_type)

    def key_block(a, carry):
        rows = pl.ds(pl.multiple_of(a * size, size), size)
        d_key, d_val = dkey[rows], dval[rows]
        d_key = (d_key + pltpu.roll(d_key, HEAD, 1)) * HEAD ** (-0.5)
        d_val = d_val + pltpu.roll(d_val, HEAD, 1)
        d_key = d_key * cos_ref[rows] - swap_halves(d_key, lanes) * sin_ref[rows]
        dproj_ref[piece_at(a, at), :, 128:] = jnp.where(lanes < HEAD, d_key, d_val).astype(
            half_type
        )
        return carry

    lax.fori_loop(0, blocks, key_block, 0)


def silu_slope(values):
    sig = jax.nn.sigmoid(values)
    return sig * (1.0 + values * (1.0 - sig))


def conv_back(d_window, keep_window, taps):
    rows = d_window.shape[0] - 8
    summed = d_window[:rows] * taps[CONV - 1 : CONV]
    for lag in range(1, CONV):
        moved = d_window * keep_window[:, lag : lag + 1]
        summed = summed + moved[lag : lag + rows] * taps[CONV - 1 - lag : CONV - lag]
    return summed


def conv_grads(d_pre, window, keep):
    rows = d_pre.shape[0]
    sums = []
    for tap in range(CONV):
        lag = CONV - 1 - tap
        moved = window[8 - lag : 8 - lag + rows]
        if lag:
            moved = moved * keep[:, lag : lag + 1]
        sums.append(jnp.sum(d_pre * moved, axis=0, keepdims=True))
    sums.append(jnp.sum(d_pre, axis=0, keepdims=True))
    sums.append(jnp.zeros((8 - len(sums), d_pre.shape[1]), jnp.float32))
    return jnp.concatenate(sums, axis=0)


def ssd_backward_body(
    heads,
    at_ref,
    dcomb_ref,
    scan_ref,
    segc_ref,
    segr_ref,
    xpre_ref,
    basis_ref,
    inputs_ref,
    rows_ref,
    cols_ref,
    dint,
    dbt,
    dcb,
    qrow,
    mixt,
    dsc,
    dst,
    cbt,
):
    length, channels = scan_ref.shape
    state = dbt.shape[0]
    size = length // 4
    blocks = 4
    half_type = jnp.bfloat16
    lanes = lane_ids(size, 128)
    dint[...] = jnp.zeros_like(dint)
    dbt[...] = jnp.zeros_like(dbt)
    head_of = jnp.where(
        lane_ids(8, channels) // HEAD == row_ids(8, channels), 1.0, 0.0
    ).astype(jnp.float32)

    def load(a, carry):
        rows = pl.ds(pl.multiple_of(a * size, size), size)
        d_scan = dcomb_ref[rows].astype(half_type)
        dsc[rows] = d_scan
        d_full = d_scan.astype(jnp.float32)
        dst[:, rows] = d_full.T.astype(half_type)
        cbt[:, rows] = basis_ref[rows, state:].astype(jnp.float32).T.astype(half_type)
        xpre = xpre_ref[rows]
        mixed = (xpre * jax.nn.sigmoid(xpre)).astype(half_type).astype(jnp.float32)
        mixt[:, rows] = mixed.T
        qrow[:, rows] = dot_nt(head_of, d_full * scan_ref[rows], precision=lax.Precision.HIGHEST)
        return carry

    lax.fori_loop(0, blocks, load, 0)

    def row_block(i, carry):
        rows_t = pl.ds(pl.multiple_of(i * size, size), size)
        basis_c = basis_ref[rows_t, state:]
        seg_t = segc_ref[rows_t]
        columns = cols_ref[rows_t]

        def pair_block(j, total):
            rows_s = pl.ds(pl.multiple_of(j * size, size), size)
            allowed = pair_mask(seg_t, segr_ref[:, rows_s], i, j)
            gram = jnp.where(allowed, dot_nt(basis_c, basis_ref[rows_s, :state]), 0.0)
            cum_s = rows_ref[8:16, rows_s]
            d_gram = jnp.zeros((size, size), jnp.float32)
            for pair in range(heads // 2):
                span = slice(pair * 128, pair * 128 + 128)
                values = inputs_ref[rows_s, span]
                d_scan = dsc[rows_t, span]
                for h in (2 * pair, 2 * pair + 1):
                    mine = (lanes < HEAD) if h % 2 == 0 else (lanes >= HEAD)
                    spread = columns[:, 8 + h : 9 + h] - cum_s[h : h + 1]
                    decay = jnp.exp(jnp.minimum(spread, 0.0))
                    weights = (gram * decay).astype(half_type)
                    d_weights = dot_nt(jnp.where(mine, d_scan, jnp.zeros_like(d_scan)), values)
                    d_gram = d_gram + d_weights * decay
                    chans = slice(h * HEAD, h * HEAD + HEAD)
                    dint[chans, rows_s] += dot_nn(dst[chans, rows_t], weights)
            d_gram = jnp.where(allowed, d_gram, 0.0).astype(half_type)
            dbt[:, rows_s] += dot_nn(cbt[:, rows_t], d_gram)
            return total + dot_nn(d_gram, basis_ref[rows_s, :state])

        dcb[rows_t] = lax.fori_loop(0, i + 1, pair_block, jnp.zeros((size, state), jnp.float32))
        return carry

    lax.fori_loop(0, blocks, row_block, 0)


def conv_backward_body(
    heads,
    at_ref,
    proj_ref,
    dcomb_ref,
    keep_ref,
    taps_ref,
    tapb_ref,
    rate_ref,
    gain_ref,
    xpre_ref,
    bpre_ref,
    rows_ref,
    dint_ref,
    dbt,
    dcb,
    qrow_ref,
    mixt,
    dproj_ref,
    gradx_ref,
    gradb_ref,
    grads_ref,
    xpad,
    bpad,
    dpx,
    dpb,
    dint,
    qrow,
):
    blocks, size = proj_ref.shape[0], proj_ref.shape[1]
    channels = xpre_ref.shape[1]
    states = bpre_ref.shape[1]
    tail = proj_ref.shape[2] - states - 128
    length = blocks * size
    at = at_ref[0]
    half_type = jnp.bfloat16
    xpad[0:8] = jnp.zeros((8, channels), jnp.float32)
    bpad[0:8] = jnp.zeros((8, states), jnp.float32)
    dpx[length : length + 8] = jnp.zeros((8, channels), jnp.float32)
    dpb[length : length + 8] = jnp.zeros((8, states), jnp.float32)

    def load(a, carry):
        padded = pl.ds(pl.multiple_of(a * size + 8, 8), size)
        block = piece_at(a, at)
        xpad[padded] = proj_ref[block, :, :channels]
        bpad[padded] = proj_ref[block, :, tail : tail + states]
        return carry

    lax.fori_loop(0, blocks, load, 0)
    step_size = rows_ref[0:8]
    raw = rows_ref[16:24]
    d_step, col_part = [], []
    for h in range(heads):
        chans = slice(h * HEAD, h * HEAD + HEAD)
        d_inputs = dint_ref[chans]
        mixed = mixt[chans]
        scaled = step_size[h : h + 1] * mixed
        d_step.append(jnp.sum(d_inputs * mixed, axis=0, keepdims=True))
        inputs = scaled.astype(half_type).astype(jnp.float32)
        col_part.append(jnp.sum(d_inputs * inputs, axis=0, keepdims=True))
        dint[chans] = d_inputs * step_size[h : h + 1]
    blank = jnp.zeros((8 - heads, length), jnp.float32)
    d_step = jnp.concatenate(d_step + [blank], axis=0)
    d_cum = qrow_ref[...] - jnp.concatenate(col_part + [blank], axis=0)
    d_log = scan_lanes(d_cum, True)
    rate = jnp.exp(rate_ref[:, 1:2])
    grad_rate = jnp.sum(d_log * (-step_size * rate), axis=1, keepdims=True)
    d_raw = (d_step - d_log * rate) * jax.nn.sigmoid(raw)
    d_raw = jnp.where(row_ids(8, length) < heads, d_raw, 0.0)
    grad_bias = jnp.sum(d_raw, axis=1, keepdims=True)
    lanes8 = lane_ids(8, 128)
    grads_ref[...] = jnp.where(lanes8 == 0, grad_bias, jnp.where(lanes8 == 1, grad_rate, 0.0))
    qrow[...] = d_raw

    def grad_block(a, carry):
        rows = pl.ds(pl.multiple_of(a * size, size), size)
        d_mixed = dint[:, rows].T + dcomb_ref[rows] * gain_ref[1:2]
        dpx[rows] = d_mixed * silu_slope(xpre_ref[rows])
        d_basis = jnp.concatenate([dbt[:, rows].T, dcb[rows]], axis=1)
        dpb[rows] = d_basis * silu_slope(bpre_ref[rows])
        return carry

    lax.fori_loop(0, blocks, grad_block, 0)

    def conv_block(a, carry):
        grad_x, grad_b = carry
        rows = pl.ds(pl.multiple_of(a * size, size), size)
        window = pl.ds(pl.multiple_of(a * size, size), size + 8)
        block = piece_at(a, at)
        keep_window = keep_ref[window]
        keep = keep_window[:size]
        d_wide = dpx[window]
        dproj_ref[block, :, :channels] = conv_back(d_wide, keep_window, taps_ref[...]).astype(
            half_type
        )
        grad_x = grad_x + conv_grads(d_wide[:size], xpad[window], keep)
        d_wide = dpb[window]
        dproj_ref[block, :, channels : channels + states] = conv_back(
            d_wide, keep_window, tapb_ref[...]
        ).astype(half_type)
        grad_b = grad_b + conv_grads(d_wide[:size], bpad[window], keep)
        d_steps = jnp.concatenate([qrow[:, rows], jnp.zeros((120, size), jnp.float32)], axis=0)
        dproj_ref[block, :, channels + states :] = d_steps.T.astype(half_type)
        return grad_x, grad_b

    grad_x, grad_b = lax.fori_loop(
        0,
        blocks,
        conv_block,
        (jnp.zeros((8, channels), jnp.float32), jnp.zeros((8, states), jnp.float32)),
    )
    gradx_ref[...] = grad_x
    gradb_ref[...] = grad_b


def stack_rows(pieces, out_ref):
    begin_at = 0
    for piece in pieces:
        out_ref[begin_at : begin_at + piece.shape[0]] = piece[...]
        begin_at = begin_at + piece.shape[0]


def project_body(count, order_ref, *refs):
    pieces, parts = refs[:4], refs[4 : 4 + count]
    first_ref, proj_ref, weight_ref, small_ref, taps_ref = refs[4 + count :]
    width = weight_ref.shape[0]
    rows = proj_ref.shape[1]
    states = taps_ref.shape[1]
    stack_rows(parts, weight_ref)
    small = weight_ref[:, weight_ref.shape[1] - 128 :].astype(jnp.float32).T[8:16]
    small_ref[...] = small
    gain = small[0:1]
    for p, piece in enumerate(pieces):
        first = (piece[:rows].astype(jnp.float32) * gain).astype(jnp.bfloat16)
        first_ref[p] = first
        proj_ref[p] = dot_nn(first, weight_ref[...])
    feature = row_ids(width, states)
    block = width // 8
    place = feature % block
    for b in range(8):
        place = place + jnp.where(feature // block == b, order_ref[b] * block, 0)
    channel = lane_ids(width, states)
    taps = []
    for k in range(CONV + 1):
        picked = jnp.where(place == channel * CONV + k % CONV, 1.0, 0.0).astype(jnp.bfloat16)
        found = dot_nn(small.astype(jnp.bfloat16), picked)
        taps.append(found[2:3] if k < CONV else found[3:4])
    taps.append(jnp.zeros((8 - len(taps), states), jnp.float32))
    taps_ref[...] = jnp.concatenate(taps, axis=0)


def product_body(_, values_ref, weight_ref, keep_ref, give_ref):
    rows = values_ref.shape[1]
    columns = slice(weight_ref.shape[1] - values_ref.shape[2], None)
    for p in (3, 1, 2, 0):
        result = dot_nt(values_ref[p], weight_ref[:, columns])
        if p < 2:
            keep_ref[p * rows : p * rows + rows] = result
        else:
            give_ref[p * rows - 2 * rows : p * rows - rows] = result.astype(jnp.bfloat16)


def first_back_body(_, gate_ref, attn_ref, scan_ref, late_ref, weight_ref, keep_ref, give_ref):
    rows, channels = gate_ref.shape[1], gate_ref.shape[2]
    wide = channels + 128
    for p in (3, 1, 2, 0):
        result = dot_nt(gate_ref[p], late_ref[:, :channels])
        result = result + dot_nt(attn_ref[p, :, :128], late_ref[:, channels:wide])
        result = result + dot_nt(attn_ref[p, :, 128:], weight_ref[:, channels:wide])
        result = result + dot_nt(scan_ref[p, :, :channels], weight_ref[:, :channels])
        result = result + dot_nt(scan_ref[p, :, channels:], weight_ref[:, wide:])
        if p < 2:
            keep_ref[p * rows : p * rows + rows] = result
        else:
            give_ref[p * rows - 2 * rows : p * rows - rows] = result.astype(jnp.bfloat16)


def ffn_body(slots, fresh, _, *refs):
    pieces, cots = refs[0:2], refs[2:4]
    if fresh:
        parts, outs = refs[4:-7], refs[-7:]
        weight_ref = outs[6]
        stack_rows(parts, weight_ref)
    else:
        weight_ref, outs = refs[4], refs[-6:]
    second_ref, cot_ref, hidden_ref, dgu_ref, dkeep, dgive = outs[:6]
    hidden_local = hidden_ref.shape[2]
    rows = second_ref.shape[1]
    gate_up_weight = weight_ref.at[:, : 2 * hidden_local]
    down_weight = weight_ref.at[:, 2 * hidden_local :]
    for p, piece, cots_ref in zip(slots, pieces, cots):
        values, cot = piece[...], cots_ref[rows:]
        second_ref[p] = values
        cot_ref[p] = cot
        gate_up = dot_nn(values, gate_up_weight[...])
        d_hidden = dot_nn(cot, down_weight[...])
        gate, up = gate_up[:, :hidden_local], gate_up[:, hidden_local:]
        sig = jax.nn.sigmoid(gate)
        act = gate * sig
        hidden = (act * up).astype(jnp.bfloat16)
        hidden_ref[p] = hidden
        d_gate = (d_hidden * up * sig * (1.0 + gate * (1.0 - sig))).astype(jnp.bfloat16)
        d_up = (d_hidden * act).astype(jnp.bfloat16)
        dgu_ref[p, :, :hidden_local] = d_gate
        dgu_ref[p, :, hidden_local:] = d_up
        d_second = dot_nt(dgu_ref[p], gate_up_weight[...])
        if p < 2:
            dkeep[...] = d_second
        else:
            dgive[...] = d_second.astype(jnp.bfloat16)


def pick_rows(values, block, rows):
    picked = jnp.zeros((rows, values.shape[1]), values.dtype)
    for g in range(values.shape[0] // rows):
        picked = jnp.where(block == g, values[g * rows : g * rows + rows], picked)
    return picked


def shared_sums_body(at_ref, bc_ref, keyval_ref, *refs):
    *sums, ffn_ref, keep_ref, give_ref = refs
    at = at_ref[0]
    rows = keep_ref.shape[0] // 2
    lanes = lane_ids(bc_ref.shape[0], 128)
    by_row = sum(ref[...] for ref in sums)
    gains = jnp.where(lanes == 0, by_row, jnp.where(lanes == 1, ffn_ref[...], 0.0))
    values = jnp.concatenate([bc_ref[...], keyval_ref[...], gains], axis=1)
    for k in range(2):
        keep_ref[k * rows : k * rows + rows] = pick_rows(values, at ^ (2 * k), rows)
        give_ref[k * rows : k * rows + rows] = pick_rows(values, at ^ (2 * k + 1), rows)


def shared_total_body(at_ref, keep_ref, near_ref, far_ref, gains_ref, bc_ref, keyval_ref, out_ref):
    rows = far_ref.shape[0]
    states = bc_ref.shape[1]
    lanes = lane_ids(rows, 128)
    chip, other = keep_ref[:rows] + near_ref[:rows], far_ref[...]
    total = chip + other
    bc_ref[...] = total[:, :states]
    heads = [side[:, states : states + 128] for side in (chip, other)]
    low, high = [
        [jnp.where(at_ref[0] < 2, heads[k], heads[1 - k]) for k in range(2)][k] for k in range(2)
    ]
    keyval_ref[:, :128] = jnp.where(lanes < HEAD, low, pltpu.roll(high, HEAD, 1))
    keyval_ref[:, 128:] = jnp.where(lanes < HEAD, pltpu.roll(low, HEAD, 1), high)
    rounded = gains_ref[...].astype(jnp.bfloat16).astype(jnp.float32)
    out_ref[...] = total[:, states + 128 :] / rounded


def pack_body(turned, _, *refs):
    out_ref = refs[-1]
    begin_at = 0
    for index, ref in enumerate(refs[:-1]):
        values = ref[...]
        if index in turned:
            values = values.T
        out_ref[:, begin_at : begin_at + values.shape[1]] = values.astype(jnp.bfloat16)
        begin_at = begin_at + values.shape[1]


def shared_body(at_ref, mine_ref, near_ref, far_ref, cross_ref, step_ref, out_ref):
    at = at_ref[0]
    rows = mine_ref.shape[0]
    lanes = lane_ids(rows, 128)
    states = mine_ref.shape[1] - 384
    for j, ref in enumerate((mine_ref, near_ref, far_ref, cross_ref)):
        values = ref[...].astype(jnp.float32)
        here = pl.ds(pl.multiple_of((at ^ j) * rows, rows), rows)
        key, value = values[:, :128], values[:, 128:256]
        low = jnp.where(lanes < HEAD, key, pltpu.roll(value, HEAD, 1))
        high = jnp.where(lanes < HEAD, pltpu.roll(key, HEAD, 1), value)
        out_ref[here, :128] = jnp.where(at < 2, low, high).astype(jnp.bfloat16)
        out_ref[here, 128 : 128 + states] = values[:, 256 : 256 + states].astype(jnp.bfloat16)
        out_ref[here, 128 + states :] = (
            values[:, 256 + states :] + step_ref[here]
        ).astype(jnp.bfloat16)


def call_kernel(body, outs, scratch, *args, deps=(), micros=2, limit=16, aliases=None):
    shapes = [jax.ShapeDtypeStruct(shape, kind) for shape, kind in outs]
    count, extra = len(args), len(deps)
    whole = pl.BlockSpec(memory_space=pltpu.VMEM)

    def wrapped(*refs):
        body(*refs[:count], *refs[count + extra :])

    return pl.pallas_call(
        wrapped,
        out_shape=shapes,
        in_specs=[pl.BlockSpec(memory_space=pltpu.SMEM)]
        + [whole] * (count - 1)
        + [whole] * extra,
        out_specs=[whole] * len(shapes),
        scratch_shapes=[pltpu.VMEM(shape, kind) for shape, kind in scratch],
        input_output_aliases=aliases or {},
        compiler_params=pltpu.CompilerParams(vmem_limit_bytes=limit * 2**20),
        cost_estimate=pl.CostEstimate(
            flops=int(micros * 1e9), bytes_accessed=0, transcendentals=0
        ),
    )(*args, *deps)


def sequence_tables(seg_ids):
    length = seg_ids.shape[0]
    places = jnp.arange(length, dtype=jnp.int32)
    starts = jnp.where((places == 0) | (seg_ids != jnp.roll(seg_ids, 1)), places, 0)
    position = places - lax.cummax(starts, axis=0)
    half_dim = HEAD // 2
    frequency = jnp.exp(-jnp.log(ROPE_BASE) * jnp.arange(half_dim, dtype=jnp.float32) / half_dim)
    angles = position.astype(jnp.float32)[:, None] * frequency[None, :]
    cosine, sine = jnp.cos(angles), jnp.sin(angles)
    cosine = jnp.concatenate([cosine] * 4, axis=1)
    sine = jnp.concatenate([-sine, sine] * 2, axis=1)
    masks = [jnp.ones((length,), jnp.float32)]
    for lag in range(1, CONV):
        masks.append(
            ((places >= lag) & (seg_ids == jnp.roll(seg_ids, lag))).astype(jnp.float32)
        )
    masks = jnp.stack(masks + [jnp.zeros((length,), jnp.float32)] * (8 - CONV), axis=1)
    return cosine, sine, jnp.pad(masks, ((0, 8), (0, 0)))


def tap_rows(kernel, offset):
    taps = jnp.concatenate([kernel.T, offset[None, :]], axis=0)
    return jnp.pad(taps, ((0, 8 - taps.shape[0]), (0, 0)))


def shards(
    tokens,
    segment_ids,
    cotangent,
    norm_gain,
    w_z,
    w_x,
    w_bc,
    w_dt,
    conv_x,
    conv_bias_x,
    conv_bc,
    conv_bias_bc,
    dt_bias,
    a_log,
    d_skip,
    mixer_gain,
    w_mixer_out,
    w_query,
    w_keyval,
    w_attn_out,
    ffn_gain,
    w_gate,
    w_up,
    w_down,
):
    half_type = jnp.bfloat16
    full_type = jnp.float32
    rows, width = tokens.shape
    length = segment_ids.shape[0]
    channels = w_z.shape[1]
    heads = w_dt.shape[1]
    hidden_local = w_gate.shape[1]
    states = 2 * STATE
    blocks = length // rows

    row_count = w_bc.shape[0]
    gain_rows = norm_gain.shape[0]
    conv_rows = conv_bc.shape[0]
    at = lax.axis_index("tp").astype(jnp.int32).reshape(1)
    order = feature_order()
    x_at, core_at = place_bits()
    x_core = jnp.zeros((1,), jnp.int32)

    row_half = ((rows, width), half_type)
    row_full = ((rows, width), full_type)
    both_mine, tok_rows = call_kernel(
        front_body,
        [((2 * rows, width), half_type), ((rows, width), half_type)],
        [],
        order,
        tokens,
        cotangent,
    )

    small = jnp.stack([norm_gain, ffn_gain, conv_bc.reshape(-1), jnp.repeat(conv_bias_bc, CONV)], 1)
    shared_in = jnp.concatenate(
        [w_keyval, w_bc, jnp.pad(small, ((0, 0), (8, 116)))], axis=1
    ).astype(half_type)
    step_wide = jnp.pad(w_dt, ((0, 0), (0, 128 - heads)))
    if staged():
        mine, far, near, cross = gather_pieces(shared_in)
        (shared_shard,) = call_kernel(
            shared_body,
            [((4 * row_count, states + 256), half_type)],
            [],
            at,
            mine,
            near,
            far,
            cross,
            step_wide,
            deps=[both_mine],
            micros=1,
        )
    else:
        shared_all = lax.all_gather(shared_in, "tp", axis=0, tiled=True)
        key_rows, value_rows = (
            jnp.where(x_at == 0, shared_all[:, k : k + HEAD], shared_all[:, k + HEAD : k + 2 * HEAD])
            for k in (0, 128)
        )
        shared_shard = jnp.concatenate(
            [
                key_rows,
                value_rows,
                shared_all[:, 256 : 256 + states],
                shared_all[:, 256 + states :] + step_wide.astype(half_type),
            ],
            axis=1,
        )
    def pack(turned, *shards, deps=()):
        width_all = sum(shard.size for shard in shards) // w_x.shape[0]
        return call_kernel(
            functools.partial(pack_body, turned),
            [((w_x.shape[0], width_all), half_type)],
            [],
            x_core,
            *shards,
            deps=deps,
            micros=1,
        )[0]

    gather = Gather(jnp.concatenate([w_x.astype(half_type), shared_shard], axis=1))
    late_gather = Gather(pack((2, 3), w_z, w_query, w_mixer_out, w_attn_out, deps=[both_mine]))
    both = gather_pieces(both_mine, late=True)
    cosine, sine, keep_masks = sequence_tables(segment_ids)
    seg_col, seg_row = segment_ids[:, None], segment_ids[None, :]
    taps_x = tap_rows(conv_x, conv_bias_x)
    rates = jnp.pad(jnp.stack([dt_bias, a_log], axis=1), ((0, 8 - heads), (0, 126)))
    gains = jnp.stack([mixer_gain, jnp.repeat(d_skip, channels // heads)])
    gains = jnp.pad(gains, ((0, 6), (0, 0)))

    for k in range(4):
        steps = gather.step(*([cosine, sine, keep_masks, taps_x, rates, gains] if k == 2 else []))
        late_steps = late_gather.step()
    ffn_shard = pack((2,), w_gate, w_up, w_down, deps=[*late_steps[:1], *steps[1:]])
    ffn_gather = Gather(ffn_shard)
    ffn_step = ffn_gather.step()

    parts = gather.parts()
    columns = channels + 128 + states + 128
    first_in, proj, weight, small_rows, taps_bc = call_kernel(
        functools.partial(project_body, len(parts)),
        [
            ((blocks, rows, width), half_type),
            ((blocks, rows, columns), full_type),
            ((width, columns), half_type),
            ((8, width), full_type),
            ((8, states), full_type),
        ],
        [],
        order,
        *both,
        *parts,
        micros=6,
    )
    gain_one, gain_two = small_rows[0:1], small_rows[1:2]

    ffn_next = ffn_gather.step(first_in)
    scan_out, x_pre, bc_pre, basis, inputs, time_rows, time_cols = call_kernel(
        functools.partial(ssd_forward_body, heads),
        [
            ((length, channels), full_type),
            ((length, channels), full_type),
            ((length, states), full_type),
            ((length, states), half_type),
            ((length, channels), half_type),
            ((24, length), full_type),
            ((length, 128), full_type),
        ],
        [
            ((length + 8, channels), full_type),
            ((length + 8, states), full_type),
            ((8, length), full_type),
        ],
        at,
        proj,
        seg_col,
        seg_row,
        keep_masks,
        taps_x,
        taps_bc,
        rates,
        deps=ffn_step,
        micros=11,
    )
    parts = late_gather.parts()
    head_half = ((length, 128), half_type)
    head_full = ((length, 128), full_type)
    ffn_step = ffn_gather.step(scan_out)
    cat, gate_in, query, keyk, valv, logs, inverse, late_weight = call_kernel(
        functools.partial(attend_forward_body, len(parts)),
        [
            ((blocks, rows, channels + 128), half_type),
            ((blocks, rows, channels), full_type),
            head_half,
            head_half,
            head_half,
            head_full,
            head_full,
            ((width, 2 * (channels + 128)), half_type),
        ],
        [],
        at,
        first_in,
        proj,
        scan_out,
        x_pre,
        seg_col,
        seg_row,
        cosine,
        sine,
        gains,
        *parts,
        deps=ffn_next,
        micros=9,
    )

    def row_products(values, weight, deps=()):
        return call_kernel(
            product_body,
            [((2 * rows, width), full_type), ((2 * rows, width), half_type)],
            [],
            x_core,
            values,
            weight,
            deps=deps,
        )

    mix_terms = reduce_pieces(*row_products(cat, late_weight, deps=ffn_step))
    ffn_step = ffn_gather.step(cat)
    after_mix, second_mine = call_kernel(
        mixed_body,
        [row_full, row_half],
        [],
        order,
        tok_rows,
        *mix_terms,
        gain_two,
        deps=ffn_step[1:],
    )
    second = gather_pieces(second_mine)

    parts = ffn_gather.parts()
    filled = [
        ((blocks, rows, width), half_type),
        ((blocks, rows, width), half_type),
        ((blocks, rows, hidden_local), half_type),
        ((blocks, rows, 2 * hidden_local), half_type),
    ]
    sums = [row_full, row_half]
    *filled_in, d_keep, d_give, ffn_weight = call_kernel(
        functools.partial(ffn_body, (0, 2), True),
        filled + sums + [((width, 3 * hidden_local), half_type)],
        [],
        x_core,
        second[0],
        second[2],
        both[0],
        both[2],
        *parts,
        micros=5,
    )
    *filled_in, d_keep_x, d_give_x = call_kernel(
        functools.partial(ffn_body, (1, 3), False),
        filled + sums,
        [],
        x_core,
        second[1],
        second[3],
        both[1],
        both[3],
        ffn_weight,
        *filled_in,
        micros=5,
        aliases={6: 0, 7: 1, 8: 2, 9: 3},
    )
    second_in, cot_all, hidden, d_gate_up = (
        array.reshape(length, array.shape[2]) for array in filled_in
    )
    near = flip(d_give, "tp", 1)
    passed = d_keep_x + flip(d_give_x, "tp", 1).astype(full_type)
    d_second = d_keep, near, flip(passed.astype(half_type), "tp", 2)
    ffn_scatter = Scatter(
        [
            contract_rows(second_in, d_gate_up).astype(half_type),
            contract_rows(cot_all, hidden).astype(half_type),
        ],
        near,
    )

    d_after, d_mix = call_kernel(
        after_back_body,
        [row_full, row_half],
        [],
        order,
        after_mix,
        both_mine,
        *d_second,
        gain_two,
    )
    d_mix_all = gather_pieces(d_mix)
    ffn_step = ffn_scatter.step(3, d_second[2])

    d_gate, d_comb, sums_mix, d_mix_whole, d_att = call_kernel(
        gate_backward_body,
        [
            ((blocks, rows, channels), half_type),
            ((length, channels), full_type),
            ((8, channels), full_type),
            ((blocks, rows, width), half_type),
            head_half,
        ],
        [],
        at,
        gate_in,
        *d_mix_all,
        late_weight,
        scan_out,
        x_pre,
        gains,
        inverse,
        deps=ffn_step,
        micros=4,
    )
    ffn_step = ffn_scatter.step(2, *d_mix_all[2:])
    out_terms = reduce_pieces(*row_products(filled_in[2], ffn_weight, deps=d_mix_all[1:]))
    first_rows = first_in.reshape(length, width)
    gate_scatter = Scatter(
        [
            contract_rows(first_rows, d_gate.reshape(length, channels)).astype(half_type),
            contract_rows(
                d_mix_whole.reshape(length, width), cat.reshape(length, channels + 128)
            ).astype(half_type),
        ],
    )
    scan_step = ffn_step
    ffn_step = ffn_scatter.step(1, d_comb)
    d_inputs_t, d_basis_b, d_basis_c, q_rows, mixed_t = call_kernel(
        functools.partial(ssd_backward_body, heads),
        [
            ((channels, length), full_type),
            ((STATE, length), full_type),
            ((length, STATE), full_type),
            ((8, length), full_type),
            ((channels, length), full_type),
        ],
        [
            ((length, channels), half_type),
            ((channels, length), half_type),
            ((STATE, length), half_type),
        ],
        at,
        d_comb,
        scan_out,
        seg_col,
        seg_row,
        x_pre,
        basis,
        inputs,
        time_rows,
        time_cols,
        deps=scan_step,
        micros=12,
    )
    gate_step = gate_scatter.step(3, d_basis_c)
    d_scan, sums_x, sums_bc, sums_rate = call_kernel(
        functools.partial(conv_backward_body, heads),
        [
            ((blocks, rows, channels + states + 128), half_type),
            ((8, channels), full_type),
            ((8, states), full_type),
            ((8, 128), full_type),
        ],
        [
            ((length + 8, channels), full_type),
            ((length + 8, states), full_type),
            ((length + 8, channels), full_type),
            ((length + 8, states), full_type),
            ((channels, length), full_type),
            ((8, length), full_type),
        ],
        at,
        proj,
        d_comb,
        keep_masks,
        taps_x,
        taps_bc,
        rates,
        gains,
        x_pre,
        bc_pre,
        time_rows,
        d_inputs_t,
        d_basis_b,
        d_basis_c,
        q_rows,
        mixed_t,
        deps=ffn_step,
        micros=7,
    )
    sum_gate, sum_up, sum_down, ffn_rows = ffn_scatter.total(
        (
            (0, hidden_local, False),
            (hidden_local, hidden_local, False),
            (2 * hidden_local, hidden_local, True),
        ),
        (0, hidden_local),
        w_gate,
        w_up,
    )
    scan_scatter = Scatter(
        [
            contract_rows(
                first_rows, d_scan.reshape(length, channels + states + 128)
            ).astype(half_type)
        ],
    )
    (d_attn,) = call_kernel(
        attend_backward_body,
        [((blocks, rows, 256), half_type)],
        [((length, 128), full_type), ((length, 128), full_type)],
        at,
        d_att,
        seg_col,
        seg_row,
        cosine,
        sine,
        query,
        keyk,
        valv,
        logs,
        deps=gate_step,
        micros=7,
    )
    gate_step = gate_scatter.step(2, d_scan)
    keep, give = call_kernel(
        first_back_body,
        [((2 * rows, width), full_type), ((2 * rows, width), half_type)],
        [],
        x_core,
        d_gate,
        d_attn,
        d_scan,
        late_weight,
        weight,
        deps=[out_terms[2]],
        micros=4,
    )
    d_first = reduce_pieces(keep, give)
    gate_scatter.step(1, d_first[1])
    scan_scatter.step(3, d_first[1])
    attn_scatter = Scatter(
        [contract_rows(first_rows, d_attn.reshape(length, 256)).astype(half_type)],
        d_first[1],
    )
    (grad_tokens,) = call_kernel(
        token_back_body,
        [row_full],
        [],
        order,
        tok_rows,
        d_after,
        *d_first,
        gain_one,
    )

    scan_scatter.step(2)
    attn_scatter.step(3)
    scan_scatter.step(1)
    attn_scatter.step(2, d_first[2])
    attn_scatter.step(1)
    sum_z, sum_mixer_out, sum_attn_out, gate_rows = gate_scatter.total(
        ((0, channels, False), (channels, channels, True), (2 * channels, 128, True)), (0,), w_z
    )
    sum_x, sum_bc, sum_step, scan_rows = scan_scatter.total(
        ((0, channels, False), (channels, states, False), (channels + states, heads, False)),
        (0, channels, channels + states),
        w_x,
        shared_shard[:, 128 : 128 + states],
        w_dt,
    )
    sum_query, sum_keyval, attn_rows = attn_scatter.total(
        ((0, 128, False), (128, 128, False)), (0, 128), w_query, shared_shard[:, :128]
    )
    keep, give = call_kernel(
        shared_sums_body,
        [((2 * row_count, states + 256), full_type)] * 2,
        [],
        at,
        sum_bc,
        sum_keyval,
        gate_rows,
        scan_rows,
        attn_rows,
        ffn_rows,
        micros=1,
    )
    near = flip(give, "tp", 1)
    far = flip(keep[row_count:] + near[row_count:], "tp", 2)
    grad_bc, grad_keyval, gain_sums = call_kernel(
        shared_total_body,
        [
            ((row_count, states), full_type),
            ((row_count, 256), full_type),
            ((row_count, 128), full_type),
        ],
        [],
        at,
        keep,
        near,
        far,
        jnp.pad(jnp.stack([norm_gain, ffn_gain], 1), ((0, 0), (0, 126)), constant_values=1.0),
        micros=1,
    )
    sum_gain_one, sum_gain_two = gain_sums[:, 0], gain_sums[:, 1]

    (layer_out,) = call_kernel(
        output_body,
        [row_half],
        [],
        order,
        after_mix,
        *out_terms,
    )
    flat = jnp.concatenate([sums_bc, sums_x, sums_mix, sums_rate], axis=1)
    flat = sum_fsdp(after(flat, d_first[1]))
    bc_sums = sum_tp(flat[:, :states])
    device = lax.axis_index("fsdp") * 4 + lax.axis_index("tp")
    sum_conv = lax.dynamic_slice_in_dim(bc_sums[:4].T, device * conv_rows, conv_rows)
    sum_bias = lax.dynamic_slice_in_dim(bc_sums[4], device * conv_rows, conv_rows)
    x_sums = flat[:, states : states + channels]
    mix_sums = flat[:, states + channels : states + 2 * channels]
    rate_sums = flat[:, states + 2 * channels :]
    return (
        layer_out,
        grad_tokens,
        sum_gain_one,
        sum_z,
        sum_x,
        grad_bc,
        sum_step,
        x_sums[:4].T,
        x_sums[4],
        sum_conv,
        sum_bias,
        rate_sums[:heads, 0],
        rate_sums[:heads, 1],
        mix_sums[1].reshape(heads, channels // heads).sum(axis=1),
        mix_sums[0],
        sum_mixer_out,
        sum_query,
        grad_keyval,
        sum_attn_out,
        sum_gain_two,
        sum_gate,
        sum_up,
        sum_down,
    )


def solution(mesh):
    placed = (
        P(("fsdp", "tp"), None),
        P("fsdp"),
        P(("fsdp", "tp"), None),
        P(("fsdp", "tp")),
        P("fsdp", "tp"),
        P("fsdp", "tp"),
        P(("fsdp", "tp"), None),
        P("fsdp", "tp"),
        P("tp", None),
        P("tp"),
        P(("fsdp", "tp"), None),
        P(("fsdp", "tp")),
        P("tp"),
        P("tp"),
        P("tp"),
        P("tp"),
        P("tp", "fsdp"),
        P("fsdp", "tp"),
        P(("fsdp", "tp"), None),
        P("tp", "fsdp"),
        P(("fsdp", "tp")),
        P("fsdp", "tp"),
        P("fsdp", "tp"),
        P("tp", "fsdp"),
    )
    return jax.shard_map(
        shards,
        mesh=mesh,
        in_specs=placed,
        out_specs=(
            P(("fsdp", "tp"), None),
            P(("fsdp", "tp"), None),
            P(("fsdp", "tp")),
            P("fsdp", "tp"),
            P("fsdp", "tp"),
            P(("fsdp", "tp"), None),
            P("fsdp", "tp"),
            P("tp", None),
            P("tp"),
            P(("fsdp", "tp"), None),
            P(("fsdp", "tp")),
            P("tp"),
            P("tp"),
            P("tp"),
            P("tp"),
            P("tp", "fsdp"),
            P("fsdp", "tp"),
            P(("fsdp", "tp"), None),
            P("tp", "fsdp"),
            P(("fsdp", "tp")),
            P("fsdp", "tp"),
            P("fsdp", "tp"),
            P("tp", "fsdp"),
        ),
        check_vma=False,
    )
```

```python
import functools

import jax
import jax.numpy as jnp
from jax import lax
from jax.experimental import pallas as pl
from jax.experimental.pallas import tpu as pltpu
from jax.sharding import PartitionSpec as P

STATE = 128
CONV = 4
HEADS = 8
KV_HEADS = 2
HEAD = 64

EPS = 1e-06
ROPE_BASE = 10000.0
NEG_FILL = -1e30


def contract_rows(left_side, right_side):
    return lax.dot_general(
        left_side, right_side, (((0,), (0,)), ((), ())), preferred_element_type=jnp.float32
    )


def contract_cols(left_side, right_side):
    return lax.dot_general(
        left_side, right_side, (((1,), (1,)), ((), ())), preferred_element_type=jnp.float32
    )


def split_cols(matrix, widths):
    pieces = []
    begin_at = 0
    for part_width in widths:
        pieces.append(matrix[:, begin_at : begin_at + part_width])
        begin_at = begin_at + part_width
    return pieces


def flip(values, axis, mask):
    size = lax.axis_size(axis)
    return lax.ppermute(values, axis, [(i, i ^ mask) for i in range(size)])


def ring(values, step):
    return lax.ppermute(values, "fsdp", [(i, (i + 2 * step) % 8) for i in range(8)])


def staged():
    return lax.axis_size("fsdp") == 8


def place_bits():
    index = lax.axis_index("tp")
    return index // 2, index % 2


def gather_pieces(rows_in, *deps):
    far = flip(rows_in, "tp", 2)
    near = flip(rows_in, "tp", 1)
    cross = flip(after(far, *deps), "tp", 1)
    return rows_in, far, near, cross


def reduce_pieces(keep, give, *deps):
    half = keep.shape[0] // 2
    near = flip(give, "tp", 1)
    passed = after((keep[half:] + near[half:].astype(jnp.float32)).astype(jnp.bfloat16), *deps)
    far = flip(passed, "tp", 2)
    return keep, near, far, passed


def fsdp_place():
    index = lax.axis_index("fsdp")
    return index // 2, index % 2


def after(value, *deps):
    if not deps:
        return value

    def body(_, value_ref, out_ref):
        out_ref[...] = value_ref[...]

    return call_kernel(
        body, [(value.shape, value.dtype)], [], no_scalar(), value, deps=deps, micros=1, limit=8
    )[0]


def no_scalar():
    return jnp.zeros((1,), jnp.int32)


def block_of(grads, rows, dy, dz):
    at = (dy * 4 + dz) * rows
    return [grad[at : at + rows] for grad in grads]


def store_side_by_side(values, out_ref):
    begin_at = 0
    for value in values:
        out_ref[:, begin_at : begin_at + value.shape[1]] = value.astype(out_ref.dtype)
        begin_at = begin_at + value.shape[1]


def add_arrivals(values, arrivals):
    sums, begin_at = [], 0
    for value in values:
        columns = slice(begin_at, begin_at + value.shape[1])
        total = value.astype(jnp.float32)
        for arrival in arrivals:
            total = total + arrival[:, columns].astype(jnp.float32)
        sums.append(total)
        begin_at = begin_at + value.shape[1]
    return sums


def first_block_body(rows, _, *refs):
    store_side_by_side(block_of(refs[:-1], rows, 1, 3), refs[-1])


def step_body(count, rows, dz, _, *refs):
    grads, arrivals, (send_ref, next_ref) = refs[:count], refs[count:-2], refs[-2:]
    sums = add_arrivals(block_of(grads, rows, 0, dz), [ref[...] for ref in arrivals])
    store_side_by_side(sums, send_ref)
    store_side_by_side(block_of(grads, rows, 1, dz - 1), next_ref)


def total_body(count, rows, columns, weighted, _, *refs):
    grads, refs = refs[:count], refs[count:]
    outs = refs[-1 - len(columns) :]
    weights = refs[-1 - len(columns) - len(weighted) : -1 - len(columns)]
    arrivals = [ref[...] for ref in refs[: -1 - len(columns) - len(weighted)]]
    sums = add_arrivals(block_of(grads, rows, 0, 0) if rows else [grads[0][...]], arrivals)
    total = jnp.concatenate(sums, axis=1) if len(sums) > 1 else sums[0]
    by_row = jnp.zeros((total.shape[0], 1), jnp.float32)
    for begin_at, weight in zip(weighted, weights):
        values = total[:, begin_at : begin_at + weight.shape[1]]
        rounded = weight[...].astype(jnp.bfloat16).astype(jnp.float32)
        by_row = by_row + jnp.sum(values * rounded, axis=1, keepdims=True)
    for (begin_at, width, turned), out_ref in zip(columns, outs):
        values = total[:, begin_at : begin_at + width]
        out_ref[...] = values.T if turned else values
    outs[-1][...] = jnp.broadcast_to(by_row, outs[-1].shape)


class Scatter:
    def __init__(self, grads, *deps):
        self.grads = grads
        self.rows = grads[0].shape[0] // 8
        self.width = sum(grad.shape[1] for grad in grads)
        self.arrivals = []
        self.ready = grads[0]
        if staged():
            (first,) = call_kernel(
                functools.partial(first_block_body, self.rows),
                [((self.rows, self.width), jnp.bfloat16)],
                [],
                no_scalar(),
                *grads,
                deps=deps,
                micros=1,
                limit=16,
            )
            self.ready = first
            self.arrivals = [flip(first, "fsdp", 1)]

    def step(self, dz, *deps):
        if not staged():
            return ()
        block = ((self.rows, self.width), jnp.bfloat16)
        send, following = call_kernel(
            functools.partial(step_body, len(self.grads), self.rows, dz),
            [block, block],
            [],
            no_scalar(),
            *self.grads,
            *self.arrivals,
            deps=deps,
            micros=1,
            limit=16,
        )
        self.ready = send
        self.arrivals = [flip(following, "fsdp", 1), ring(send, 1)]
        return self.arrivals

    def total(self, columns, weighted, *weights):
        if staged():
            grads, rows = self.grads, self.rows
        else:
            grads = [
                lax.psum_scatter(
                    jnp.concatenate(self.grads, axis=1), "fsdp", scatter_dimension=0, tiled=True
                )
            ]
            rows = 0
        own = grads[0].shape[0] // 8 if rows else grads[0].shape[0]
        shapes = [
            ((width, own) if turned else (own, width), jnp.float32)
            for _, width, turned in columns
        ]
        return call_kernel(
            functools.partial(total_body, len(grads), rows, columns, weighted),
            shapes + [((own, 128), jnp.float32)],
            [],
            no_scalar(),
            *grads,
            *self.arrivals,
            *weights,
            micros=1,
        )


class SumStages:
    def __init__(self, values, shared):
        self.values, self.shared, self.done = values, shared, 0
        self.stages = [("fsdp", 1), ("fsdp", 2), ("fsdp", 6)] if staged() else []
        if not staged():
            self.values = lax.psum(values, "fsdp")
        self.came = self.exchange()

    def exchange(self):
        if not self.stages:
            return None
        return flip(self.values, *self.stages[0])

    def turn(self, *deps):
        if self.came is None:
            return ()
        self.values = add_arrays(self.values, self.came, *deps)
        self.stages = self.stages[1:]
        self.came = self.exchange()
        return (self.values,)

    def total(self):
        while self.stages:
            self.turn()
        shared = self.values[:, : self.shared]
        for mask in (1, 2):
            shared = add_arrays(shared, flip(shared, "tp", mask))
        return self.values, shared


def add_arrays(left_side, right_side, *deps):
    def body(_, left_ref, right_ref, out_ref):
        out_ref[...] = left_ref[...] + right_ref[...]

    outs = [(left_side.shape, left_side.dtype)]
    return call_kernel(
        body, outs, [], no_scalar(), left_side, right_side, deps=deps, micros=1, limit=8
    )[0]


class Gather:
    def __init__(self, shard):
        self.shard = self.ready = shard
        if staged():
            self.along, self.across = [shard], []
        self.arrivals = []

    def step(self, *deps):
        if not staged():
            return ()
        held = self.ready = after(self.along[-1], *self.across[-1:], *deps)
        if len(self.along) < 4:
            self.along.append(ring(held, 1))
        self.across.append(flip(held, "fsdp", 1))
        self.arrivals = [self.along[-1], self.across[-1]]
        return self.arrivals

    def parts(self):
        if not staged():
            return [lax.all_gather(self.shard, "fsdp", axis=0, tiled=True)]
        return [blocks[-dz % 4] for blocks in (self.along, self.across) for dz in range(4)]


def sum_fsdp(values):
    if not staged():
        return lax.psum(values, "fsdp")
    for mask in (1, 2, 6):
        values = values + flip(values, "fsdp", mask)
    return values


def sum_tp(values):
    for mask in (1, 2):
        values = values + flip(values, "tp", mask)
    return values


def feature_order():
    if not staged():
        return jnp.arange(8, dtype=jnp.int32)
    z_at, y_at = fsdp_place()
    steps = jnp.arange(8, dtype=jnp.int32)
    return (z_at + steps % 4) % 4 * 2 + (y_at ^ (steps // 4))


CHUNK = 128


def row_chunks(rows, body, carry=0):
    def step(k, carry):
        return body(pl.ds(pl.multiple_of(k * CHUNK, CHUNK), CHUNK), carry)

    return lax.fori_loop(0, rows // CHUNK, step, carry)


def front_body(order_ref, tok_ref, cot_ref, both_ref, tok_rel):
    rows_all, width = tok_ref.shape
    block = width // 8

    def chunk(rows, carry):
        below = pl.ds(pl.multiple_of(rows.start + rows_all, CHUNK), CHUNK)
        for b in range(8):
            there = pl.ds(pl.multiple_of(order_ref[b] * block, block), block)
            here = slice(b * block, b * block + block)
            tok_rel[rows, here] = tok_ref[rows, there]
            both_ref[below, here] = cot_ref[rows, there]
        values = tok_rel[rows].astype(jnp.float32)
        normed = values * lax.rsqrt(jnp.mean(values * values, axis=-1, keepdims=True) + EPS)
        both_ref[rows] = normed.astype(jnp.bfloat16)
        return carry

    row_chunks(rows_all, chunk)


def summed_rows(rows, keep_ref, near_ref, far_ref):
    return (
        keep_ref[rows] + near_ref[rows].astype(jnp.float32) + far_ref[rows].astype(jnp.float32)
    )


def mixed_body(_, tok_ref, keep_ref, near_ref, far_ref, gain_ref, after_ref, second_ref):
    def chunk(rows, carry):
        after = tok_ref[rows].astype(jnp.float32) + summed_rows(rows, keep_ref, near_ref, far_ref)
        after_ref[rows] = after
        normed = after * lax.rsqrt(jnp.mean(after * after, axis=-1, keepdims=True) + EPS)
        second_ref[rows] = (normed * gain_ref[...]).astype(jnp.bfloat16)
        return carry

    row_chunks(tok_ref.shape[0], chunk)


def output_body(order_ref, after_ref, keep_ref, near_ref, far_ref, out_ref):
    block = after_ref.shape[1] // 8

    def chunk(rows, carry):
        values = after_ref[rows] + summed_rows(rows, keep_ref, near_ref, far_ref)
        values = values.astype(jnp.bfloat16)
        for b in range(8):
            there = pl.ds(pl.multiple_of(order_ref[b] * block, block), block)
            out_ref[rows, there] = values[:, b * block : b * block + block]
        return carry

    row_chunks(after_ref.shape[0], chunk)


def norm_back(values, d_out, gain):
    inverse = lax.rsqrt(jnp.mean(values * values, axis=-1, keepdims=True) + EPS)
    normed = values * inverse
    scaled = d_out * gain
    return inverse * (scaled - normed * jnp.mean(scaled * normed, axis=-1, keepdims=True))


def after_back_body(
    _, after_ref, cot_ref, keep_ref, near_ref, far_ref, gain_ref, d_after_ref, d_mix_ref
):
    def chunk(rows, carry):
        d_second = summed_rows(rows, keep_ref, near_ref, far_ref)
        lower = pl.ds(pl.multiple_of(rows.start + after_ref.shape[0], CHUNK), CHUNK)
        d_after = cot_ref[lower].astype(jnp.float32) + norm_back(
            after_ref[rows], d_second, gain_ref[...]
        )
        d_after_ref[rows] = d_after
        d_mix_ref[rows] = d_after.astype(jnp.bfloat16)
        return carry

    row_chunks(after_ref.shape[0], chunk)


def token_back_body(
    order_ref, tok_ref, d_after_ref, keep_ref, near_ref, far_ref, gain_ref, out_ref
):
    block = tok_ref.shape[1] // 8

    def chunk(rows, carry):
        d_first = summed_rows(rows, keep_ref, near_ref, far_ref)
        values = d_after_ref[rows] + norm_back(
            tok_ref[rows].astype(jnp.float32), d_first, gain_ref[...]
        )
        for b in range(8):
            there = pl.ds(pl.multiple_of(order_ref[b] * block, block), block)
            out_ref[rows, there] = values[:, b * block : b * block + block]
        return carry

    row_chunks(tok_ref.shape[0], chunk)


def piece_at(block, at):
    apart = block ^ at
    return (apart & 1) * 2 + (apart >> 1)


def head_lanes(columns, first, lanes):
    rows = columns.shape[0]
    even = jnp.broadcast_to(columns[:, first : first + 1], (rows, 128))
    odd = jnp.broadcast_to(columns[:, first + 1 : first + 2], (rows, 128))
    return jnp.where(lanes < HEAD, even, odd)


def lane_ids(rows, cols):
    return lax.broadcasted_iota(jnp.int32, (rows, cols), 1)


def row_ids(rows, cols):
    return lax.broadcasted_iota(jnp.int32, (rows, cols), 0)


def dot_nt(left_side, right_side, **kw):
    return lax.dot_general(
        left_side, right_side, (((1,), (1,)), ((), ())), preferred_element_type=jnp.float32, **kw
    )


def dot_nn(left_side, right_side):
    return jnp.dot(left_side, right_side, preferred_element_type=jnp.float32)


def dot_tn(left_side, right_side):
    return lax.dot_general(
        left_side, right_side, (((0,), (0,)), ((), ())), preferred_element_type=jnp.float32
    )


def conv_window(window, taps, offset, keep):
    rows = window.shape[0] - 8
    summed = window[8:] * taps[CONV - 1 : CONV] + offset
    for lag in range(1, CONV):
        summed = summed + window[8 - lag : 8 - lag + rows] * keep[:, lag : lag + 1] * (
            taps[CONV - 1 - lag : CONV - lag]
        )
    return summed


def log_one_plus(values):
    ratio = values / (2.0 + values)
    square = ratio * ratio
    series = jnp.full_like(values, 1.0 / 15.0)
    for odd in (13, 11, 9, 7, 5, 3, 1):
        series = series * square + 1.0 / odd
    return 2.0 * ratio * series


def scan_lanes(values, reverse):
    length = values.shape[1]
    lanes = lane_ids(*values.shape)
    step = 1
    while step < length:
        if reverse:
            moved = jnp.where(lanes < length - step, pltpu.roll(values, length - step, 1), 0.0)
        else:
            moved = jnp.where(lanes >= step, pltpu.roll(values, step, 1), 0.0)
        values = values + moved
        step = step * 2
    return values


def pair_mask(seg_col, seg_row, at_t, at_s):
    size = seg_col.shape[0]
    rows = row_ids(size, size) + at_t * size
    cols = lane_ids(size, size) + at_s * size
    return (seg_col == seg_row) & (rows >= cols)


def swap_halves(values, lanes):
    half = HEAD // 2
    return jnp.where(
        lanes % HEAD < half, pltpu.roll(values, 128 - half, 1), pltpu.roll(values, half, 1)
    )


def ssd_forward_body(
    heads,
    at_ref,
    proj_ref,
    segc_ref,
    segr_ref,
    keep_ref,
    taps_ref,
    tapb_ref,
    rate_ref,
    scan_ref,
    mixed_ref,
    raw_ref,
    pre_ref,
    basis_ref,
    inputs_ref,
    rows_ref,
    cols_ref,
    xpad,
    bpad,
    dtr,
):
    blocks, size = proj_ref.shape[0], proj_ref.shape[1]
    channels = mixed_ref.shape[1]
    states = basis_ref.shape[1]
    tail = proj_ref.shape[2] - states - 128
    at = at_ref[0]
    xpad[0:8] = jnp.zeros((8, channels), jnp.float32)
    bpad[0:8] = jnp.zeros((8, states), jnp.float32)

    def load(a, carry):
        rows = pl.ds(pl.multiple_of(a * size + 8, 8), size)
        block = piece_at(a, at)
        xpad[rows] = proj_ref[block, :, :channels]
        bpad[rows] = proj_ref[block, :, tail : tail + states]
        here = pl.ds(pl.multiple_of(a * size, size), size)
        raw_ref[here, :channels] = proj_ref[block, :, :channels].astype(jnp.bfloat16)
        raw_ref[here, channels:] = proj_ref[block, :, tail : tail + states].astype(jnp.bfloat16)
        steps = proj_ref[block, :, tail + states :]
        dtr[:, pl.ds(pl.multiple_of(a * size, size), size)] = steps.T[0:8]
        return carry

    lax.fori_loop(0, blocks, load, 0)
    raw = dtr[...] + rate_ref[:, 0:1]
    step_size = jnp.maximum(raw, 0.0) + log_one_plus(jnp.exp(-jnp.abs(raw)))
    log_rate = -step_size * jnp.exp(rate_ref[:, 1:2])
    cum = scan_lanes(log_rate, False)
    length = raw.shape[1]
    rows_ref[0:8] = step_size
    rows_ref[8:16] = cum
    rows_ref[16:24] = raw
    cols_ref[...] = jnp.concatenate(
        [step_size, cum, jnp.zeros((112, length), jnp.float32)], axis=0
    ).T
    lanes = lane_ids(size, 128)

    def prepare_block(a, carry):
        window = pl.ds(pl.multiple_of(a * size, size), size + 8)
        rows = pl.ds(pl.multiple_of(a * size, size), size)
        keep = keep_ref[rows]
        columns = cols_ref[rows]
        bpre = conv_window(bpad[window], tapb_ref[0:4], tapb_ref[4:5], keep)
        pre_ref[rows, channels:] = bpre.astype(jnp.bfloat16)
        basis_ref[rows] = (bpre * jax.nn.sigmoid(bpre)).astype(jnp.bfloat16)
        for pair in range(channels // 128):
            span = slice(pair * 128, pair * 128 + 128)
            xpre = conv_window(xpad[window, span], taps_ref[0:4, span], taps_ref[4:5, span], keep)
            pre_ref[rows, span] = xpre.astype(jnp.bfloat16)
            mixed = (xpre * jax.nn.sigmoid(xpre)).astype(jnp.bfloat16)
            mixed_ref[rows, span] = mixed
            steps = head_lanes(columns, 2 * pair, lanes)
            inputs_ref[rows, span] = (steps * mixed.astype(jnp.float32)).astype(jnp.bfloat16)
        return carry

    lax.fori_loop(0, blocks, prepare_block, 0)
    state = states // 2

    def row_block(i, carry):
        rows_t = pl.ds(pl.multiple_of(i * size, size), size)
        basis_c = basis_ref[rows_t, state:]
        seg_t = segc_ref[rows_t]
        columns = cols_ref[rows_t]

        def pair_block(j, totals):
            rows_s = pl.ds(pl.multiple_of(j * size, size), size)
            allowed = pair_mask(seg_t, segr_ref[:, rows_s], i, j)
            gram = jnp.where(allowed, dot_nt(basis_c, basis_ref[rows_s, :state]), 0.0)
            cum_s = rows_ref[8:16, rows_s]
            fresh = []
            for pair in range(heads // 2):
                values = inputs_ref[rows_s, pair * 128 : pair * 128 + 128]
                outs = []
                for h in (2 * pair, 2 * pair + 1):
                    spread = columns[:, 8 + h : 9 + h] - cum_s[h : h + 1]
                    weights = (gram * jnp.exp(jnp.minimum(spread, 0.0))).astype(jnp.bfloat16)
                    outs.append(dot_nn(weights, values))
                fresh.append(totals[pair] + jnp.where(lanes < HEAD, outs[0], outs[1]))
            return tuple(fresh)

        zero = jnp.zeros((size, 128), jnp.float32)
        totals = lax.fori_loop(0, i + 1, pair_block, (zero,) * (heads // 2))
        for pair in range(heads // 2):
            scan_ref[rows_t, pair * 128 : pair * 128 + 128] = totals[pair]
        return carry

    lax.fori_loop(0, blocks, row_block, 0)


def attend_forward_body(
    count,
    at_ref,
    first_ref,
    proj_ref,
    scan_ref,
    mixed_ref,
    segc_ref,
    segr_ref,
    cos_ref,
    sin_ref,
    gain_ref,
    *refs,
):
    parts = refs[:count]
    cat_ref, gate_ref, combined_ref, query_ref, keyk_ref, valv_ref, logs_ref = refs[count:-2]
    weight_ref, out_weight_ref = refs[-2:]
    wide = weight_ref.shape[1]
    stack_rows([part.at[:, :wide] for part in parts], weight_ref)
    stack_rows([part.at[:, wide:] for part in parts], out_weight_ref)
    blocks, size = proj_ref.shape[0], proj_ref.shape[1]
    channels = scan_ref.shape[1]
    at = at_ref[0]
    lanes = lane_ids(size, 128)
    half_type = jnp.bfloat16

    def finish_block(a, carry):
        rows = pl.ds(pl.multiple_of(a * size, size), size)
        block = piece_at(a, at)
        mine = dot_nn(first_ref[block], weight_ref[...])
        gate, query = mine[:, :channels], mine[:, channels:]
        gate_ref[block] = gate.astype(half_type)
        combined = scan_ref[rows] + gain_ref[1:2] * mixed_ref[rows].astype(jnp.float32)
        combined_ref[rows] = combined.astype(half_type)
        gated = combined * (gate * jax.nn.sigmoid(gate))
        inverse = lax.rsqrt(jnp.mean(gated * gated, axis=-1, keepdims=True) + EPS)
        cat_ref[block, :, :channels] = (gated * inverse * gain_ref[0:1]).astype(half_type)
        cosine, sine = cos_ref[rows], sin_ref[rows]
        query_ref[rows] = (query * cosine + swap_halves(query, lanes) * sine).astype(half_type)
        keyval = proj_ref[block, :, channels : channels + 128]
        keyval = keyval * jnp.where(lanes < HEAD, cosine, 1.0) + swap_halves(
            keyval, lanes
        ) * jnp.where(lanes < HEAD, sine, 0.0)
        moved = pltpu.roll(keyval, HEAD, 1)
        keyk_ref[rows] = jnp.where(lanes < HEAD, keyval, moved).astype(half_type)
        valv_ref[rows] = jnp.where(lanes < HEAD, moved, keyval).astype(half_type)
        return carry

    lax.fori_loop(0, blocks, finish_block, 0)
    for i in range(blocks):
        width = (i + 1) * size
        rows = slice(i * size, width)
        query = query_ref[rows]
        places = row_ids(size, width) + i * size
        allowed = (segc_ref[rows] == segr_ref[:, :width]) & (places >= lane_ids(size, width))
        outs, logs = [], []
        for h in range(2):
            mine = (lanes < HEAD) if h == 0 else (lanes >= HEAD)
            masked = jnp.where(mine, query, jnp.zeros_like(query))
            scores = dot_nt(masked, keyk_ref[:width]) * HEAD ** (-0.5)
            scores = jnp.where(allowed, scores, NEG_FILL)
            top = jnp.max(scores, axis=-1, keepdims=True)
            powers = jnp.exp(scores - top)
            total = jnp.sum(powers, axis=-1, keepdims=True)
            outs.append(dot_nn(powers.astype(half_type), valv_ref[:width]) / total)
            logs.append(top + jnp.log(total))
        cat_ref[piece_at(i, at), :, channels:] = jnp.where(lanes < HEAD, outs[0], outs[1]).astype(half_type)
        logs_ref[rows] = jnp.where(lanes < HEAD, logs[0], logs[1])


def gate_backward_body(
    at_ref,
    gate_ref,
    mine_ref,
    far_ref,
    near_ref,
    cross_ref,
    weight_ref,
    combined_ref,
    gain_ref,
    dgate_ref,
    dcomb_ref,
    small_ref,
    dmix_ref,
    datt_ref,
):
    blocks, size = gate_ref.shape[0], gate_ref.shape[1]
    channels = combined_ref.shape[1]
    at = at_ref[0]
    half_type = jnp.bfloat16
    for p, piece in enumerate((mine_ref, far_ref, near_ref, cross_ref)):
        dmix_ref[p] = piece[...]

    def finish_block(a, carry):
        grad_gain = carry
        rows = pl.ds(pl.multiple_of(a * size, size), size)
        block = piece_at(a, at)
        d_cat = dot_nn(dmix_ref[block], weight_ref[...])
        datt_ref[rows] = d_cat[:, channels:].astype(half_type)
        gate = gate_ref[block].astype(jnp.float32)
        sig = jax.nn.sigmoid(gate)
        act = gate * sig
        combined = combined_ref[rows].astype(jnp.float32)
        gated = combined * act
        inverse = lax.rsqrt(jnp.mean(gated * gated, axis=-1, keepdims=True) + EPS)
        normed = gated * inverse
        d_out = d_cat[:, :channels]
        grad_gain = grad_gain + jnp.sum(d_out * normed, axis=0, keepdims=True)
        scaled = d_out * gain_ref[0:1]
        d_gated = inverse * (scaled - normed * jnp.mean(scaled * normed, axis=-1, keepdims=True))
        d_comb = d_gated * act
        dcomb_ref[rows] = d_comb
        d_gate = d_gated * combined * sig * (1.0 + gate * (1.0 - sig))
        dgate_ref[block] = d_gate.astype(half_type)
        return grad_gain

    grad_gain = lax.fori_loop(0, blocks, finish_block, jnp.zeros((1, channels), jnp.float32))
    small_ref[...] = jnp.broadcast_to(grad_gain, small_ref.shape)


def attend_backward_body(
    at_ref,
    datt_ref,
    segc_ref,
    segr_ref,
    cos_ref,
    sin_ref,
    query_ref,
    keyk_ref,
    valv_ref,
    logs_ref,
    dproj_ref,
    dkey,
    dval,
):
    blocks, size = dproj_ref.shape[0], dproj_ref.shape[1]
    at = at_ref[0]
    lanes = lane_ids(size, 128)
    half_type = jnp.bfloat16
    dkey[...] = jnp.zeros_like(dkey)
    dval[...] = jnp.zeros_like(dval)
    for i in range(blocks):
        width = (i + 1) * size
        rows = slice(i * size, width)
        query = query_ref[rows]
        d_att = datt_ref[rows]
        logs = logs_ref[rows]
        places = row_ids(size, width) + i * size
        allowed = (segc_ref[rows] == segr_ref[:, :width]) & (places >= lane_ids(size, width))
        outs = []
        for h in range(2):
            mine = (lanes < HEAD) if h == 0 else (lanes >= HEAD)
            masked = jnp.where(mine, query, jnp.zeros_like(query))
            d_masked = jnp.where(mine, d_att, jnp.zeros_like(d_att))
            scores = dot_nt(masked, keyk_ref[:width]) * HEAD ** (-0.5)
            scores = jnp.where(allowed, scores, NEG_FILL)
            probs = jnp.exp(scores - logs[:, h * HEAD : h * HEAD + 1])
            d_probs = dot_nt(d_masked, valv_ref[:width])
            mean = jnp.sum(probs * d_probs, axis=-1, keepdims=True)
            d_scores = (probs * (d_probs - mean)).astype(half_type)
            outs.append(dot_nn(d_scores, keyk_ref[:width]))
            dkey[:width] += dot_tn(d_scores, masked)
            dval[:width] += dot_tn(probs.astype(half_type), d_masked)
        d_query = jnp.where(lanes < HEAD, outs[0], outs[1]) * HEAD ** (-0.5)
        cosine, sine = cos_ref[rows], sin_ref[rows]
        d_query = d_query * cosine - swap_halves(d_query, lanes) * sine
        dproj_ref[piece_at(i, at), :, :128] = d_query.astype(half_type)

    def key_block(a, carry):
        rows = pl.ds(pl.multiple_of(a * size, size), size)
        d_key, d_val = dkey[rows], dval[rows]
        d_key = (d_key + pltpu.roll(d_key, HEAD, 1)) * HEAD ** (-0.5)
        d_val = d_val + pltpu.roll(d_val, HEAD, 1)
        d_key = d_key * cos_ref[rows] - swap_halves(d_key, lanes) * sin_ref[rows]
        dproj_ref[piece_at(a, at), :, 128:] = jnp.where(lanes < HEAD, d_key, d_val).astype(
            half_type
        )
        return carry

    lax.fori_loop(0, blocks, key_block, 0)


def silu_slope(values):
    sig = jax.nn.sigmoid(values)
    return sig * (1.0 + values * (1.0 - sig))


def conv_back(d_window, keep_window, taps):
    rows = d_window.shape[0] - 8
    summed = d_window[:rows] * taps[CONV - 1 : CONV]
    for lag in range(1, CONV):
        moved = d_window * keep_window[:, lag : lag + 1]
        summed = summed + moved[lag : lag + rows] * taps[CONV - 1 - lag : CONV - lag]
    return summed


def conv_grads(d_pre, window, keep):
    rows = d_pre.shape[0]
    sums = []
    for tap in range(CONV):
        lag = CONV - 1 - tap
        moved = window[8 - lag : 8 - lag + rows]
        if lag:
            moved = moved * keep[:, lag : lag + 1]
        sums.append(jnp.sum(d_pre * moved, axis=0, keepdims=True))
    sums.append(jnp.sum(d_pre, axis=0, keepdims=True))
    sums.append(jnp.zeros((8 - len(sums), d_pre.shape[1]), jnp.float32))
    return jnp.concatenate(sums, axis=0)


def ssd_backward_body(
    heads,
    at_ref,
    dcomb_ref,
    scan_ref,
    segc_ref,
    segr_ref,
    mixed_ref,
    basis_ref,
    inputs_ref,
    rows_ref,
    cols_ref,
    dint,
    dbt,
    dcb,
    qrow,
    mixt,
    skip_ref,
    dsc,
    dst,
    cbt,
):
    length, channels = scan_ref.shape
    state = dbt.shape[0]
    size = length // 4
    blocks = 4
    half_type = jnp.bfloat16
    lanes = lane_ids(size, 128)
    dint[...] = jnp.zeros_like(dint)
    dbt[...] = jnp.zeros_like(dbt)
    head_of = jnp.where(
        lane_ids(8, channels) // HEAD == row_ids(8, channels), 1.0, 0.0
    ).astype(jnp.float32)

    def load(a, carry):
        rows = pl.ds(pl.multiple_of(a * size, size), size)
        d_comb = dcomb_ref[rows]
        d_scan = d_comb.astype(half_type)
        dsc[rows] = d_scan
        d_full = d_scan.astype(jnp.float32)
        dst[:, rows] = d_full.T.astype(half_type)
        cbt[:, rows] = basis_ref[rows, state:].astype(jnp.float32).T.astype(half_type)
        mixed = mixed_ref[rows].astype(jnp.float32)
        mixt[:, rows] = mixed.T
        qrow[:, rows] = dot_nt(head_of, d_full * scan_ref[rows], precision=lax.Precision.HIGHEST)
        return carry + jnp.sum(d_comb * mixed, axis=0, keepdims=True)

    skips = lax.fori_loop(0, blocks, load, jnp.zeros((1, channels), jnp.float32))
    skip_ref[...] = jnp.broadcast_to(skips, skip_ref.shape)

    def row_block(i, carry):
        rows_t = pl.ds(pl.multiple_of(i * size, size), size)
        basis_c = basis_ref[rows_t, state:]
        seg_t = segc_ref[rows_t]
        columns = cols_ref[rows_t]

        def pair_block(j, total):
            rows_s = pl.ds(pl.multiple_of(j * size, size), size)
            allowed = pair_mask(seg_t, segr_ref[:, rows_s], i, j)
            gram = jnp.where(allowed, dot_nt(basis_c, basis_ref[rows_s, :state]), 0.0)
            cum_s = rows_ref[8:16, rows_s]
            d_gram = jnp.zeros((size, size), jnp.float32)
            for pair in range(heads // 2):
                span = slice(pair * 128, pair * 128 + 128)
                values = inputs_ref[rows_s, span]
                d_scan = dsc[rows_t, span]
                for h in (2 * pair, 2 * pair + 1):
                    mine = (lanes < HEAD) if h % 2 == 0 else (lanes >= HEAD)
                    spread = columns[:, 8 + h : 9 + h] - cum_s[h : h + 1]
                    decay = jnp.exp(jnp.minimum(spread, 0.0))
                    weights = (gram * decay).astype(half_type)
                    d_weights = dot_nt(jnp.where(mine, d_scan, jnp.zeros_like(d_scan)), values)
                    d_gram = d_gram + d_weights * decay
                    chans = slice(h * HEAD, h * HEAD + HEAD)
                    dint[chans, rows_s] += dot_nn(dst[chans, rows_t], weights)
            d_gram = jnp.where(allowed, d_gram, 0.0).astype(half_type)
            dbt[:, rows_s] += dot_nn(cbt[:, rows_t], d_gram)
            return total + dot_nn(d_gram, basis_ref[rows_s, :state])

        dcb[rows_t] = lax.fori_loop(0, i + 1, pair_block, jnp.zeros((size, state), jnp.float32))
        return carry

    lax.fori_loop(0, blocks, row_block, 0)


def conv_backward_body(
    heads,
    at_ref,
    raw_ref,
    dcomb_ref,
    keep_ref,
    taps_ref,
    tapb_ref,
    rate_ref,
    gain_ref,
    pre_ref,
    rows_ref,
    dint_ref,
    dbt,
    dcb,
    qrow_ref,
    mixt,
    dproj_ref,
    gradx_ref,
    gradb_ref,
    grads_ref,
    xpad,
    bpad,
    dpx,
    dpb,
    dint,
    qrow,
):
    blocks, size = dproj_ref.shape[0], dproj_ref.shape[1]
    channels = dcomb_ref.shape[1]
    states = pre_ref.shape[1] - channels
    length = blocks * size
    at = at_ref[0]
    half_type = jnp.bfloat16
    xpad[0:8] = jnp.zeros((8, channels), jnp.float32)
    bpad[0:8] = jnp.zeros((8, states), jnp.float32)
    dpx[length : length + 8] = jnp.zeros((8, channels), jnp.float32)
    dpb[length : length + 8] = jnp.zeros((8, states), jnp.float32)

    def load(a, carry):
        padded = pl.ds(pl.multiple_of(a * size + 8, 8), size)
        rows = pl.ds(pl.multiple_of(a * size, size), size)
        xpad[padded] = raw_ref[rows, :channels].astype(jnp.float32)
        bpad[padded] = raw_ref[rows, channels:].astype(jnp.float32)
        return carry

    lax.fori_loop(0, blocks, load, 0)
    step_size = rows_ref[0:8]
    raw = rows_ref[16:24]
    d_step, col_part = [], []
    for h in range(heads):
        chans = slice(h * HEAD, h * HEAD + HEAD)
        d_inputs = dint_ref[chans]
        mixed = mixt[chans]
        scaled = step_size[h : h + 1] * mixed
        d_step.append(jnp.sum(d_inputs * mixed, axis=0, keepdims=True))
        inputs = scaled.astype(half_type).astype(jnp.float32)
        col_part.append(jnp.sum(d_inputs * inputs, axis=0, keepdims=True))
        dint[chans] = d_inputs * step_size[h : h + 1]
    blank = jnp.zeros((8 - heads, length), jnp.float32)
    d_step = jnp.concatenate(d_step + [blank], axis=0)
    d_cum = qrow_ref[...] - jnp.concatenate(col_part + [blank], axis=0)
    d_log = scan_lanes(d_cum, True)
    rate = jnp.exp(rate_ref[:, 1:2])
    grad_rate = jnp.sum(d_log * (-step_size * rate), axis=1, keepdims=True)
    d_raw = (d_step - d_log * rate) * jax.nn.sigmoid(raw)
    d_raw = jnp.where(row_ids(8, length) < heads, d_raw, 0.0)
    grad_bias = jnp.sum(d_raw, axis=1, keepdims=True)
    lanes8 = lane_ids(8, 128)
    grads_ref[...] = jnp.where(lanes8 == 0, grad_bias, jnp.where(lanes8 == 1, grad_rate, 0.0))
    qrow[...] = d_raw

    def grad_block(a, carry):
        rows = pl.ds(pl.multiple_of(a * size, size), size)
        d_mixed = dint[:, rows].T + dcomb_ref[rows] * gain_ref[1:2]
        dpx[rows] = d_mixed * silu_slope(pre_ref[rows, :channels].astype(jnp.float32))
        d_basis = jnp.concatenate([dbt[:, rows].T, dcb[rows]], axis=1)
        dpb[rows] = d_basis * silu_slope(pre_ref[rows, channels:].astype(jnp.float32))
        return carry

    lax.fori_loop(0, blocks, grad_block, 0)

    def conv_block(a, carry):
        grad_x, grad_b = carry
        rows = pl.ds(pl.multiple_of(a * size, size), size)
        window = pl.ds(pl.multiple_of(a * size, size), size + 8)
        block = piece_at(a, at)
        keep_window = keep_ref[window]
        keep = keep_window[:size]
        d_wide = dpx[window]
        dproj_ref[block, :, :channels] = conv_back(d_wide, keep_window, taps_ref[...]).astype(
            half_type
        )
        grad_x = grad_x + conv_grads(d_wide[:size], xpad[window], keep)
        d_wide = dpb[window]
        dproj_ref[block, :, channels : channels + states] = conv_back(
            d_wide, keep_window, tapb_ref[...]
        ).astype(half_type)
        grad_b = grad_b + conv_grads(d_wide[:size], bpad[window], keep)
        d_steps = jnp.concatenate([qrow[:, rows], jnp.zeros((120, size), jnp.float32)], axis=0)
        dproj_ref[block, :, channels + states :] = d_steps.T.astype(half_type)
        return grad_x, grad_b

    grad_x, grad_b = lax.fori_loop(
        0,
        blocks,
        conv_block,
        (jnp.zeros((8, channels), jnp.float32), jnp.zeros((8, states), jnp.float32)),
    )
    gradx_ref[...] = grad_x
    gradb_ref[...] = grad_b


def stack_rows(pieces, out_ref):
    begin_at = 0
    for piece in pieces:
        out_ref[begin_at : begin_at + piece.shape[0]] = piece[...]
        begin_at = begin_at + piece.shape[0]


def project_body(count, order_ref, *refs):
    pieces, parts = refs[:4], refs[4 : 4 + count]
    first_ref, proj_ref, weight_ref, small_ref, taps_ref = refs[4 + count :]
    width = weight_ref.shape[0]
    rows = proj_ref.shape[1]
    states = taps_ref.shape[1]
    stack_rows(parts, weight_ref)
    small = weight_ref[:, weight_ref.shape[1] - 128 :].astype(jnp.float32).T[8:16]
    small_ref[...] = small
    gain = small[0:1]
    for p, piece in enumerate(pieces):
        first = (piece[:rows].astype(jnp.float32) * gain).astype(jnp.bfloat16)
        first_ref[p] = first
        proj_ref[p] = dot_nn(first, weight_ref[...])
    feature = row_ids(width, states)
    block = width // 8
    place = feature % block
    for b in range(8):
        place = place + jnp.where(feature // block == b, order_ref[b] * block, 0)
    channel = lane_ids(width, states)
    taps = []
    for k in range(CONV + 1):
        picked = jnp.where(place == channel * CONV + k % CONV, 1.0, 0.0).astype(jnp.bfloat16)
        found = dot_nn(small.astype(jnp.bfloat16), picked)
        taps.append(found[2:3] if k < CONV else found[3:4])
    taps.append(jnp.zeros((8 - len(taps), states), jnp.float32))
    taps_ref[...] = jnp.concatenate(taps, axis=0)


def product_body(_, values_ref, weight_ref, keep_ref, give_ref):
    rows = values_ref.shape[1]
    columns = slice(weight_ref.shape[1] - values_ref.shape[2], None)
    for p in (3, 1, 2, 0):
        result = dot_nt(values_ref[p], weight_ref[:, columns])
        if p < 2:
            keep_ref[p * rows : p * rows + rows] = result
        else:
            give_ref[p * rows - 2 * rows : p * rows - rows] = result.astype(jnp.bfloat16)


def first_back_body(
    pieces, _, gate_ref, attn_ref, scan_ref, late_ref, weight_ref, out_ref
):
    rows, channels = gate_ref.shape[1], gate_ref.shape[2]
    wide = channels + 128
    for k, p in enumerate(pieces):
        result = dot_nt(gate_ref[p], late_ref[:, :channels])
        result = result + dot_nt(attn_ref[p, :, :128], late_ref[:, channels:wide])
        result = result + dot_nt(attn_ref[p, :, 128:], weight_ref[:, channels:wide])
        result = result + dot_nt(scan_ref[p, :, :channels], weight_ref[:, :channels])
        result = result + dot_nt(scan_ref[p, :, channels:], weight_ref[:, wide:])
        out_ref[k * rows : k * rows + rows] = result.astype(out_ref.dtype)


def ffn_body(slots, fresh, _, *refs):
    pieces, cots = refs[0:2], refs[2:4]
    if fresh:
        parts, outs = refs[4:-7], refs[-7:]
        weight_ref = outs[6]
        stack_rows(parts, weight_ref)
    else:
        weight_ref, outs = refs[4], refs[-6:]
    second_ref, cot_ref, hidden_ref, dgu_ref, dkeep, dgive = outs[:6]
    hidden_local = hidden_ref.shape[2]
    rows = second_ref.shape[1]
    gate_up_weight = weight_ref.at[:, : 2 * hidden_local]
    down_weight = weight_ref.at[:, 2 * hidden_local :]
    for p, piece, cots_ref in zip(slots, pieces, cots):
        values, cot = piece[...], cots_ref[rows:]
        second_ref[p] = values
        cot_ref[p] = cot
        gate_up = dot_nn(values, gate_up_weight[...])
        d_hidden = dot_nn(cot, down_weight[...])
        gate, up = gate_up[:, :hidden_local], gate_up[:, hidden_local:]
        sig = jax.nn.sigmoid(gate)
        act = gate * sig
        hidden = (act * up).astype(jnp.bfloat16)
        hidden_ref[p] = hidden
        d_gate = (d_hidden * up * sig * (1.0 + gate * (1.0 - sig))).astype(jnp.bfloat16)
        d_up = (d_hidden * act).astype(jnp.bfloat16)
        dgu_ref[p, :, :hidden_local] = d_gate
        dgu_ref[p, :, hidden_local:] = d_up
        d_second = dot_nt(dgu_ref[p], gate_up_weight[...])
        if p < 2:
            dkeep[...] = d_second
        else:
            dgive[...] = d_second.astype(jnp.bfloat16)


def pick_rows(values, block, rows):
    picked = jnp.zeros((rows, values.shape[1]), values.dtype)
    for g in range(values.shape[0] // rows):
        picked = jnp.where(block == g, values[g * rows : g * rows + rows], picked)
    return picked


def shared_sums_body(at_ref, bc_ref, keyval_ref, *refs):
    *sums, ffn_ref, keep_ref, give_ref = refs
    at = at_ref[0]
    rows = keep_ref.shape[0] // 2
    lanes = lane_ids(bc_ref.shape[0], 128)
    by_row = sum(ref[...] for ref in sums)
    gains = jnp.where(lanes == 0, by_row, jnp.where(lanes == 1, ffn_ref[...], 0.0))
    values = jnp.concatenate([bc_ref[...], keyval_ref[...], gains], axis=1)
    for k in range(2):
        keep_ref[k * rows : k * rows + rows] = pick_rows(values, at ^ (2 * k), rows)
        give_ref[k * rows : k * rows + rows] = pick_rows(values, at ^ (2 * k + 1), rows)


def shared_total_body(at_ref, keep_ref, near_ref, far_ref, gains_ref, bc_ref, keyval_ref, out_ref):
    rows = far_ref.shape[0]
    states = bc_ref.shape[1]
    lanes = lane_ids(rows, 128)
    chip, other = keep_ref[:rows] + near_ref[:rows], far_ref[...]
    total = chip + other
    bc_ref[...] = total[:, :states]
    heads = [side[:, states : states + 128] for side in (chip, other)]
    low, high = [
        [jnp.where(at_ref[0] < 2, heads[k], heads[1 - k]) for k in range(2)][k] for k in range(2)
    ]
    keyval_ref[:, :128] = jnp.where(lanes < HEAD, low, pltpu.roll(high, HEAD, 1))
    keyval_ref[:, 128:] = jnp.where(lanes < HEAD, pltpu.roll(low, HEAD, 1), high)
    rounded = gains_ref[...].astype(jnp.bfloat16).astype(jnp.float32)
    out_ref[...] = total[:, states + 128 :] / rounded


def pack_body(turned, _, *refs):
    out_ref = refs[-1]
    begin_at = 0
    for index, ref in enumerate(refs[:-1]):
        values = ref[...]
        if index in turned:
            values = values.T
        out_ref[:, begin_at : begin_at + values.shape[1]] = values.astype(jnp.bfloat16)
        begin_at = begin_at + values.shape[1]


def shared_body(at_ref, mine_ref, near_ref, far_ref, cross_ref, step_ref, out_ref):
    at = at_ref[0]
    rows = mine_ref.shape[0]
    lanes = lane_ids(rows, 128)
    states = mine_ref.shape[1] - 384
    for j, ref in enumerate((mine_ref, near_ref, far_ref, cross_ref)):
        values = ref[...].astype(jnp.float32)
        here = pl.ds(pl.multiple_of((at ^ j) * rows, rows), rows)
        key, value = values[:, :128], values[:, 128:256]
        low = jnp.where(lanes < HEAD, key, pltpu.roll(value, HEAD, 1))
        high = jnp.where(lanes < HEAD, pltpu.roll(key, HEAD, 1), value)
        out_ref[here, :128] = jnp.where(at < 2, low, high).astype(jnp.bfloat16)
        out_ref[here, 128 : 128 + states] = values[:, 256 : 256 + states].astype(jnp.bfloat16)
        out_ref[here, 128 + states :] = (
            values[:, 256 + states :] + step_ref[here]
        ).astype(jnp.bfloat16)


def call_kernel(body, outs, scratch, *args, deps=(), micros=2, limit=12, aliases=None):
    shapes = [jax.ShapeDtypeStruct(shape, kind) for shape, kind in outs]
    count, extra = len(args), len(deps)
    whole = pl.BlockSpec(memory_space=pltpu.VMEM)

    def wrapped(*refs):
        body(*refs[:count], *refs[count + extra :])

    return pl.pallas_call(
        wrapped,
        out_shape=shapes,
        in_specs=[pl.BlockSpec(memory_space=pltpu.SMEM)]
        + [whole] * (count - 1)
        + [whole] * extra,
        out_specs=[whole] * len(shapes),
        scratch_shapes=[pltpu.VMEM(shape, kind) for shape, kind in scratch],
        input_output_aliases=aliases or {},
        compiler_params=pltpu.CompilerParams(vmem_limit_bytes=limit * 2**20),
        cost_estimate=pl.CostEstimate(
            flops=int(micros * 1e9), bytes_accessed=0, transcendentals=0
        ),
    )(*args, *deps)


def sequence_tables(seg_ids):
    length = seg_ids.shape[0]
    places = jnp.arange(length, dtype=jnp.int32)
    starts = jnp.where((places == 0) | (seg_ids != jnp.roll(seg_ids, 1)), places, 0)
    position = places - lax.cummax(starts, axis=0)
    half_dim = HEAD // 2
    frequency = jnp.exp(-jnp.log(ROPE_BASE) * jnp.arange(half_dim, dtype=jnp.float32) / half_dim)
    angles = position.astype(jnp.float32)[:, None] * frequency[None, :]
    cosine, sine = jnp.cos(angles), jnp.sin(angles)
    cosine = jnp.concatenate([cosine] * 4, axis=1)
    sine = jnp.concatenate([-sine, sine] * 2, axis=1)
    masks = [jnp.ones((length,), jnp.float32)]
    for lag in range(1, CONV):
        masks.append(
            ((places >= lag) & (seg_ids == jnp.roll(seg_ids, lag))).astype(jnp.float32)
        )
    masks = jnp.stack(masks + [jnp.zeros((length,), jnp.float32)] * (8 - CONV), axis=1)
    return cosine, sine, jnp.pad(masks, ((0, 8), (0, 0)))


def tap_rows(kernel, offset):
    taps = jnp.concatenate([kernel.T, offset[None, :]], axis=0)
    return jnp.pad(taps, ((0, 8 - taps.shape[0]), (0, 0)))


def shards(
    tokens,
    segment_ids,
    cotangent,
    norm_gain,
    w_z,
    w_x,
    w_bc,
    w_dt,
    conv_x,
    conv_bias_x,
    conv_bc,
    conv_bias_bc,
    dt_bias,
    a_log,
    d_skip,
    mixer_gain,
    w_mixer_out,
    w_query,
    w_keyval,
    w_attn_out,
    ffn_gain,
    w_gate,
    w_up,
    w_down,
):
    half_type = jnp.bfloat16
    full_type = jnp.float32
    rows, width = tokens.shape
    length = segment_ids.shape[0]
    channels = w_z.shape[1]
    heads = w_dt.shape[1]
    hidden_local = w_gate.shape[1]
    states = 2 * STATE
    blocks = length // rows

    row_count = w_bc.shape[0]
    gain_rows = norm_gain.shape[0]
    conv_rows = conv_bc.shape[0]
    at = lax.axis_index("tp").astype(jnp.int32).reshape(1)
    order = feature_order()
    x_at, core_at = place_bits()
    x_core = jnp.zeros((1,), jnp.int32)

    row_half = ((rows, width), half_type)
    row_full = ((rows, width), full_type)
    both_mine, tok_rows = call_kernel(
        front_body,
        [((2 * rows, width), half_type), ((rows, width), half_type)],
        [],
        order,
        tokens,
        cotangent,
    )

    small = jnp.stack([norm_gain, ffn_gain, conv_bc.reshape(-1), jnp.repeat(conv_bias_bc, CONV)], 1)
    shared_in = jnp.concatenate(
        [w_keyval, w_bc, jnp.pad(small, ((0, 0), (8, 116)))], axis=1
    ).astype(half_type)
    step_wide = jnp.pad(w_dt, ((0, 0), (0, 128 - heads)))
    if staged():
        mine, far, near, cross = gather_pieces(shared_in)
        (shared_shard,) = call_kernel(
            shared_body,
            [((4 * row_count, states + 256), half_type)],
            [],
            at,
            mine,
            near,
            far,
            cross,
            step_wide,
            deps=[both_mine],
            micros=1,
        )
    else:
        shared_all = lax.all_gather(shared_in, "tp", axis=0, tiled=True)
        key_rows, value_rows = (
            jnp.where(x_at == 0, shared_all[:, k : k + HEAD], shared_all[:, k + HEAD : k + 2 * HEAD])
            for k in (0, 128)
        )
        shared_shard = jnp.concatenate(
            [
                key_rows,
                value_rows,
                shared_all[:, 256 : 256 + states],
                shared_all[:, 256 + states :] + step_wide.astype(half_type),
            ],
            axis=1,
        )
    def pack(turned, *shards, deps=()):
        width_all = sum(shard.size for shard in shards) // w_x.shape[0]
        return call_kernel(
            functools.partial(pack_body, turned),
            [((w_x.shape[0], width_all), half_type)],
            [],
            x_core,
            *shards,
            deps=deps,
            micros=1,
        )[0]

    gather = Gather(jnp.concatenate([w_x.astype(half_type), shared_shard], axis=1))
    both = gather_pieces(both_mine)
    late_gather = Gather(
        pack((2, 3), w_z, w_query, w_mixer_out, w_attn_out, deps=[shared_shard, both[2]])
    )
    seg_ids = after(segment_ids.reshape(-1, 128), shared_shard).reshape(-1)
    cosine, sine, keep_masks = sequence_tables(seg_ids)
    seg_col, seg_row = seg_ids[:, None], seg_ids[None, :]
    taps_x = tap_rows(conv_x, conv_bias_x)
    rates = jnp.pad(jnp.stack([dt_bias, a_log], axis=1), ((0, 8 - heads), (0, 126)))
    gains = jnp.stack([mixer_gain, jnp.repeat(d_skip, channels // heads)])
    gains = jnp.pad(gains, ((0, 6), (0, 0)))

    keep_masks = after(keep_masks, shared_shard)
    tables = [cosine, sine, keep_masks, taps_x, rates, gains]
    for k in range(3):
        gather.step(*(tables if k == 2 else []))
        late_step = late_gather.step()
    steps = gather.step()
    late_last = late_gather.step()
    ffn_shard = pack((2,), w_gate, w_up, w_down, deps=[*late_step[:1], *steps[1:]])
    ffn_gather = Gather(ffn_shard)

    parts = gather.parts()
    columns = channels + 128 + states + 128
    first_in, proj, weight, small_rows, taps_bc = call_kernel(
        functools.partial(project_body, len(parts)),
        [
            ((blocks, rows, width), half_type),
            ((blocks, rows, columns), full_type),
            ((width, columns), half_type),
            ((8, width), full_type),
            ((8, states), full_type),
        ],
        [],
        order,
        *both,
        *parts,
        micros=6,
        limit=20,
    )
    gain_one, gain_two = small_rows[0:1], small_rows[1:2]

    ffn_gather.step(first_in)
    scan_out, mixed, raw, pre, basis, inputs, time_rows, time_cols = call_kernel(
        functools.partial(ssd_forward_body, heads),
        [
            ((length, channels), full_type),
            ((length, channels), half_type),
            ((length, channels + states), half_type),
            ((length, channels + states), half_type),
            ((length, states), half_type),
            ((length, channels), half_type),
            ((24, length), full_type),
            ((length, 128), full_type),
        ],
        [
            ((length + 8, channels), full_type),
            ((length + 8, states), full_type),
            ((8, length), full_type),
        ],
        at,
        proj,
        seg_col,
        seg_row,
        keep_masks,
        taps_x,
        taps_bc,
        rates,
        deps=[ffn_shard, late_gather.ready],
        micros=11,
        limit=20,
    )
    parts = late_gather.parts()
    head_half = ((length, 128), half_type)
    head_full = ((length, 128), full_type)
    ffn_gather.step(scan_out, *late_last[1:])
    cat, gate_in, combined, query, keyk, valv, logs, late_weight, out_weight = call_kernel(
        functools.partial(attend_forward_body, len(parts)),
        [
            ((blocks, rows, channels + 128), half_type),
            ((blocks, rows, channels), half_type),
            ((length, channels), half_type),
            head_half,
            head_half,
            head_half,
            head_full,
            ((width, channels + 128), half_type),
            ((width, channels + 128), half_type),
        ],
        [],
        at,
        first_in,
        proj,
        scan_out,
        mixed,
        seg_col,
        seg_row,
        cosine,
        sine,
        gains,
        *parts,
        deps=[ffn_gather.ready],
        micros=9,
        limit=20,
    )

    def row_products(values, weight, deps=()):
        return call_kernel(
            product_body,
            [((2 * rows, width), full_type), ((2 * rows, width), half_type)],
            [],
            x_core,
            values,
            weight,
            deps=deps,
        )

    keep, give = row_products(cat, out_weight, deps=ffn_gather.arrivals)
    ffn_gather.step(cat)
    mix_terms = reduce_pieces(keep, give, ffn_gather.ready)
    ffn_gather.step()
    after_mix, second_mine = call_kernel(
        mixed_body,
        [row_full, row_half],
        [],
        order,
        tok_rows,
        *mix_terms[:3],
        gain_two,
        deps=[ffn_gather.ready],
    )
    second_far = flip(second_mine, "tp", 2)
    second_near = flip(second_mine, "tp", 1)

    parts = ffn_gather.parts()
    filled = [
        ((blocks, rows, width), half_type),
        ((blocks, rows, width), half_type),
        ((blocks, rows, hidden_local), half_type),
        ((blocks, rows, 2 * hidden_local), half_type),
    ]
    sums = [row_full, row_half]
    *filled_in, d_keep, d_give, ffn_weight = call_kernel(
        functools.partial(ffn_body, (0, 2), True),
        filled + sums + [((width, 3 * hidden_local), half_type)],
        [],
        x_core,
        second_mine,
        second_near,
        both[0],
        both[2],
        *parts,
        micros=5,
        limit=20,
    )
    *filled_in, d_keep_x, d_give_x = call_kernel(
        functools.partial(ffn_body, (1, 3), False),
        filled + sums,
        [],
        x_core,
        second_far,
        flip(after(second_far, d_give), "tp", 1),
        both[1],
        both[3],
        ffn_weight,
        *filled_in,
        micros=5,
        limit=20,
        aliases={6: 0, 7: 1, 8: 2, 9: 3},
    )
    second_in, cot_all, hidden, d_gate_up = (
        array.reshape(length, array.shape[2]) for array in filled_in
    )
    near = flip(d_give, "tp", 1)
    passed = d_keep_x + flip(d_give_x, "tp", 1).astype(full_type)
    d_second = d_keep, near, flip(passed.astype(half_type), "tp", 2)
    ffn_scatter = Scatter(
        [
            contract_rows(second_in, d_gate_up).astype(half_type),
            contract_rows(cot_all, hidden).astype(half_type),
        ],
        d_second[2],
    )

    d_after, d_mix = call_kernel(
        after_back_body,
        [row_full, row_half],
        [],
        order,
        after_mix,
        both_mine,
        *d_second,
        gain_two,
        deps=[ffn_scatter.ready],
    )
    d_mix_all = gather_pieces(d_mix, *ffn_scatter.arrivals)

    ffn_scatter.step(3)
    d_gate, d_comb, sums_gain, d_mix_whole, d_att = call_kernel(
        gate_backward_body,
        [
            ((blocks, rows, channels), half_type),
            ((length, channels), full_type),
            ((8, channels), full_type),
            ((blocks, rows, width), half_type),
            head_half,
        ],
        [],
        at,
        gate_in,
        *d_mix_all,
        out_weight,
        combined,
        gains,
        deps=[ffn_scatter.ready],
        micros=4,
    )
    (d_attn,) = call_kernel(
        attend_backward_body,
        [((blocks, rows, 256), half_type)],
        [((length, 128), full_type), ((length, 128), full_type)],
        at,
        d_att,
        seg_col,
        seg_row,
        cosine,
        sine,
        query,
        keyk,
        valv,
        logs,
        micros=7,
    )
    out_terms = reduce_pieces(*row_products(filled_in[2], ffn_weight, deps=[d_comb]))
    first_rows = first_in.reshape(length, width)
    gate_scatter = Scatter(
        [
            contract_rows(first_rows, d_gate.reshape(length, channels)).astype(half_type),
            contract_rows(first_rows, d_attn.reshape(length, 256)).astype(half_type),
            contract_rows(
                d_mix_whole.reshape(length, width), cat.reshape(length, channels + 128)
            ).astype(half_type),
        ],
    )
    ffn_scatter.step(2, d_attn)
    d_inputs_t, d_basis_b, d_basis_c, q_rows, mixed_t, sums_skip = call_kernel(
        functools.partial(ssd_backward_body, heads),
        [
            ((channels, length), full_type),
            ((STATE, length), full_type),
            ((length, STATE), full_type),
            ((8, length), full_type),
            ((channels, length), full_type),
            ((8, channels), full_type),
        ],
        [
            ((length, channels), half_type),
            ((channels, length), half_type),
            ((STATE, length), half_type),
        ],
        at,
        d_comb,
        scan_out,
        seg_col,
        seg_row,
        mixed,
        basis,
        inputs,
        time_rows,
        time_cols,
        deps=[ffn_scatter.ready, gate_scatter.ready, out_terms[3]],
        micros=12,
        limit=20,
    )
    ffn_scatter.step(1, d_basis_c)
    gate_scatter.step(3, d_basis_c)
    d_scan, sums_x, sums_bc, sums_rate = call_kernel(
        functools.partial(conv_backward_body, heads),
        [
            ((blocks, rows, channels + states + 128), half_type),
            ((8, channels), full_type),
            ((8, states), full_type),
            ((8, 128), full_type),
        ],
        [
            ((length + 8, channels), full_type),
            ((length + 8, states), full_type),
            ((length + 8, channels), full_type),
            ((length + 8, states), full_type),
            ((channels, length), full_type),
            ((8, length), full_type),
        ],
        at,
        raw,
        d_comb,
        keep_masks,
        taps_x,
        taps_bc,
        rates,
        gains,
        pre,
        time_rows,
        d_inputs_t,
        d_basis_b,
        d_basis_c,
        q_rows,
        mixed_t,
        deps=[ffn_scatter.ready, gate_scatter.ready, out_terms[2]],
        micros=7,
        limit=24,
    )
    sum_gate, sum_up, sum_down, ffn_rows = ffn_scatter.total(
        (
            (0, hidden_local, False),
            (hidden_local, hidden_local, False),
            (2 * hidden_local, hidden_local, True),
        ),
        (0, hidden_local),
        w_gate,
        w_up,
    )
    scan_scatter = Scatter(
        [
            contract_rows(
                first_rows, d_scan.reshape(length, channels + states + 128)
            ).astype(half_type)
        ],
    )
    sums_mix = jnp.concatenate([sums_gain[:4], sums_skip[:4]], axis=0)
    smalls = SumStages(jnp.concatenate([sums_bc, sums_x, sums_mix, sums_rate], axis=1), states)
    def first_product(kind, pieces, deps):
        return call_kernel(
            functools.partial(first_back_body, pieces),
            [((2 * rows, width), kind)],
            [],
            x_core,
            d_gate,
            d_attn,
            d_scan,
            late_weight,
            weight,
            deps=deps,
            micros=2,
        )[0]

    give = first_product(half_type, (2, 3), [scan_scatter.ready])
    gate_scatter.step(2, give)
    keep = first_product(full_type, (0, 1), [gate_scatter.ready, *ffn_scatter.arrivals])
    scan_scatter.step(3, keep)
    d_first = reduce_pieces(keep, give, scan_scatter.ready)
    scan_scatter.step(2, d_first[3])
    gate_scatter.step(1, d_first[3])
    scan_scatter.step(1, d_first[2])
    scan_ready = scan_scatter.ready
    smalls.turn(d_first[2])
    flat, bc_sums = smalls.total()
    device = lax.axis_index("fsdp") * 4 + lax.axis_index("tp")
    sum_conv = lax.dynamic_slice_in_dim(bc_sums[:4].T, device * conv_rows, conv_rows)
    sum_bias = lax.dynamic_slice_in_dim(bc_sums[4], device * conv_rows, conv_rows)
    (grad_tokens,) = call_kernel(
        token_back_body,
        [row_full],
        [],
        order,
        tok_rows,
        d_after,
        *d_first[:3],
        gain_one,
        deps=[scan_ready],
    )

    sum_z, sum_mixer_out, sum_attn_out, sum_query, sum_keyval, gate_rows = gate_scatter.total(
        (
            (0, channels, False),
            (channels + 256, channels, True),
            (2 * channels + 256, 128, True),
            (channels, 128, False),
            (channels + 128, 128, False),
        ),
        (0, channels, channels + 128),
        w_z,
        w_query,
        shared_shard[:, :128],
    )
    sum_x, sum_bc, sum_step, scan_rows = scan_scatter.total(
        ((0, channels, False), (channels, states, False), (channels + states, heads, False)),
        (0, channels, channels + states),
        w_x,
        shared_shard[:, 128 : 128 + states],
        w_dt,
    )
    keep, give = call_kernel(
        shared_sums_body,
        [((2 * row_count, states + 256), full_type)] * 2,
        [],
        at,
        sum_bc,
        sum_keyval,
        gate_rows,
        scan_rows,
        ffn_rows,
        deps=[grad_tokens],
        micros=1,
    )
    near = flip(give, "tp", 1)
    far = flip(keep[row_count:] + near[row_count:], "tp", 2)
    grad_bc, grad_keyval, gain_sums = call_kernel(
        shared_total_body,
        [
            ((row_count, states), full_type),
            ((row_count, 256), full_type),
            ((row_count, 128), full_type),
        ],
        [],
        at,
        keep,
        near,
        far,
        jnp.pad(jnp.stack([norm_gain, ffn_gain], 1), ((0, 0), (0, 126)), constant_values=1.0),
        micros=1,
    )
    sum_gain_one, sum_gain_two = gain_sums[:, 0], gain_sums[:, 1]

    (layer_out,) = call_kernel(
        output_body,
        [row_half],
        [],
        order,
        after_mix,
        *out_terms[:3],
    )
    x_sums = flat[:, states : states + channels]
    mix_sums = flat[:, states + channels : states + 2 * channels]
    rate_sums = flat[:, states + 2 * channels :]
    return (
        layer_out,
        grad_tokens,
        sum_gain_one,
        sum_z,
        sum_x,
        grad_bc,
        sum_step,
        x_sums[:4].T,
        x_sums[4],
        sum_conv,
        sum_bias,
        rate_sums[:heads, 0],
        rate_sums[:heads, 1],
        mix_sums[4].reshape(heads, channels // heads).sum(axis=1),
        mix_sums[0],
        sum_mixer_out,
        sum_query,
        grad_keyval,
        sum_attn_out,
        sum_gain_two,
        sum_gate,
        sum_up,
        sum_down,
    )


def solution(mesh):
    placed = (
        P(("fsdp", "tp"), None),
        P("fsdp"),
        P(("fsdp", "tp"), None),
        P(("fsdp", "tp")),
        P("fsdp", "tp"),
        P("fsdp", "tp"),
        P(("fsdp", "tp"), None),
        P("fsdp", "tp"),
        P("tp", None),
        P("tp"),
        P(("fsdp", "tp"), None),
        P(("fsdp", "tp")),
        P("tp"),
        P("tp"),
        P("tp"),
        P("tp"),
        P("tp", "fsdp"),
        P("fsdp", "tp"),
        P(("fsdp", "tp"), None),
        P("tp", "fsdp"),
        P(("fsdp", "tp")),
        P("fsdp", "tp"),
        P("fsdp", "tp"),
        P("tp", "fsdp"),
    )
    return jax.shard_map(
        shards,
        mesh=mesh,
        in_specs=placed,
        out_specs=(
            P(("fsdp", "tp"), None),
            P(("fsdp", "tp"), None),
            P(("fsdp", "tp")),
            P("fsdp", "tp"),
            P("fsdp", "tp"),
            P(("fsdp", "tp"), None),
            P("fsdp", "tp"),
            P("tp", None),
            P("tp"),
            P(("fsdp", "tp"), None),
            P(("fsdp", "tp")),
            P("tp"),
            P("tp"),
            P("tp"),
            P("tp"),
            P("tp", "fsdp"),
            P("fsdp", "tp"),
            P(("fsdp", "tp"), None),
            P("tp", "fsdp"),
            P(("fsdp", "tp")),
            P("fsdp", "tp"),
            P("fsdp", "tp"),
            P("tp", "fsdp"),
        ),
        check_vma=False,
    )
```

```python
import functools

import jax
import jax.numpy as jnp
from jax import lax
from jax.experimental import pallas as pl
from jax.experimental.pallas import tpu as pltpu
from jax.sharding import PartitionSpec as P

STATE = 128
CONV = 4
HEADS = 8
KV_HEADS = 2
HEAD = 64

EPS = 1e-06
ROPE_BASE = 10000.0
NEG_FILL = -1e30
LOG2_E = 1.4426950408889634


def contract_rows(left_side, right_side):
    return lax.dot_general(
        left_side, right_side, (((0,), (0,)), ((), ())), preferred_element_type=jnp.float32
    )


def contract_cols(left_side, right_side):
    return lax.dot_general(
        left_side, right_side, (((1,), (1,)), ((), ())), preferred_element_type=jnp.float32
    )


def split_cols(matrix, widths):
    pieces = []
    begin_at = 0
    for part_width in widths:
        pieces.append(matrix[:, begin_at : begin_at + part_width])
        begin_at = begin_at + part_width
    return pieces


def flip(values, axis, mask):
    size = lax.axis_size(axis)
    return lax.ppermute(values, axis, [(i, i ^ mask) for i in range(size)])


def ring(values, step):
    return lax.ppermute(values, "fsdp", [(i, (i + 2 * step) % 8) for i in range(8)])


def staged():
    return lax.axis_size("fsdp") == 8


def place_bits():
    index = lax.axis_index("tp")
    return index // 2, index % 2


def gather_pieces(rows_in, *deps):
    far = flip(rows_in, "tp", 2)
    near = flip(rows_in, "tp", 1)
    cross = flip(after(far, *deps), "tp", 1)
    return rows_in, far, near, cross


def reduce_pieces(keep, give, *deps):
    half = keep.shape[0] // 2
    near = flip(give, "tp", 1)
    passed = after((keep[half:] + near[half:].astype(jnp.float32)).astype(jnp.bfloat16), *deps)
    far = flip(passed, "tp", 2)
    return keep, near, far, passed


def fsdp_place():
    index = lax.axis_index("fsdp")
    return index // 2, index % 2


def after(value, *deps):
    if not deps:
        return value

    def body(_, value_ref, out_ref):
        out_ref[...] = value_ref[...]

    return call_kernel(
        body, [(value.shape, value.dtype)], [], no_scalar(), value, deps=deps, micros=1, limit=8
    )[0]


def no_scalar():
    return jnp.zeros((1,), jnp.int32)


def fetch_blocks(grads, rows, places, held, sems):
    copies = []
    for k, (grad, here) in enumerate(zip(grads, held)):
        for n, (dy, dz) in enumerate(places):
            copies.append(
                pltpu.make_async_copy(
                    grad.at[pl.ds((dy * 4 + dz) * rows, rows)],
                    here.at[pl.ds(n * rows, rows)],
                    sems.at[k * len(places) + n],
                )
            )
    for copy in copies:
        copy.start()

    def blocks(n):
        for k in range(len(grads)):
            copies[k * len(places) + n].wait()
        return [here[n * rows : n * rows + rows] for here in held]

    return blocks


def store_side_by_side(values, out_ref):
    begin_at = 0
    for value in values:
        out_ref[:, begin_at : begin_at + value.shape[1]] = value.astype(out_ref.dtype)
        begin_at = begin_at + value.shape[1]


def add_arrivals(values, arrivals):
    sums, begin_at = [], 0
    for value in values:
        columns = slice(begin_at, begin_at + value.shape[1])
        total = value.astype(jnp.float32)
        for arrival in arrivals:
            total = total + arrival[:, columns].astype(jnp.float32)
        sums.append(total)
        begin_at = begin_at + value.shape[1]
    return sums


def put_extra(values, out_ref, rows):
    width = out_ref.shape[1]
    halves = jnp.concatenate([values[:, :width], values[:, width:]], axis=0)
    out_ref[rows : rows + 16] = halves.astype(out_ref.dtype)


def get_extra(ref, rows):
    values = ref[rows : rows + 16].astype(jnp.float32)
    return jnp.concatenate([values[:8], values[8:]], axis=1)


def first_block_body(count, rows, extra, _, *refs):
    extra_ref, refs = (refs[0], refs[1:]) if extra else (None, refs)
    grads, out_ref, held, sems = refs[:count], refs[count], refs[count + 1 : -1], refs[-1]
    blocks = fetch_blocks(grads, rows, [(1, 3)], held, sems)
    if extra:
        put_extra(extra_ref[...], out_ref, rows)
    store_side_by_side(blocks(0), out_ref.at[:rows])


def step_body(count, arriving, rows, dz, extra, _, *refs):
    extra_ref, refs = (refs[0], refs[1:]) if extra else (None, refs)
    arrivals, refs = refs[:arriving], refs[arriving:]
    grads, (send_ref, next_ref), refs = refs[:count], refs[count : count + 2], refs[count + 2 :]
    if extra:
        extra_out, refs = refs[0], refs[1:]
    blocks = fetch_blocks(grads, rows, [(1, dz - 1), (0, dz)], refs[:-1], refs[-1])
    if extra:
        came = get_extra(arrivals[-1], rows)
        total = extra_ref[...] + came
        extra_out[...] = total
        put_extra(total if arriving == 1 else came, send_ref, rows)
        next_ref[rows : rows + 16] = jnp.zeros((16, next_ref.shape[1]), next_ref.dtype)
    store_side_by_side(blocks(0), next_ref.at[:rows])
    sums = add_arrivals(blocks(1), [ref[:rows] for ref in arrivals])
    store_side_by_side(sums, send_ref.at[:rows])


def total_body(count, rows, columns, weighted, arriving, extra, _, *refs):
    size = len(weighted)
    extra_ref, refs = (refs[0], refs[1:]) if extra else (None, refs)
    arrivals, refs = refs[:arriving], refs[arriving:]
    grads, weights, refs = refs[:count], refs[count : count + size], refs[count + size :]
    outs, by_row_ref = refs[: len(columns)], refs[len(columns)]
    if extra:
        refs[len(columns) + 1][...] = extra_ref[...] + get_extra(arrivals[-1], rows)
    held, sems = refs[len(columns) + 1 + extra : -1], refs[-1]
    arrivals = [ref[:rows] for ref in arrivals]
    blocks = fetch_blocks(grads, rows, [(0, 0)], held[:count], sems)
    held = held[count:]
    copies = [
        pltpu.make_async_copy(weight, here, sems.at[count + k])
        for k, (weight, here) in enumerate(zip(weights, held))
    ]
    for copy in copies:
        copy.start()
    sums = add_arrivals(blocks(0), arrivals)
    total = jnp.concatenate(sums, axis=1) if len(sums) > 1 else sums[0]
    for (begin_at, width, turned), out_ref in zip(columns, outs):
        values = total[:, begin_at : begin_at + width]
        out_ref[...] = values.T if turned else values
    by_row = jnp.zeros((total.shape[0], 1), jnp.float32)
    for (begin_at, offset, width), copy, here in zip(weighted, copies, held):
        copy.wait()
        values = total[:, begin_at : begin_at + width]
        rounded = here[:, offset : offset + width].astype(jnp.bfloat16).astype(jnp.float32)
        by_row = by_row + jnp.sum(values * rounded, axis=1, keepdims=True)
    by_row_ref[...] = jnp.broadcast_to(by_row, by_row_ref.shape)


class Scatter:
    def __init__(self, grads, *deps, extra=None):
        self.grads = grads
        self.rows = grads[0].shape[0] // 8
        self.width = sum(grad.shape[1] for grad in grads)
        self.arrivals = []
        self.ready = grads[0]
        self.extra = [] if extra is None else [extra]
        if staged():
            (first,) = call_kernel(
                functools.partial(first_block_body, len(grads), self.rows, len(self.extra)),
                [((self.rows + 16 * len(self.extra), self.width), jnp.bfloat16)],
                [((self.rows, grad.shape[1]), grad.dtype) for grad in grads],
                no_scalar(),
                *self.extra,
                *grads,
                deps=deps,
                micros=1,
                distant=len(grads),
                sems=len(grads),
            )
            self.ready = first
            self.arrivals = [flip(first, "fsdp", 1)]

    def step(self, dz, *deps):
        if not staged():
            return ()
        block = ((self.rows + 16 * len(self.extra), self.width), jnp.bfloat16)
        send, following, *self.extra = call_kernel(
            functools.partial(
                step_body, len(self.grads), len(self.arrivals), self.rows, dz, len(self.extra)
            ),
            [block, block] + [(extra.shape, extra.dtype) for extra in self.extra],
            [((2 * self.rows, grad.shape[1]), grad.dtype) for grad in self.grads],
            no_scalar(),
            *self.extra,
            *self.arrivals,
            *self.grads,
            deps=deps,
            micros=1,
            distant=len(self.grads),
            sems=2 * len(self.grads),
        )
        self.ready = send
        self.arrivals = [flip(following, "fsdp", 1), ring(send, 1)]
        return self.arrivals

    def total(self, columns, weighted, *weights, deps=()):
        extra = self.extra if staged() else []
        if staged():
            grads, rows = self.grads, self.rows
        else:
            grads = [
                lax.psum_scatter(
                    jnp.concatenate(self.grads, axis=1), "fsdp", scatter_dimension=0, tiled=True
                )
            ]
            rows = grads[0].shape[0]
        shapes = [
            ((width, rows) if turned else (rows, width), jnp.float32)
            for _, width, turned in columns
        ]
        outs = call_kernel(
            functools.partial(
                total_body, len(grads), rows, columns, weighted, len(self.arrivals), len(extra)
            ),
            shapes + [((rows, 128), jnp.float32)] + [(item.shape, item.dtype) for item in extra],
            [((rows, grad.shape[1]), grad.dtype) for grad in grads]
            + [(weight.shape, weight.dtype) for weight in weights],
            no_scalar(),
            *extra,
            *self.arrivals,
            *grads,
            *weights,
            deps=deps,
            micros=1,
            distant=len(grads) + len(weights),
            sems=len(grads) + len(weights),
        )
        if not staged():
            outs = list(outs) + [lax.psum(item, "fsdp") for item in self.extra]
        return outs


def join_columns(arrays, *deps):
    def body(_, *refs):
        store_side_by_side([ref[...] for ref in refs[:-1]], refs[-1])

    rows, width = arrays[0].shape[0], sum(array.shape[1] for array in arrays)
    outs = [((rows, width), arrays[0].dtype)]
    return call_kernel(body, outs, [], no_scalar(), *arrays, deps=deps, micros=1, limit=8)[0]


class Gather:
    def __init__(self, shard):
        self.shard = self.ready = shard
        if staged():
            self.along, self.across = [shard], []
        self.arrivals = []

    def step(self, *deps):
        if not staged():
            return ()
        held = self.ready = after(self.along[-1], *self.across[-1:], *deps)
        if len(self.along) < 4:
            self.along.append(ring(held, 1))
        self.across.append(flip(held, "fsdp", 1))
        self.arrivals = [self.along[-1], self.across[-1]]
        return self.arrivals

    def parts(self):
        if not staged():
            return [lax.all_gather(self.shard, "fsdp", axis=0, tiled=True)]
        return [blocks[-dz % 4] for blocks in (self.along, self.across) for dz in range(4)]


def sum_fsdp(values):
    if not staged():
        return lax.psum(values, "fsdp")
    for mask in (1, 2, 6):
        values = values + flip(values, "fsdp", mask)
    return values


def sum_tp(values):
    for mask in (1, 2):
        values = values + flip(values, "tp", mask)
    return values


def feature_order():
    if not staged():
        return jnp.arange(8, dtype=jnp.int32)
    z_at, y_at = fsdp_place()
    steps = jnp.arange(8, dtype=jnp.int32)
    return (z_at + steps % 4) % 4 * 2 + (y_at ^ (steps // 4))


CHUNK = 128


def row_chunks(rows, body, carry=0):
    def step(k, carry):
        return body(pl.ds(pl.multiple_of(k * CHUNK, CHUNK), CHUNK), carry)

    return lax.fori_loop(0, rows // CHUNK, step, carry)


def front_body(order_ref, tok_ref, cot_ref, normed_ref, tok_rel, cot_rel):
    rows_all, width = tok_ref.shape
    block = width // 8

    def chunk(rows, carry):
        for b in range(8):
            there = pl.ds(pl.multiple_of(order_ref[b] * block, block), block)
            here = slice(b * block, b * block + block)
            tok_rel[rows, here] = tok_ref[rows, there]
            cot_rel[rows, here] = cot_ref[rows, there]
        values = tok_rel[rows].astype(jnp.float32)
        normed = values * lax.rsqrt(jnp.mean(values * values, axis=-1, keepdims=True) + EPS)
        normed_ref[rows] = normed.astype(jnp.bfloat16)
        return carry

    row_chunks(rows_all, chunk)


def summed_rows(rows, keep_ref, near_ref, far_ref):
    return (
        keep_ref[rows] + near_ref[rows].astype(jnp.float32) + far_ref[rows].astype(jnp.float32)
    )


def mixed_body(_, tok_ref, keep_ref, near_ref, far_ref, gain_ref, after_ref, second_ref):
    def chunk(rows, carry):
        after = tok_ref[rows].astype(jnp.float32) + summed_rows(rows, keep_ref, near_ref, far_ref)
        after_ref[rows] = after
        normed = after * lax.rsqrt(jnp.mean(after * after, axis=-1, keepdims=True) + EPS)
        second_ref[rows] = (normed * gain_ref[...]).astype(jnp.bfloat16)
        return carry

    row_chunks(tok_ref.shape[0], chunk)


def output_body(order_ref, after_ref, keep_ref, near_ref, far_ref, out_ref):
    block = after_ref.shape[1] // 8

    def chunk(rows, carry):
        values = after_ref[rows] + summed_rows(rows, keep_ref, near_ref, far_ref)
        values = values.astype(jnp.bfloat16)
        for b in range(8):
            there = pl.ds(pl.multiple_of(order_ref[b] * block, block), block)
            out_ref[rows, there] = values[:, b * block : b * block + block]
        return carry

    row_chunks(after_ref.shape[0], chunk)


def norm_back(values, d_out, gain):
    inverse = lax.rsqrt(jnp.mean(values * values, axis=-1, keepdims=True) + EPS)
    normed = values * inverse
    scaled = d_out * gain
    return inverse * (scaled - normed * jnp.mean(scaled * normed, axis=-1, keepdims=True))


def after_back_body(
    _, after_ref, cot_ref, keep_ref, near_ref, far_ref, gain_ref, d_after_ref, d_mix_ref
):
    def chunk(rows, carry):
        d_second = summed_rows(rows, keep_ref, near_ref, far_ref)
        d_after = cot_ref[rows].astype(jnp.float32) + norm_back(
            after_ref[rows], d_second, gain_ref[...]
        )
        d_after_ref[rows] = d_after
        d_mix_ref[rows] = d_after.astype(jnp.bfloat16)
        return carry

    row_chunks(after_ref.shape[0], chunk)


def token_back_body(
    order_ref, tok_ref, d_after_ref, keep_ref, near_ref, far_ref, gain_ref, out_ref
):
    block = tok_ref.shape[1] // 8

    def chunk(rows, carry):
        d_first = summed_rows(rows, keep_ref, near_ref, far_ref)
        values = d_after_ref[rows] + norm_back(
            tok_ref[rows].astype(jnp.float32), d_first, gain_ref[...]
        )
        for b in range(8):
            there = pl.ds(pl.multiple_of(order_ref[b] * block, block), block)
            out_ref[rows, there] = values[:, b * block : b * block + block]
        return carry

    row_chunks(tok_ref.shape[0], chunk)


def piece_at(block, at):
    apart = block ^ at
    return (apart & 1) * 2 + (apart >> 1)


def head_lanes(columns, first, lanes):
    rows = columns.shape[0]
    even = jnp.broadcast_to(columns[:, first : first + 1], (rows, 128))
    odd = jnp.broadcast_to(columns[:, first + 1 : first + 2], (rows, 128))
    return jnp.where(lanes < HEAD, even, odd)


def lane_ids(rows, cols):
    return lax.broadcasted_iota(jnp.int32, (rows, cols), 1)


def row_ids(rows, cols):
    return lax.broadcasted_iota(jnp.int32, (rows, cols), 0)


def dot_nt(left_side, right_side, **kw):
    return lax.dot_general(
        left_side, right_side, (((1,), (1,)), ((), ())), preferred_element_type=jnp.float32, **kw
    )


def dot_nn(left_side, right_side):
    return jnp.dot(left_side, right_side, preferred_element_type=jnp.float32)


def dot_tn(left_side, right_side):
    return lax.dot_general(
        left_side, right_side, (((0,), (0,)), ((), ())), preferred_element_type=jnp.float32
    )


def conv_window(window, taps, offset, keep):
    rows = window.shape[0] - 8
    summed = window[8:] * taps[CONV - 1 : CONV] + offset
    for lag in range(1, CONV):
        summed = summed + window[8 - lag : 8 - lag + rows] * keep[:, lag : lag + 1] * (
            taps[CONV - 1 - lag : CONV - lag]
        )
    return summed


def log_one_plus(values):
    ratio = values / (2.0 + values)
    square = ratio * ratio
    series = jnp.full_like(values, 1.0 / 15.0)
    for odd in (13, 11, 9, 7, 5, 3, 1):
        series = series * square + 1.0 / odd
    return 2.0 * ratio * series


def scan_lanes(values, reverse):
    length = values.shape[1]
    lanes = lane_ids(*values.shape)
    step = 1
    while step < length:
        if reverse:
            moved = jnp.where(lanes < length - step, pltpu.roll(values, length - step, 1), 0.0)
        else:
            moved = jnp.where(lanes >= step, pltpu.roll(values, step, 1), 0.0)
        values = values + moved
        step = step * 2
    return values


def pair_mask(seg_col, seg_row, at_t, at_s):
    size = seg_col.shape[0]
    rows = row_ids(size, size) + at_t * size
    cols = lane_ids(size, size) + at_s * size
    return (seg_col == seg_row) & (rows >= cols)


def swap_halves(values, lanes):
    half = HEAD // 2
    return jnp.where(
        lanes % HEAD < half, pltpu.roll(values, 128 - half, 1), pltpu.roll(values, half, 1)
    )


def ssd_forward_body(
    heads,
    at_ref,
    proj_ref,
    segc_ref,
    segr_ref,
    keep_ref,
    taps_ref,
    tapb_ref,
    rate_ref,
    scan_ref,
    mixed_ref,
    raw_ref,
    pre_ref,
    basis_ref,
    inputs_ref,
    rows_ref,
    cols_ref,
    xpad,
    bpad,
    dtr,
):
    blocks, size = proj_ref.shape[0], proj_ref.shape[1]
    channels = mixed_ref.shape[1]
    states = basis_ref.shape[1]
    tail = proj_ref.shape[2] - states - 128
    at = at_ref[0]
    xpad[0:8] = jnp.zeros((8, channels), jnp.float32)
    bpad[0:8] = jnp.zeros((8, states), jnp.float32)

    def load(a, carry):
        rows = pl.ds(pl.multiple_of(a * size + 8, 8), size)
        block = piece_at(a, at)
        xpad[rows] = proj_ref[block, :, :channels]
        bpad[rows] = proj_ref[block, :, tail : tail + states]
        here = pl.ds(pl.multiple_of(a * size, size), size)
        raw_ref[here, :channels] = proj_ref[block, :, :channels].astype(jnp.bfloat16)
        raw_ref[here, channels:] = proj_ref[block, :, tail : tail + states].astype(jnp.bfloat16)
        steps = proj_ref[block, :, tail + states :]
        dtr[:, pl.ds(pl.multiple_of(a * size, size), size)] = steps.T[0:8]
        return carry

    lax.fori_loop(0, blocks, load, 0)
    raw = dtr[...] + rate_ref[:, 0:1]
    step_size = jnp.maximum(raw, 0.0) + log_one_plus(jnp.exp(-jnp.abs(raw)))
    log_rate = -step_size * jnp.exp(rate_ref[:, 1:2])
    cum = scan_lanes(log_rate, False) * LOG2_E
    length = raw.shape[1]
    rows_ref[0:8] = step_size
    rows_ref[8:16] = cum
    rows_ref[16:24] = raw
    cols_ref[...] = jnp.concatenate(
        [step_size, cum, jnp.zeros((112, length), jnp.float32)], axis=0
    ).T
    lanes = lane_ids(size, 128)

    def prepare_block(a, carry):
        window = pl.ds(pl.multiple_of(a * size, size), size + 8)
        rows = pl.ds(pl.multiple_of(a * size, size), size)
        keep = keep_ref[rows]
        columns = cols_ref[rows]
        bpre = conv_window(bpad[window], tapb_ref[0:4], tapb_ref[4:5], keep)
        pre_ref[rows, channels:] = bpre.astype(jnp.bfloat16)
        basis_ref[rows] = (bpre * jax.nn.sigmoid(bpre)).astype(jnp.bfloat16)
        for pair in range(channels // 128):
            span = slice(pair * 128, pair * 128 + 128)
            xpre = conv_window(xpad[window, span], taps_ref[0:4, span], taps_ref[4:5, span], keep)
            pre_ref[rows, span] = xpre.astype(jnp.bfloat16)
            mixed = (xpre * jax.nn.sigmoid(xpre)).astype(jnp.bfloat16)
            mixed_ref[rows, span] = mixed
            steps = head_lanes(columns, 2 * pair, lanes)
            inputs_ref[rows, span] = (steps * mixed.astype(jnp.float32)).astype(jnp.bfloat16)
        return carry

    lax.fori_loop(0, blocks, prepare_block, 0)
    state = states // 2

    def row_block(i, carry):
        rows_t = pl.ds(pl.multiple_of(i * size, size), size)
        basis_c = basis_ref[rows_t, state:]
        seg_t = segc_ref[rows_t]
        columns = cols_ref[rows_t]

        def pair_block(j, totals):
            rows_s = pl.ds(pl.multiple_of(j * size, size), size)
            allowed = pair_mask(seg_t, segr_ref[:, rows_s], i, j)
            gram = jnp.where(allowed, dot_nt(basis_c, basis_ref[rows_s, :state]), 0.0)
            cum_s = rows_ref[8:16, rows_s]
            fresh = []
            for pair in range(heads // 2):
                values = inputs_ref[rows_s, pair * 128 : pair * 128 + 128]
                outs = []
                for h in (2 * pair, 2 * pair + 1):
                    spread = columns[:, 8 + h : 9 + h] - cum_s[h : h + 1]
                    weights = (gram * jnp.exp2(jnp.minimum(spread, 0.0))).astype(jnp.bfloat16)
                    outs.append(dot_nn(weights, values))
                fresh.append(totals[pair] + jnp.where(lanes < HEAD, outs[0], outs[1]))
            return tuple(fresh)

        zero = jnp.zeros((size, 128), jnp.float32)
        totals = lax.fori_loop(0, i + 1, pair_block, (zero,) * (heads // 2))
        for pair in range(heads // 2):
            scan_ref[rows_t, pair * 128 : pair * 128 + 128] = totals[pair]
        return carry

    lax.fori_loop(0, blocks, row_block, 0)


def attend_forward_body(
    count,
    at_ref,
    first_ref,
    proj_ref,
    scan_ref,
    mixed_ref,
    segc_ref,
    segr_ref,
    cos_ref,
    sin_ref,
    gain_ref,
    *refs,
):
    parts = refs[:count]
    cat_ref, gate_ref, combined_ref, query_ref, keyk_ref, valv_ref, logs_ref = refs[count:-2]
    weight_ref, out_weight_ref = refs[-2:]
    wide = weight_ref.shape[1]
    stack_rows([part.at[:, :wide] for part in parts], weight_ref)
    stack_rows([part.at[:, wide:] for part in parts], out_weight_ref)
    blocks, size = proj_ref.shape[0], proj_ref.shape[1]
    channels = scan_ref.shape[1]
    at = at_ref[0]
    lanes = lane_ids(size, 128)
    half_type = jnp.bfloat16

    def finish_block(a, carry):
        rows = pl.ds(pl.multiple_of(a * size, size), size)
        block = piece_at(a, at)
        mine = dot_nn(first_ref[block], weight_ref[...])
        gate, query = mine[:, :channels], mine[:, channels:]
        gate_ref[block] = gate.astype(half_type)
        combined = scan_ref[rows] + gain_ref[1:2] * mixed_ref[rows].astype(jnp.float32)
        combined_ref[rows] = combined.astype(half_type)
        gated = combined * (gate * jax.nn.sigmoid(gate))
        inverse = lax.rsqrt(jnp.mean(gated * gated, axis=-1, keepdims=True) + EPS)
        cat_ref[block, :, :channels] = (gated * inverse * gain_ref[0:1]).astype(half_type)
        cosine, sine = cos_ref[rows], sin_ref[rows]
        query_ref[rows] = (query * cosine + swap_halves(query, lanes) * sine).astype(half_type)
        keyval = proj_ref[block, :, channels : channels + 128]
        keyval = keyval * jnp.where(lanes < HEAD, cosine, 1.0) + swap_halves(
            keyval, lanes
        ) * jnp.where(lanes < HEAD, sine, 0.0)
        moved = pltpu.roll(keyval, HEAD, 1)
        keyk_ref[rows] = jnp.where(lanes < HEAD, keyval, moved).astype(half_type)
        valv_ref[rows] = jnp.where(lanes < HEAD, moved, keyval).astype(half_type)
        return carry

    lax.fori_loop(0, blocks, finish_block, 0)
    for i in range(blocks):
        width = (i + 1) * size
        rows = slice(i * size, width)
        query = query_ref[rows]
        places = row_ids(size, width) + i * size
        allowed = (segc_ref[rows] == segr_ref[:, :width]) & (places >= lane_ids(size, width))
        outs, logs = [], []
        for h in range(2):
            mine = (lanes < HEAD) if h == 0 else (lanes >= HEAD)
            masked = jnp.where(mine, query, jnp.zeros_like(query))
            scores = dot_nt(masked, keyk_ref[:width]) * HEAD ** (-0.5)
            scores = jnp.where(allowed, scores, NEG_FILL)
            top = jnp.max(scores, axis=-1, keepdims=True)
            powers = jnp.exp(scores - top)
            total = jnp.sum(powers, axis=-1, keepdims=True)
            outs.append(dot_nn(powers.astype(half_type), valv_ref[:width]) / total)
            logs.append(top + jnp.log(total))
        cat_ref[piece_at(i, at), :, channels:] = jnp.where(lanes < HEAD, outs[0], outs[1]).astype(half_type)
        logs_ref[rows] = jnp.where(lanes < HEAD, logs[0], logs[1])


def gate_backward_body(
    at_ref,
    gate_ref,
    mine_ref,
    far_ref,
    near_ref,
    cross_ref,
    weight_ref,
    combined_ref,
    gain_ref,
    dgate_ref,
    dcomb_ref,
    small_ref,
    dmix_ref,
    datt_ref,
):
    blocks, size = gate_ref.shape[0], gate_ref.shape[1]
    channels = combined_ref.shape[1]
    at = at_ref[0]
    half_type = jnp.bfloat16
    for p, piece in enumerate((mine_ref, far_ref, near_ref, cross_ref)):
        dmix_ref[p] = piece[...]

    def finish_block(a, carry):
        grad_gain = carry
        rows = pl.ds(pl.multiple_of(a * size, size), size)
        block = piece_at(a, at)
        d_cat = dot_nn(dmix_ref[block], weight_ref[...])
        datt_ref[rows] = d_cat[:, channels:].astype(half_type)
        gate = gate_ref[block].astype(jnp.float32)
        sig = jax.nn.sigmoid(gate)
        act = gate * sig
        combined = combined_ref[rows].astype(jnp.float32)
        gated = combined * act
        inverse = lax.rsqrt(jnp.mean(gated * gated, axis=-1, keepdims=True) + EPS)
        normed = gated * inverse
        d_out = d_cat[:, :channels]
        grad_gain = grad_gain + jnp.sum(d_out * normed, axis=0, keepdims=True)
        scaled = d_out * gain_ref[0:1]
        d_gated = inverse * (scaled - normed * jnp.mean(scaled * normed, axis=-1, keepdims=True))
        d_comb = d_gated * act
        dcomb_ref[rows] = d_comb
        d_gate = d_gated * combined * sig * (1.0 + gate * (1.0 - sig))
        dgate_ref[block] = d_gate.astype(half_type)
        return grad_gain

    grad_gain = lax.fori_loop(0, blocks, finish_block, jnp.zeros((1, channels), jnp.float32))
    small_ref[...] = jnp.broadcast_to(grad_gain, small_ref.shape)


def attend_backward_body(
    at_ref,
    datt_ref,
    segc_ref,
    segr_ref,
    cos_ref,
    sin_ref,
    query_ref,
    keyk_ref,
    valv_ref,
    logs_ref,
    dproj_ref,
    dkey,
    dval,
):
    blocks, size = dproj_ref.shape[0], dproj_ref.shape[1]
    at = at_ref[0]
    lanes = lane_ids(size, 128)
    half_type = jnp.bfloat16
    dkey[...] = jnp.zeros_like(dkey)
    dval[...] = jnp.zeros_like(dval)
    for i in range(blocks):
        width = (i + 1) * size
        rows = slice(i * size, width)
        query = query_ref[rows]
        d_att = datt_ref[rows]
        logs = logs_ref[rows]
        places = row_ids(size, width) + i * size
        allowed = (segc_ref[rows] == segr_ref[:, :width]) & (places >= lane_ids(size, width))
        outs = []
        for h in range(2):
            mine = (lanes < HEAD) if h == 0 else (lanes >= HEAD)
            masked = jnp.where(mine, query, jnp.zeros_like(query))
            d_masked = jnp.where(mine, d_att, jnp.zeros_like(d_att))
            scores = dot_nt(masked, keyk_ref[:width]) * HEAD ** (-0.5)
            scores = jnp.where(allowed, scores, NEG_FILL)
            probs = jnp.exp(scores - logs[:, h * HEAD : h * HEAD + 1])
            d_probs = dot_nt(d_masked, valv_ref[:width])
            mean = jnp.sum(probs * d_probs, axis=-1, keepdims=True)
            d_scores = (probs * (d_probs - mean)).astype(half_type)
            outs.append(dot_nn(d_scores, keyk_ref[:width]))
            dkey[:width] += dot_tn(d_scores, masked)
            dval[:width] += dot_tn(probs.astype(half_type), d_masked)
        d_query = jnp.where(lanes < HEAD, outs[0], outs[1]) * HEAD ** (-0.5)
        cosine, sine = cos_ref[rows], sin_ref[rows]
        d_query = d_query * cosine - swap_halves(d_query, lanes) * sine
        dproj_ref[piece_at(i, at), :, :128] = d_query.astype(half_type)

    def key_block(a, carry):
        rows = pl.ds(pl.multiple_of(a * size, size), size)
        d_key, d_val = dkey[rows], dval[rows]
        d_key = (d_key + pltpu.roll(d_key, HEAD, 1)) * HEAD ** (-0.5)
        d_val = d_val + pltpu.roll(d_val, HEAD, 1)
        d_key = d_key * cos_ref[rows] - swap_halves(d_key, lanes) * sin_ref[rows]
        dproj_ref[piece_at(a, at), :, 128:] = jnp.where(lanes < HEAD, d_key, d_val).astype(
            half_type
        )
        return carry

    lax.fori_loop(0, blocks, key_block, 0)


def silu_slope(values):
    sig = jax.nn.sigmoid(values)
    return sig * (1.0 + values * (1.0 - sig))


def conv_back(d_window, keep_window, taps):
    rows = d_window.shape[0] - 8
    summed = d_window[:rows] * taps[CONV - 1 : CONV]
    for lag in range(1, CONV):
        moved = d_window * keep_window[:, lag : lag + 1]
        summed = summed + moved[lag : lag + rows] * taps[CONV - 1 - lag : CONV - lag]
    return summed


def conv_grads(d_pre, window, keep):
    rows = d_pre.shape[0]
    sums = []
    for tap in range(CONV):
        lag = CONV - 1 - tap
        moved = window[8 - lag : 8 - lag + rows]
        if lag:
            moved = moved * keep[:, lag : lag + 1]
        sums.append(jnp.sum(d_pre * moved, axis=0, keepdims=True))
    sums.append(jnp.sum(d_pre, axis=0, keepdims=True))
    sums.append(jnp.zeros((8 - len(sums), d_pre.shape[1]), jnp.float32))
    return jnp.concatenate(sums, axis=0)


def ssd_backward_body(
    heads,
    at_ref,
    dcomb_ref,
    scan_ref,
    segc_ref,
    segr_ref,
    mixed_ref,
    basis_ref,
    inputs_ref,
    rows_ref,
    cols_ref,
    dint,
    dbt,
    dcb,
    qrow,
    mixt,
    skip_ref,
    dsc,
    dst,
    cbt,
):
    length, channels = scan_ref.shape
    state = dbt.shape[0]
    size = length // 4
    blocks = 4
    half_type = jnp.bfloat16
    lanes = lane_ids(size, 128)
    dint[...] = jnp.zeros_like(dint)
    dbt[...] = jnp.zeros_like(dbt)
    head_of = jnp.where(
        lane_ids(8, channels) // HEAD == row_ids(8, channels), 1.0, 0.0
    ).astype(jnp.float32)

    def load(a, carry):
        rows = pl.ds(pl.multiple_of(a * size, size), size)
        d_comb = dcomb_ref[rows]
        d_scan = d_comb.astype(half_type)
        dsc[rows] = d_scan
        d_full = d_scan.astype(jnp.float32)
        dst[:, rows] = d_full.T.astype(half_type)
        cbt[:, rows] = basis_ref[rows, state:].astype(jnp.float32).T.astype(half_type)
        mixed = mixed_ref[rows].astype(jnp.float32)
        mixt[:, rows] = mixed.T
        qrow[:, rows] = dot_nt(head_of, d_full * scan_ref[rows], precision=lax.Precision.HIGHEST)
        return carry + jnp.sum(d_comb * mixed, axis=0, keepdims=True)

    skips = lax.fori_loop(0, blocks, load, jnp.zeros((1, channels), jnp.float32))
    skip_ref[...] = jnp.broadcast_to(skips, skip_ref.shape)

    def row_block(i, carry):
        rows_t = pl.ds(pl.multiple_of(i * size, size), size)
        basis_c = basis_ref[rows_t, state:]
        seg_t = segc_ref[rows_t]
        columns = cols_ref[rows_t]

        def pair_block(j, total):
            rows_s = pl.ds(pl.multiple_of(j * size, size), size)
            allowed = pair_mask(seg_t, segr_ref[:, rows_s], i, j)
            gram = jnp.where(allowed, dot_nt(basis_c, basis_ref[rows_s, :state]), 0.0)
            cum_s = rows_ref[8:16, rows_s]
            d_gram = jnp.zeros((size, size), jnp.float32)
            for pair in range(heads // 2):
                span = slice(pair * 128, pair * 128 + 128)
                values = inputs_ref[rows_s, span]
                d_scan = dsc[rows_t, span]
                for h in (2 * pair, 2 * pair + 1):
                    mine = (lanes < HEAD) if h % 2 == 0 else (lanes >= HEAD)
                    spread = columns[:, 8 + h : 9 + h] - cum_s[h : h + 1]
                    decay = jnp.exp2(jnp.minimum(spread, 0.0))
                    weights = (gram * decay).astype(half_type)
                    d_weights = dot_nt(jnp.where(mine, d_scan, jnp.zeros_like(d_scan)), values)
                    d_gram = d_gram + d_weights * decay
                    chans = slice(h * HEAD, h * HEAD + HEAD)
                    dint[chans, rows_s] += dot_nn(dst[chans, rows_t], weights)
            d_gram = jnp.where(allowed, d_gram, 0.0).astype(half_type)
            dbt[:, rows_s] += dot_nn(cbt[:, rows_t], d_gram)
            return total + dot_nn(d_gram, basis_ref[rows_s, :state])

        dcb[rows_t] = lax.fori_loop(0, i + 1, pair_block, jnp.zeros((size, state), jnp.float32))
        return carry

    lax.fori_loop(0, blocks, row_block, 0)


def conv_backward_body(
    heads,
    at_ref,
    raw_ref,
    dcomb_ref,
    keep_ref,
    taps_ref,
    tapb_ref,
    rate_ref,
    gain_ref,
    pre_ref,
    rows_ref,
    dint_ref,
    dbt,
    dcb,
    qrow_ref,
    mixt,
    dproj_ref,
    gradx_ref,
    gradb_ref,
    grads_ref,
    xpad,
    bpad,
    dpx,
    dpb,
    dint,
    qrow,
):
    blocks, size = dproj_ref.shape[0], dproj_ref.shape[1]
    channels = dcomb_ref.shape[1]
    states = pre_ref.shape[1] - channels
    length = blocks * size
    at = at_ref[0]
    half_type = jnp.bfloat16
    xpad[0:8] = jnp.zeros((8, channels), jnp.float32)
    bpad[0:8] = jnp.zeros((8, states), jnp.float32)
    dpx[length : length + 8] = jnp.zeros((8, channels), jnp.float32)
    dpb[length : length + 8] = jnp.zeros((8, states), jnp.float32)

    def load(a, carry):
        padded = pl.ds(pl.multiple_of(a * size + 8, 8), size)
        rows = pl.ds(pl.multiple_of(a * size, size), size)
        xpad[padded] = raw_ref[rows, :channels].astype(jnp.float32)
        bpad[padded] = raw_ref[rows, channels:].astype(jnp.float32)
        return carry

    lax.fori_loop(0, blocks, load, 0)
    step_size = rows_ref[0:8]
    raw = rows_ref[16:24]
    d_step, col_part = [], []
    for h in range(heads):
        chans = slice(h * HEAD, h * HEAD + HEAD)
        d_inputs = dint_ref[chans]
        mixed = mixt[chans]
        scaled = step_size[h : h + 1] * mixed
        d_step.append(jnp.sum(d_inputs * mixed, axis=0, keepdims=True))
        inputs = scaled.astype(half_type).astype(jnp.float32)
        col_part.append(jnp.sum(d_inputs * inputs, axis=0, keepdims=True))
        dint[chans] = d_inputs * step_size[h : h + 1]
    blank = jnp.zeros((8 - heads, length), jnp.float32)
    d_step = jnp.concatenate(d_step + [blank], axis=0)
    d_cum = qrow_ref[...] - jnp.concatenate(col_part + [blank], axis=0)
    d_log = scan_lanes(d_cum, True)
    rate = jnp.exp(rate_ref[:, 1:2])
    grad_rate = jnp.sum(d_log * (-step_size * rate), axis=1, keepdims=True)
    d_raw = (d_step - d_log * rate) * jax.nn.sigmoid(raw)
    d_raw = jnp.where(row_ids(8, length) < heads, d_raw, 0.0)
    grad_bias = jnp.sum(d_raw, axis=1, keepdims=True)
    lanes8 = lane_ids(8, 128)
    grads_ref[...] = jnp.where(lanes8 == 0, grad_bias, jnp.where(lanes8 == 1, grad_rate, 0.0))
    qrow[...] = d_raw

    def grad_block(a, carry):
        rows = pl.ds(pl.multiple_of(a * size, size), size)
        d_mixed = dint[:, rows].T + dcomb_ref[rows] * gain_ref[1:2]
        dpx[rows] = d_mixed * silu_slope(pre_ref[rows, :channels].astype(jnp.float32))
        d_basis = jnp.concatenate([dbt[:, rows].T, dcb[rows]], axis=1)
        dpb[rows] = d_basis * silu_slope(pre_ref[rows, channels:].astype(jnp.float32))
        return carry

    lax.fori_loop(0, blocks, grad_block, 0)

    def conv_block(a, carry):
        grad_x, grad_b = carry
        rows = pl.ds(pl.multiple_of(a * size, size), size)
        window = pl.ds(pl.multiple_of(a * size, size), size + 8)
        block = piece_at(a, at)
        keep_window = keep_ref[window]
        keep = keep_window[:size]
        d_wide = dpx[window]
        dproj_ref[block, :, :channels] = conv_back(d_wide, keep_window, taps_ref[...]).astype(
            half_type
        )
        grad_x = grad_x + conv_grads(d_wide[:size], xpad[window], keep)
        d_wide = dpb[window]
        dproj_ref[block, :, channels : channels + states] = conv_back(
            d_wide, keep_window, tapb_ref[...]
        ).astype(half_type)
        grad_b = grad_b + conv_grads(d_wide[:size], bpad[window], keep)
        d_steps = jnp.concatenate([qrow[:, rows], jnp.zeros((120, size), jnp.float32)], axis=0)
        dproj_ref[block, :, channels + states :] = d_steps.T.astype(half_type)
        return grad_x, grad_b

    grad_x, grad_b = lax.fori_loop(
        0,
        blocks,
        conv_block,
        (jnp.zeros((8, channels), jnp.float32), jnp.zeros((8, states), jnp.float32)),
    )
    gradx_ref[...] = grad_x
    gradb_ref[...] = grad_b


def stack_rows(pieces, out_ref):
    begin_at = 0
    for piece in pieces:
        out_ref[begin_at : begin_at + piece.shape[0]] = piece[...]
        begin_at = begin_at + piece.shape[0]


def project_body(count, order_ref, *refs):
    pieces, parts = refs[:4], refs[4 : 4 + count]
    first_ref, proj_ref, weight_ref, small_ref, taps_ref = refs[4 + count :]
    width = weight_ref.shape[0]
    rows = proj_ref.shape[1]
    states = taps_ref.shape[1]
    stack_rows(parts, weight_ref)
    small = weight_ref[:, weight_ref.shape[1] - 128 :].astype(jnp.float32).T[8:16]
    small_ref[...] = small
    gain = small[0:1]
    for p, piece in enumerate(pieces):
        first = (piece[...].astype(jnp.float32) * gain).astype(jnp.bfloat16)
        first_ref[p] = first
        proj_ref[p] = dot_nn(first, weight_ref[...])
    feature = row_ids(width, states)
    block = width // 8
    place = feature % block
    for b in range(8):
        place = place + jnp.where(feature // block == b, order_ref[b] * block, 0)
    channel = lane_ids(width, states)
    taps = []
    for k in range(CONV + 1):
        picked = jnp.where(place == channel * CONV + k % CONV, 1.0, 0.0).astype(jnp.bfloat16)
        found = dot_nn(small.astype(jnp.bfloat16), picked)
        taps.append(found[2:3] if k < CONV else found[3:4])
    taps.append(jnp.zeros((8 - len(taps), states), jnp.float32))
    taps_ref[...] = jnp.concatenate(taps, axis=0)


def product_body(_, values_ref, weight_ref, keep_ref, give_ref):
    rows = values_ref.shape[1]
    columns = slice(weight_ref.shape[1] - values_ref.shape[2], None)
    for p in (3, 1, 2, 0):
        result = dot_nt(values_ref[p], weight_ref[:, columns])
        if p < 2:
            keep_ref[p * rows : p * rows + rows] = result
        else:
            give_ref[p * rows - 2 * rows : p * rows - rows] = result.astype(jnp.bfloat16)


def first_back_body(
    _, gate_ref, attn_ref, scan_ref, late_ref, weight_ref, keep_ref, give_ref, token_ref
):
    token_ref[...] = jnp.zeros_like(token_ref)
    rows, channels = gate_ref.shape[1], gate_ref.shape[2]
    wide = channels + 128
    for p in (3, 2, 1, 0):
        result = dot_nt(gate_ref[p], late_ref[:, :channels])
        result = result + dot_nt(attn_ref[p, :, :128], late_ref[:, channels:wide])
        result = result + dot_nt(attn_ref[p, :, 128:], weight_ref[:, channels:wide])
        result = result + dot_nt(scan_ref[p, :, :channels], weight_ref[:, :channels])
        result = result + dot_nt(scan_ref[p, :, channels:], weight_ref[:, wide:])
        if p < 2:
            keep_ref[p * rows : p * rows + rows] = result
        else:
            give_ref[p * rows - 2 * rows : p * rows - rows] = result.astype(jnp.bfloat16)


def ffn_body(slots, fresh, _, *refs):
    pieces, cots = refs[0:2], refs[2:4]
    if fresh:
        parts, outs = refs[4:-7], refs[-7:]
        weight_ref = outs[6]
        stack_rows(parts, weight_ref)
    else:
        weight_ref, outs = refs[4], refs[-6:]
    second_ref, cot_ref, hidden_ref, dgu_ref, dkeep, dgive = outs[:6]
    hidden_local = hidden_ref.shape[2]
    rows = second_ref.shape[1]
    gate_up_weight = weight_ref.at[:, : 2 * hidden_local]
    down_weight = weight_ref.at[:, 2 * hidden_local :]
    for p, piece, cots_ref in zip(slots, pieces, cots):
        values, cot = piece[...], cots_ref[...]
        second_ref[p] = values
        cot_ref[p] = cot
        gate_up = dot_nn(values, gate_up_weight[...])
        d_hidden = dot_nn(cot, down_weight[...])
        gate, up = gate_up[:, :hidden_local], gate_up[:, hidden_local:]
        sig = jax.nn.sigmoid(gate)
        act = gate * sig
        hidden = (act * up).astype(jnp.bfloat16)
        hidden_ref[p] = hidden
        d_gate = (d_hidden * up * sig * (1.0 + gate * (1.0 - sig))).astype(jnp.bfloat16)
        d_up = (d_hidden * act).astype(jnp.bfloat16)
        dgu_ref[p, :, :hidden_local] = d_gate
        dgu_ref[p, :, hidden_local:] = d_up
        d_second = dot_nt(dgu_ref[p], gate_up_weight[...])
        if p < 2:
            dkeep[...] = d_second
        else:
            dgive[...] = d_second.astype(jnp.bfloat16)


def pick_rows(values, block, rows):
    picked = jnp.zeros((rows, values.shape[1]), values.dtype)
    for g in range(values.shape[0] // rows):
        picked = jnp.where(block == g, values[g * rows : g * rows + rows], picked)
    return picked


def shared_sums_body(conv_rows, at_ref, bc_ref, keyval_ref, *refs):
    *sums, ffn_ref, small_ref, keep_ref, give_ref = refs
    at, place = at_ref[0], at_ref[1]
    rows = keep_ref.shape[0] // 2
    states = bc_ref.shape[1]
    size = 4 * rows
    lanes = lane_ids(size, 128)
    by_row = sum(ref[...] for ref in sums)
    small = jnp.concatenate(
        [
            jnp.zeros((8, states), jnp.float32),
            small_ref[:, :states],
            jnp.zeros((112, states), jnp.float32),
        ],
        axis=0,
    ).T
    spot = row_ids(size, states)
    channel = (place * 4 + spot // rows) * conv_rows + spot % rows
    chosen = (channel == lane_ids(size, states)) & (spot % rows < conv_rows)
    small = jnp.dot(
        jnp.where(chosen, 1.0, 0.0),
        small,
        precision=lax.Precision.HIGHEST,
        preferred_element_type=jnp.float32,
    )
    gains = jnp.where(lanes == 0, by_row, jnp.where(lanes == 1, ffn_ref[...], small))
    values = jnp.concatenate([bc_ref[...], keyval_ref[...], gains], axis=1)
    for k in range(2):
        keep_ref[k * rows : k * rows + rows] = pick_rows(values, at ^ (2 * k), rows)
        give_ref[k * rows : k * rows + rows] = pick_rows(values, at ^ (2 * k + 1), rows)


def shared_total_body(at_ref, keep_ref, near_ref, far_ref, gains_ref, bc_ref, keyval_ref, out_ref):
    rows = far_ref.shape[0]
    states = bc_ref.shape[1]
    lanes = lane_ids(rows, 128)
    chip, other = keep_ref[:rows] + near_ref[:rows], far_ref[...]
    total = chip + other
    bc_ref[...] = total[:, :states]
    heads = [side[:, states : states + 128] for side in (chip, other)]
    low, high = [
        [jnp.where(at_ref[0] < 2, heads[k], heads[1 - k]) for k in range(2)][k] for k in range(2)
    ]
    keyval_ref[:, :128] = jnp.where(lanes < HEAD, low, pltpu.roll(high, HEAD, 1))
    keyval_ref[:, 128:] = jnp.where(lanes < HEAD, pltpu.roll(low, HEAD, 1), high)
    rounded = gains_ref[...].astype(jnp.bfloat16).astype(jnp.float32)
    out_ref[...] = total[:, states + 128 :] / rounded


def pack_body(turned, _, *refs):
    out_ref = refs[-1]
    begin_at = 0
    for index, ref in enumerate(refs[:-1]):
        values = ref[...]
        if index in turned:
            values = values.T
        out_ref[:, begin_at : begin_at + values.shape[1]] = values.astype(jnp.bfloat16)
        begin_at = begin_at + values.shape[1]


def shared_body(at_ref, mine_ref, near_ref, far_ref, cross_ref, step_ref, out_ref):
    at = at_ref[0]
    rows = mine_ref.shape[0]
    lanes = lane_ids(rows, 128)
    states = mine_ref.shape[1] - 384
    for j, ref in enumerate((mine_ref, near_ref, far_ref, cross_ref)):
        values = ref[...].astype(jnp.float32)
        here = pl.ds(pl.multiple_of((at ^ j) * rows, rows), rows)
        key, value = values[:, :128], values[:, 128:256]
        low = jnp.where(lanes < HEAD, key, pltpu.roll(value, HEAD, 1))
        high = jnp.where(lanes < HEAD, pltpu.roll(key, HEAD, 1), value)
        out_ref[here, :128] = jnp.where(at < 2, low, high).astype(jnp.bfloat16)
        out_ref[here, 128 : 128 + states] = values[:, 256 : 256 + states].astype(jnp.bfloat16)
        out_ref[here, 128 + states :] = (
            values[:, 256 + states :] + step_ref[here]
        ).astype(jnp.bfloat16)


def call_kernel(body, outs, scratch, *args, deps=(), micros=2, limit=8, aliases=None, distant=0, sems=0):
    shapes = [jax.ShapeDtypeStruct(shape, kind) for shape, kind in outs]
    count, extra = len(args), len(deps)
    whole = pl.BlockSpec(memory_space=pltpu.VMEM)

    def wrapped(*refs):
        body(*refs[:count], *refs[count + extra :])

    return pl.pallas_call(
        wrapped,
        out_shape=shapes,
        in_specs=[pl.BlockSpec(memory_space=pltpu.SMEM)]
        + [whole] * (count - 1 - distant)
        + [pl.BlockSpec(memory_space=pltpu.HBM)] * distant
        + [whole] * extra,
        out_specs=[whole] * len(shapes),
        scratch_shapes=[pltpu.VMEM(shape, kind) for shape, kind in scratch]
        + ([pltpu.SemaphoreType.DMA((sems,))] if sems else []),
        input_output_aliases=aliases or {},
        compiler_params=pltpu.CompilerParams(vmem_limit_bytes=limit * 2**20),
        cost_estimate=pl.CostEstimate(
            flops=int(micros * 1e9), bytes_accessed=0, transcendentals=0
        ),
    )(*args, *deps)


def sequence_tables(seg_ids):
    length = seg_ids.shape[0]
    places = jnp.arange(length, dtype=jnp.int32)
    starts = jnp.where((places == 0) | (seg_ids != jnp.roll(seg_ids, 1)), places, 0)
    position = places - lax.cummax(starts, axis=0)
    half_dim = HEAD // 2
    frequency = jnp.exp(-jnp.log(ROPE_BASE) * jnp.arange(half_dim, dtype=jnp.float32) / half_dim)
    angles = position.astype(jnp.float32)[:, None] * frequency[None, :]
    cosine, sine = jnp.cos(angles), jnp.sin(angles)
    cosine = jnp.concatenate([cosine] * 4, axis=1)
    sine = jnp.concatenate([-sine, sine] * 2, axis=1)
    masks = [jnp.ones((length,), jnp.float32)]
    for lag in range(1, CONV):
        masks.append(
            ((places >= lag) & (seg_ids == jnp.roll(seg_ids, lag))).astype(jnp.float32)
        )
    masks = jnp.stack(masks + [jnp.zeros((length,), jnp.float32)] * (8 - CONV), axis=1)
    return cosine, sine, jnp.pad(masks, ((0, 8), (0, 0)))


def tap_rows(kernel, offset):
    taps = jnp.concatenate([kernel.T, offset[None, :]], axis=0)
    return jnp.pad(taps, ((0, 8 - taps.shape[0]), (0, 0)))


def shards(
    tokens,
    segment_ids,
    cotangent,
    norm_gain,
    w_z,
    w_x,
    w_bc,
    w_dt,
    conv_x,
    conv_bias_x,
    conv_bc,
    conv_bias_bc,
    dt_bias,
    a_log,
    d_skip,
    mixer_gain,
    w_mixer_out,
    w_query,
    w_keyval,
    w_attn_out,
    ffn_gain,
    w_gate,
    w_up,
    w_down,
):
    half_type = jnp.bfloat16
    full_type = jnp.float32
    rows, width = tokens.shape
    length = segment_ids.shape[0]
    channels = w_z.shape[1]
    heads = w_dt.shape[1]
    hidden_local = w_gate.shape[1]
    states = 2 * STATE
    blocks = length // rows

    row_count = w_bc.shape[0]
    gain_rows = norm_gain.shape[0]
    conv_rows = conv_bc.shape[0]
    at = lax.axis_index("tp").astype(jnp.int32).reshape(1)
    order = feature_order()
    x_at, core_at = place_bits()
    x_core = jnp.zeros((1,), jnp.int32)

    row_half = ((rows, width), half_type)
    row_full = ((rows, width), full_type)
    normed_mine, tok_rows, cot_mine = call_kernel(
        front_body, [row_half, row_half, row_half], [], order, tokens, cotangent
    )

    small = jnp.stack([norm_gain, ffn_gain, conv_bc.reshape(-1), jnp.repeat(conv_bias_bc, CONV)], 1)
    shared_in = jnp.concatenate(
        [w_keyval, w_bc, jnp.pad(small, ((0, 0), (8, 116)))], axis=1
    ).astype(half_type)
    step_wide = jnp.pad(w_dt, ((0, 0), (0, 128 - heads)))
    if staged():
        mine, far, near, cross = gather_pieces(shared_in)
        (shared_shard,) = call_kernel(
            shared_body,
            [((4 * row_count, states + 256), half_type)],
            [],
            at,
            mine,
            near,
            far,
            cross,
            step_wide,
            deps=[normed_mine],
            micros=1,
        )
    else:
        shared_all = lax.all_gather(shared_in, "tp", axis=0, tiled=True)
        key_rows, value_rows = (
            jnp.where(x_at == 0, shared_all[:, k : k + HEAD], shared_all[:, k + HEAD : k + 2 * HEAD])
            for k in (0, 128)
        )
        shared_shard = jnp.concatenate(
            [
                key_rows,
                value_rows,
                shared_all[:, 256 : 256 + states],
                shared_all[:, 256 + states :] + step_wide.astype(half_type),
            ],
            axis=1,
        )
    def pack(turned, *shards, deps=()):
        width_all = sum(shard.size for shard in shards) // w_x.shape[0]
        return call_kernel(
            functools.partial(pack_body, turned),
            [((w_x.shape[0], width_all), half_type)],
            [],
            x_core,
            *shards,
            deps=deps,
            micros=1,
        )[0]

    gather = Gather(jnp.concatenate([w_x.astype(half_type), shared_shard], axis=1))
    normed = gather_pieces(after(normed_mine, shared_shard))
    late_gather = Gather(
        pack((2, 3), w_z, w_query, w_mixer_out, w_attn_out, deps=[shared_shard, normed[2]])
    )
    seg_ids = after(segment_ids.reshape(-1, 128), shared_shard).reshape(-1)
    cosine, sine, keep_masks = sequence_tables(seg_ids)
    seg_col, seg_row = seg_ids[:, None], seg_ids[None, :]
    taps_x = tap_rows(conv_x, conv_bias_x)
    rates = jnp.pad(jnp.stack([dt_bias, a_log], axis=1), ((0, 8 - heads), (0, 126)))
    gains = jnp.stack([mixer_gain, jnp.repeat(d_skip, channels // heads)])
    gains = jnp.pad(gains, ((0, 6), (0, 0)))

    keep_masks = after(keep_masks, shared_shard)
    tables = [cosine, sine, keep_masks, taps_x, rates, gains]
    for k in range(3):
        gather.step(*(tables if k == 2 else []))
        late_step = late_gather.step()
    steps = gather.step()
    late_last = late_gather.step()
    ffn_shard = pack((2,), w_gate, w_up, w_down, deps=[*late_step[:1], *steps[1:]])
    ffn_gather = Gather(ffn_shard)

    parts = gather.parts()
    columns = channels + 128 + states + 128
    first_in, proj, weight, small_rows, taps_bc = call_kernel(
        functools.partial(project_body, len(parts)),
        [
            ((blocks, rows, width), half_type),
            ((blocks, rows, columns), full_type),
            ((width, columns), half_type),
            ((8, width), full_type),
            ((8, states), full_type),
        ],
        [],
        order,
        *normed,
        *parts,
        micros=6,
        limit=12,
    )
    gain_one, gain_two = small_rows[0:1], small_rows[1:2]

    ffn_gather.step(small_rows)
    cot = gather_pieces(after(cot_mine, small_rows))
    scan_out, mixed, raw, pre, basis, inputs, time_rows, time_cols = call_kernel(
        functools.partial(ssd_forward_body, heads),
        [
            ((length, channels), full_type),
            ((length, channels), half_type),
            ((length, channels + states), half_type),
            ((length, channels + states), half_type),
            ((length, states), half_type),
            ((length, channels), half_type),
            ((24, length), full_type),
            ((length, 128), full_type),
        ],
        [
            ((length + 8, channels), full_type),
            ((length + 8, states), full_type),
            ((8, length), full_type),
        ],
        at,
        proj,
        seg_col,
        seg_row,
        keep_masks,
        taps_x,
        taps_bc,
        rates,
        deps=[ffn_shard, late_gather.ready],
        micros=11,
        limit=12,
    )
    parts = late_gather.parts()
    head_half = ((length, 128), half_type)
    head_full = ((length, 128), full_type)
    ffn_gather.step(time_rows, *late_last[1:])
    cat, gate_in, combined, query, keyk, valv, logs, late_weight, out_weight = call_kernel(
        functools.partial(attend_forward_body, len(parts)),
        [
            ((blocks, rows, channels + 128), half_type),
            ((blocks, rows, channels), half_type),
            ((length, channels), half_type),
            head_half,
            head_half,
            head_half,
            head_full,
            ((width, channels + 128), half_type),
            ((width, channels + 128), half_type),
        ],
        [],
        at,
        first_in,
        proj,
        scan_out,
        mixed,
        seg_col,
        seg_row,
        cosine,
        sine,
        gains,
        *parts,
        deps=[ffn_gather.ready, cot[1]],
        micros=9,
        limit=12,
    )

    def row_products(values, weight, deps=()):
        return call_kernel(
            product_body,
            [((2 * rows, width), full_type), ((2 * rows, width), half_type)],
            [],
            x_core,
            values,
            weight,
            deps=deps,
        )

    keep, give = row_products(cat, out_weight, deps=ffn_gather.arrivals)
    ffn_gather.step(query)
    mix_terms = reduce_pieces(keep, give, ffn_gather.ready)
    ffn_gather.step()
    after_mix, second_mine = call_kernel(
        mixed_body,
        [row_full, row_half],
        [],
        order,
        tok_rows,
        *mix_terms[:3],
        gain_two,
        deps=[ffn_gather.ready],
    )
    second_far = flip(second_mine, "tp", 2)
    second_near = flip(second_mine, "tp", 1)

    parts = ffn_gather.parts()
    filled = [
        ((blocks, rows, width), half_type),
        ((blocks, rows, width), half_type),
        ((blocks, rows, hidden_local), half_type),
        ((blocks, rows, 2 * hidden_local), half_type),
    ]
    sums = [row_full, row_half]
    *filled_in, d_keep, d_give, ffn_weight = call_kernel(
        functools.partial(ffn_body, (0, 2), True),
        filled + sums + [((width, 3 * hidden_local), half_type)],
        [],
        x_core,
        second_mine,
        second_near,
        cot[0],
        cot[2],
        *parts,
        micros=5,
        limit=12,
    )
    *filled_in, d_keep_x, d_give_x = call_kernel(
        functools.partial(ffn_body, (1, 3), False),
        filled + sums,
        [],
        x_core,
        second_far,
        flip(after(second_far, d_give), "tp", 1),
        cot[1],
        cot[3],
        ffn_weight,
        *filled_in,
        micros=5,
        limit=12,
        aliases={6: 0, 7: 1, 8: 2, 9: 3},
    )
    second_in, cot_all, hidden, d_gate_up = (
        array.reshape(length, array.shape[2]) for array in filled_in
    )
    near = flip(d_give, "tp", 1)
    passed = d_keep_x + flip(d_give_x, "tp", 1).astype(full_type)
    d_second = d_keep, near, flip(passed.astype(half_type), "tp", 2)
    ffn_scatter = Scatter(
        [
            contract_rows(second_in, d_gate_up).astype(half_type),
            contract_rows(cot_all, hidden).astype(half_type),
        ],
    )

    d_after, d_mix = call_kernel(
        after_back_body,
        [row_full, row_half],
        [],
        order,
        after_mix,
        cot_mine,
        *d_second,
        gain_two,
        deps=ffn_scatter.arrivals,
    )
    ffn_scatter.step(3)
    d_mix_all = gather_pieces(d_mix, *ffn_scatter.arrivals)

    ffn_scatter.step(2)
    d_gate, d_comb, sums_gain, d_mix_whole, d_att = call_kernel(
        gate_backward_body,
        [
            ((blocks, rows, channels), half_type),
            ((length, channels), full_type),
            ((8, channels), full_type),
            ((blocks, rows, width), half_type),
            head_half,
        ],
        [],
        at,
        gate_in,
        *d_mix_all,
        out_weight,
        combined,
        gains,
        deps=[ffn_scatter.ready],
        micros=4,
    )
    (d_attn,) = call_kernel(
        attend_backward_body,
        [((blocks, rows, 256), half_type)],
        [((length, 128), full_type), ((length, 128), full_type)],
        at,
        d_att,
        seg_col,
        seg_row,
        cosine,
        sine,
        query,
        keyk,
        valv,
        logs,
        micros=7,
    )
    out_terms = reduce_pieces(*row_products(filled_in[2], ffn_weight, deps=[sums_gain]))
    first_rows = first_in.reshape(length, width)
    gate_scatter = Scatter(
        [
            contract_rows(first_rows, d_gate.reshape(length, channels)).astype(half_type),
            contract_rows(first_rows, d_attn.reshape(length, 256)).astype(half_type),
            contract_rows(
                d_mix_whole.reshape(length, width), cat.reshape(length, channels + 128)
            ).astype(half_type),
        ],
    )
    ffn_scatter.step(1, d_attn)
    d_inputs_t, d_basis_b, d_basis_c, q_rows, mixed_t, sums_skip = call_kernel(
        functools.partial(ssd_backward_body, heads),
        [
            ((channels, length), full_type),
            ((STATE, length), full_type),
            ((length, STATE), full_type),
            ((8, length), full_type),
            ((channels, length), full_type),
            ((8, channels), full_type),
        ],
        [
            ((length, channels), half_type),
            ((channels, length), half_type),
            ((STATE, length), half_type),
        ],
        at,
        d_comb,
        scan_out,
        seg_col,
        seg_row,
        mixed,
        basis,
        inputs,
        time_rows,
        time_cols,
        deps=[ffn_scatter.ready, gate_scatter.ready, out_terms[3]],
        micros=12,
        limit=12,
    )
    gate_scatter.step(3, sums_skip)
    d_scan, sums_x, sums_bc, sums_rate = call_kernel(
        functools.partial(conv_backward_body, heads),
        [
            ((blocks, rows, channels + states + 128), half_type),
            ((8, channels), full_type),
            ((8, states), full_type),
            ((8, 128), full_type),
        ],
        [
            ((length + 8, channels), full_type),
            ((length + 8, states), full_type),
            ((length + 8, channels), full_type),
            ((length + 8, states), full_type),
            ((channels, length), full_type),
            ((8, length), full_type),
        ],
        at,
        raw,
        d_comb,
        keep_masks,
        taps_x,
        taps_bc,
        rates,
        gains,
        pre,
        time_rows,
        d_inputs_t,
        d_basis_b,
        d_basis_c,
        q_rows,
        mixed_t,
        deps=[gate_scatter.ready, out_terms[2], *ffn_scatter.arrivals],
        micros=7,
        limit=14,
    )
    smalls = join_columns([sums_bc, sums_x, sums_gain, sums_skip, sums_rate])
    scan_scatter = Scatter(
        [
            contract_rows(
                first_rows, d_scan.reshape(length, channels + states + 128)
            ).astype(half_type)
        ],
        extra=smalls,
    )
    keep, give, token = call_kernel(
        first_back_body,
        [
            ((2 * rows, width), full_type),
            ((2 * rows, width), half_type),
            ((8, 128), full_type),
        ],
        [],
        x_core,
        d_gate,
        d_attn,
        d_scan,
        late_weight,
        weight,
        deps=[*scan_scatter.arrivals, *gate_scatter.arrivals],
        micros=4,
    )
    d_first = reduce_pieces(keep, give)
    scan_scatter.step(3, token)
    gate_scatter.step(2, d_first[3])
    scan_scatter.step(2, d_first[3])
    gate_scatter.step(1)
    scan_scatter.step(1, d_first[2])
    scan_ready = scan_scatter.ready
    sum_gate, sum_up, sum_down, ffn_rows = ffn_scatter.total(
        (
            (0, hidden_local, False),
            (hidden_local, hidden_local, False),
            (2 * hidden_local, hidden_local, True),
        ),
        ((0, 0, hidden_local), (hidden_local, 0, hidden_local)),
        w_gate,
        w_up,
        deps=[d_first[2]],
    )
    (grad_tokens,) = call_kernel(
        token_back_body,
        [row_full],
        [],
        order,
        tok_rows,
        d_after,
        *d_first[:3],
        gain_one,
        deps=[scan_ready],
    )

    sum_z, sum_mixer_out, sum_attn_out, sum_query, sum_keyval, gate_rows = gate_scatter.total(
        (
            (0, channels, False),
            (channels + 256, channels, True),
            (2 * channels + 256, 128, True),
            (channels, 128, False),
            (channels + 128, 128, False),
        ),
        ((0, 0, channels), (channels, 0, 128), (channels + 128, 0, 128)),
        w_z,
        w_query,
        shared_shard,
    )
    sum_x, sum_bc, sum_step, scan_rows, flat = scan_scatter.total(
        ((0, channels, False), (channels, states, False), (channels + states, heads, False)),
        ((0, 0, channels), (channels, 128, states), (channels + states, 0, heads)),
        w_x,
        shared_shard,
        w_dt,
    )
    keep, give = call_kernel(
        functools.partial(shared_sums_body, conv_rows),
        [((2 * row_count, states + 256), full_type)] * 2,
        [],
        jnp.concatenate([at, lax.axis_index("fsdp").astype(jnp.int32).reshape(1)]),
        sum_bc,
        sum_keyval,
        gate_rows,
        scan_rows,
        ffn_rows,
        flat,
        deps=[grad_tokens],
        micros=1,
    )
    near = flip(give, "tp", 1)
    far = flip(keep[row_count:] + near[row_count:], "tp", 2)
    grad_bc, grad_keyval, gain_sums = call_kernel(
        shared_total_body,
        [
            ((row_count, states), full_type),
            ((row_count, 256), full_type),
            ((row_count, 128), full_type),
        ],
        [],
        at,
        keep,
        near,
        far,
        jnp.pad(jnp.stack([norm_gain, ffn_gain], 1), ((0, 0), (0, 126)), constant_values=1.0),
        micros=1,
    )
    sum_gain_one, sum_gain_two = gain_sums[:, 0], gain_sums[:, 1]
    sum_conv, sum_bias = gain_sums[:conv_rows, 8:12], gain_sums[:conv_rows, 12]

    (layer_out,) = call_kernel(
        output_body,
        [row_half],
        [],
        order,
        after_mix,
        *out_terms[:3],
        deps=[d_first[3]],
    )
    x_sums = flat[:, states : states + channels]
    mixer_sums = flat[0, states + channels : states + 2 * channels]
    skip_sums = flat[0, states + 2 * channels : states + 3 * channels]
    rate_sums = flat[:, states + 3 * channels :]
    return (
        layer_out,
        grad_tokens,
        sum_gain_one,
        sum_z,
        sum_x,
        grad_bc,
        sum_step,
        x_sums[:4].T,
        x_sums[4],
        sum_conv,
        sum_bias,
        rate_sums[:heads, 0],
        rate_sums[:heads, 1],
        skip_sums.reshape(heads, channels // heads).sum(axis=1),
        mixer_sums,
        sum_mixer_out,
        sum_query,
        grad_keyval,
        sum_attn_out,
        sum_gain_two,
        sum_gate,
        sum_up,
        sum_down,
    )


def solution(mesh):
    placed = (
        P(("fsdp", "tp"), None),
        P("fsdp"),
        P(("fsdp", "tp"), None),
        P(("fsdp", "tp")),
        P("fsdp", "tp"),
        P("fsdp", "tp"),
        P(("fsdp", "tp"), None),
        P("fsdp", "tp"),
        P("tp", None),
        P("tp"),
        P(("fsdp", "tp"), None),
        P(("fsdp", "tp")),
        P("tp"),
        P("tp"),
        P("tp"),
        P("tp"),
        P("tp", "fsdp"),
        P("fsdp", "tp"),
        P(("fsdp", "tp"), None),
        P("tp", "fsdp"),
        P(("fsdp", "tp")),
        P("fsdp", "tp"),
        P("fsdp", "tp"),
        P("tp", "fsdp"),
    )
    return jax.shard_map(
        shards,
        mesh=mesh,
        in_specs=placed,
        out_specs=(
            P(("fsdp", "tp"), None),
            P(("fsdp", "tp"), None),
            P(("fsdp", "tp")),
            P("fsdp", "tp"),
            P("fsdp", "tp"),
            P(("fsdp", "tp"), None),
            P("fsdp", "tp"),
            P("tp", None),
            P("tp"),
            P(("fsdp", "tp"), None),
            P(("fsdp", "tp")),
            P("tp"),
            P("tp"),
            P("tp"),
            P("tp"),
            P("tp", "fsdp"),
            P("fsdp", "tp"),
            P(("fsdp", "tp"), None),
            P("tp", "fsdp"),
            P(("fsdp", "tp")),
            P("fsdp", "tp"),
            P("fsdp", "tp"),
            P("tp", "fsdp"),
        ),
        check_vma=False,
    )
```

```python
import functools

import jax
import jax.numpy as jnp
from jax import lax
from jax.experimental import pallas as pl
from jax.experimental.pallas import tpu as pltpu
from jax.sharding import PartitionSpec as P

STATE = 128
CONV = 4
HEADS = 8
KV_HEADS = 2
HEAD = 64

EPS = 1e-06
ROPE_BASE = 10000.0
NEG_FILL = -1e30
LOG2_E = 1.4426950408889634


def contract_rows(left_side, right_side):
    return lax.dot_general(
        left_side, right_side, (((0,), (0,)), ((), ())), preferred_element_type=jnp.float32
    )


def contract_cols(left_side, right_side):
    return lax.dot_general(
        left_side, right_side, (((1,), (1,)), ((), ())), preferred_element_type=jnp.float32
    )


def split_cols(matrix, widths):
    pieces = []
    begin_at = 0
    for part_width in widths:
        pieces.append(matrix[:, begin_at : begin_at + part_width])
        begin_at = begin_at + part_width
    return pieces


def flip(values, axis, mask):
    size = lax.axis_size(axis)
    return lax.ppermute(values, axis, [(i, i ^ mask) for i in range(size)])


def ring(values, step):
    return lax.ppermute(values, "fsdp", [(i, (i + 2 * step) % 8) for i in range(8)])


def staged():
    return lax.axis_size("fsdp") == 8


def place_bits():
    index = lax.axis_index("tp")
    return index // 2, index % 2


def gather_pieces(rows_in, *deps):
    far = flip(rows_in, "tp", 2)
    near = flip(rows_in, "tp", 1)
    cross = flip(after(far, *deps), "tp", 1)
    return rows_in, far, near, cross


def reduce_pieces(keep, give, *deps):
    half = keep.shape[0] // 2
    near = flip(give, "tp", 1)
    passed = after((keep[half:] + near[half:].astype(jnp.float32)).astype(jnp.bfloat16), *deps)
    far = flip(passed, "tp", 2)
    return keep, near, far, passed


def fsdp_place():
    index = lax.axis_index("fsdp")
    return index // 2, index % 2


def after(value, *deps):
    if not deps:
        return value

    def body(_, value_ref, out_ref):
        out_ref[...] = value_ref[...]

    return call_kernel(
        body, [(value.shape, value.dtype)], [], no_scalar(), value, deps=deps, micros=1, limit=8
    )[0]


def no_scalar():
    return jnp.zeros((1,), jnp.int32)


def fetch_blocks(grads, rows, places, held, sems):
    copies = []
    for k, (grad, here) in enumerate(zip(grads, held)):
        for n, (dy, dz) in enumerate(places):
            copies.append(
                pltpu.make_async_copy(
                    grad.at[pl.ds((dy * 4 + dz) * rows, rows)],
                    here.at[pl.ds(n * rows, rows)],
                    sems.at[k * len(places) + n],
                )
            )
    for copy in copies:
        copy.start()

    def blocks(n):
        for k in range(len(grads)):
            copies[k * len(places) + n].wait()
        return [here[n * rows : n * rows + rows] for here in held]

    return blocks


def store_side_by_side(values, out_ref):
    begin_at = 0
    for value in values:
        out_ref[:, begin_at : begin_at + value.shape[1]] = value.astype(out_ref.dtype)
        begin_at = begin_at + value.shape[1]


def add_arrivals(values, arrivals):
    sums, begin_at = [], 0
    for value in values:
        columns = slice(begin_at, begin_at + value.shape[1])
        total = value.astype(jnp.float32)
        for arrival in arrivals:
            total = total + arrival[:, columns].astype(jnp.float32)
        sums.append(total)
        begin_at = begin_at + value.shape[1]
    return sums


def put_extra(values, out_ref, rows):
    width = out_ref.shape[1]
    halves = jnp.concatenate([values[:, :width], values[:, width:]], axis=0)
    out_ref[rows : rows + 16] = halves.astype(out_ref.dtype)


def get_extra(ref, rows):
    values = ref[rows : rows + 16].astype(jnp.float32)
    return jnp.concatenate([values[:8], values[8:]], axis=1)


def first_block_body(count, rows, extra, _, *refs):
    extra_ref, refs = (refs[0], refs[1:]) if extra else (None, refs)
    grads, out_ref, held, sems = refs[:count], refs[count], refs[count + 1 : -1], refs[-1]
    blocks = fetch_blocks(grads, rows, [(1, 3)], held, sems)
    if extra:
        put_extra(extra_ref[...], out_ref, rows)
    store_side_by_side(blocks(0), out_ref.at[:rows])


def step_body(count, arriving, rows, dz, extra, _, *refs):
    extra_ref, refs = (refs[0], refs[1:]) if extra else (None, refs)
    arrivals, refs = refs[:arriving], refs[arriving:]
    grads, (send_ref, next_ref), refs = refs[:count], refs[count : count + 2], refs[count + 2 :]
    if extra:
        extra_out, refs = refs[0], refs[1:]
    blocks = fetch_blocks(grads, rows, [(1, dz - 1), (0, dz)], refs[:-1], refs[-1])
    if extra:
        came = get_extra(arrivals[-1], rows)
        total = extra_ref[...] + came
        extra_out[...] = total
        put_extra(total if arriving == 1 else came, send_ref, rows)
        next_ref[rows : rows + 16] = jnp.zeros((16, next_ref.shape[1]), next_ref.dtype)
    store_side_by_side(blocks(0), next_ref.at[:rows])
    sums = add_arrivals(blocks(1), [ref[:rows] for ref in arrivals])
    store_side_by_side(sums, send_ref.at[:rows])


def total_body(count, rows, columns, weighted, arriving, extra, _, *refs):
    size = len(weighted)
    extra_ref, refs = (refs[0], refs[1:]) if extra else (None, refs)
    arrivals, refs = refs[:arriving], refs[arriving:]
    grads, weights, refs = refs[:count], refs[count : count + size], refs[count + size :]
    outs, by_row_ref = refs[: len(columns)], refs[len(columns)]
    if extra:
        refs[len(columns) + 1][...] = extra_ref[...] + get_extra(arrivals[-1], rows)
    held, sems = refs[len(columns) + 1 + extra : -1], refs[-1]
    arrivals = [ref[:rows] for ref in arrivals]
    blocks = fetch_blocks(grads, rows, [(0, 0)], held[:count], sems)
    held = held[count:]
    copies = [
        pltpu.make_async_copy(weight, here, sems.at[count + k])
        for k, (weight, here) in enumerate(zip(weights, held))
    ]
    for copy in copies:
        copy.start()
    sums = add_arrivals(blocks(0), arrivals)
    total = jnp.concatenate(sums, axis=1) if len(sums) > 1 else sums[0]
    for (begin_at, width, turned), out_ref in zip(columns, outs):
        values = total[:, begin_at : begin_at + width]
        out_ref[...] = values.T if turned else values
    by_row = jnp.zeros((total.shape[0], 1), jnp.float32)
    for (begin_at, offset, width), copy, here in zip(weighted, copies, held):
        copy.wait()
        values = total[:, begin_at : begin_at + width]
        rounded = here[:, offset : offset + width].astype(jnp.bfloat16).astype(jnp.float32)
        by_row = by_row + jnp.sum(values * rounded, axis=1, keepdims=True)
    by_row_ref[...] = jnp.broadcast_to(by_row, by_row_ref.shape)


class Scatter:
    def __init__(self, grads, *deps, extra=None):
        self.grads = grads
        self.rows = grads[0].shape[0] // 8
        self.width = sum(grad.shape[1] for grad in grads)
        self.arrivals = []
        self.ready = grads[0]
        self.extra = [] if extra is None else [extra]
        if staged():
            (first,) = call_kernel(
                functools.partial(first_block_body, len(grads), self.rows, len(self.extra)),
                [((self.rows + 16 * len(self.extra), self.width), jnp.bfloat16)],
                [((self.rows, grad.shape[1]), grad.dtype) for grad in grads],
                no_scalar(),
                *self.extra,
                *grads,
                deps=deps,
                micros=1,
                distant=len(grads),
                sems=len(grads),
            )
            self.ready = first
            self.arrivals = [flip(first, "fsdp", 1)]

    def step(self, dz, *deps):
        if not staged():
            return ()
        block = ((self.rows + 16 * len(self.extra), self.width), jnp.bfloat16)
        send, following, *self.extra = call_kernel(
            functools.partial(
                step_body, len(self.grads), len(self.arrivals), self.rows, dz, len(self.extra)
            ),
            [block, block] + [(extra.shape, extra.dtype) for extra in self.extra],
            [((2 * self.rows, grad.shape[1]), grad.dtype) for grad in self.grads],
            no_scalar(),
            *self.extra,
            *self.arrivals,
            *self.grads,
            deps=deps,
            micros=1,
            distant=len(self.grads),
            sems=2 * len(self.grads),
        )
        self.ready = send
        self.arrivals = [flip(following, "fsdp", 1), ring(send, 1)]
        return self.arrivals

    def total(self, columns, weighted, *weights, deps=()):
        extra = self.extra if staged() else []
        if staged():
            grads, rows = self.grads, self.rows
        else:
            grads = [
                lax.psum_scatter(
                    jnp.concatenate(self.grads, axis=1), "fsdp", scatter_dimension=0, tiled=True
                )
            ]
            rows = grads[0].shape[0]
        shapes = [
            ((width, rows) if turned else (rows, width), jnp.float32)
            for _, width, turned in columns
        ]
        outs = call_kernel(
            functools.partial(
                total_body, len(grads), rows, columns, weighted, len(self.arrivals), len(extra)
            ),
            shapes + [((rows, 128), jnp.float32)] + [(item.shape, item.dtype) for item in extra],
            [((rows, grad.shape[1]), grad.dtype) for grad in grads]
            + [(weight.shape, weight.dtype) for weight in weights],
            no_scalar(),
            *extra,
            *self.arrivals,
            *grads,
            *weights,
            deps=deps,
            micros=1,
            distant=len(grads) + len(weights),
            sems=len(grads) + len(weights),
        )
        if not staged():
            outs = list(outs) + [lax.psum(item, "fsdp") for item in self.extra]
        return outs


def join_columns(arrays, *deps):
    def body(_, *refs):
        store_side_by_side([ref[...] for ref in refs[:-1]], refs[-1])

    rows, width = arrays[0].shape[0], sum(array.shape[1] for array in arrays)
    outs = [((rows, width), arrays[0].dtype)]
    return call_kernel(body, outs, [], no_scalar(), *arrays, deps=deps, micros=1, limit=8)[0]


class Gather:
    def __init__(self, shard):
        self.shard = self.ready = shard
        if staged():
            self.along, self.across = [shard], []
        self.arrivals = []

    def step(self, *deps):
        if not staged():
            return ()
        held = self.ready = after(self.along[-1], *self.across[-1:], *deps)
        if len(self.along) < 4:
            self.along.append(ring(held, 1))
        self.across.append(flip(held, "fsdp", 1))
        self.arrivals = [self.along[-1], self.across[-1]]
        return self.arrivals

    def parts(self):
        if not staged():
            return [lax.all_gather(self.shard, "fsdp", axis=0, tiled=True)]
        return [blocks[-dz % 4] for blocks in (self.along, self.across) for dz in range(4)]


def sum_fsdp(values):
    if not staged():
        return lax.psum(values, "fsdp")
    for mask in (1, 2, 6):
        values = values + flip(values, "fsdp", mask)
    return values


def sum_tp(values):
    for mask in (1, 2):
        values = values + flip(values, "tp", mask)
    return values


def feature_order():
    if not staged():
        return jnp.arange(8, dtype=jnp.int32)
    z_at, y_at = fsdp_place()
    steps = jnp.arange(8, dtype=jnp.int32)
    return (z_at + steps % 4) % 4 * 2 + (y_at ^ (steps // 4))


CHUNK = 128


def row_chunks(rows, body, carry=0):
    def step(k, carry):
        return body(pl.ds(pl.multiple_of(k * CHUNK, CHUNK), CHUNK), carry)

    return lax.fori_loop(0, rows // CHUNK, step, carry)


def front_body(order_ref, tok_ref, cot_ref, normed_ref, tok_rel, cot_rel):
    rows_all, width = tok_ref.shape
    block = width // 8

    def chunk(rows, carry):
        for b in range(8):
            there = pl.ds(pl.multiple_of(order_ref[b] * block, block), block)
            here = slice(b * block, b * block + block)
            tok_rel[rows, here] = tok_ref[rows, there]
            cot_rel[rows, here] = cot_ref[rows, there]
        values = tok_rel[rows].astype(jnp.float32)
        normed = values * lax.rsqrt(jnp.mean(values * values, axis=-1, keepdims=True) + EPS)
        normed_ref[rows] = normed.astype(jnp.bfloat16)
        return carry

    row_chunks(rows_all, chunk)


def summed_rows(rows, keep_ref, near_ref, far_ref):
    return (
        keep_ref[rows] + near_ref[rows].astype(jnp.float32) + far_ref[rows].astype(jnp.float32)
    )


def mixed_body(_, tok_ref, keep_ref, near_ref, far_ref, gain_ref, after_ref, second_ref):
    def chunk(rows, carry):
        after = tok_ref[rows].astype(jnp.float32) + summed_rows(rows, keep_ref, near_ref, far_ref)
        after_ref[rows] = after
        normed = after * lax.rsqrt(jnp.mean(after * after, axis=-1, keepdims=True) + EPS)
        second_ref[rows] = (normed * gain_ref[...]).astype(jnp.bfloat16)
        return carry

    row_chunks(tok_ref.shape[0], chunk)


def output_body(order_ref, after_ref, keep_ref, near_ref, far_ref, out_ref):
    block = after_ref.shape[1] // 8

    def chunk(rows, carry):
        values = after_ref[rows] + summed_rows(rows, keep_ref, near_ref, far_ref)
        values = values.astype(jnp.bfloat16)
        for b in range(8):
            there = pl.ds(pl.multiple_of(order_ref[b] * block, block), block)
            out_ref[rows, there] = values[:, b * block : b * block + block]
        return carry

    row_chunks(after_ref.shape[0], chunk)


def norm_back(values, d_out, gain):
    inverse = lax.rsqrt(jnp.mean(values * values, axis=-1, keepdims=True) + EPS)
    normed = values * inverse
    scaled = d_out * gain
    return inverse * (scaled - normed * jnp.mean(scaled * normed, axis=-1, keepdims=True))


def after_back_body(
    _, after_ref, cot_ref, keep_ref, near_ref, far_ref, gain_ref, d_after_ref, d_mix_ref
):
    def chunk(rows, carry):
        d_second = summed_rows(rows, keep_ref, near_ref, far_ref)
        d_after = cot_ref[rows].astype(jnp.float32) + norm_back(
            after_ref[rows], d_second, gain_ref[...]
        )
        d_after_ref[rows] = d_after
        d_mix_ref[rows] = d_after.astype(jnp.bfloat16)
        return carry

    row_chunks(after_ref.shape[0], chunk)


def token_back_body(
    order_ref, tok_ref, d_after_ref, keep_ref, near_ref, far_ref, gain_ref, out_ref
):
    block = tok_ref.shape[1] // 8

    def chunk(rows, carry):
        d_first = summed_rows(rows, keep_ref, near_ref, far_ref)
        values = d_after_ref[rows] + norm_back(
            tok_ref[rows].astype(jnp.float32), d_first, gain_ref[...]
        )
        for b in range(8):
            there = pl.ds(pl.multiple_of(order_ref[b] * block, block), block)
            out_ref[rows, there] = values[:, b * block : b * block + block]
        return carry

    row_chunks(tok_ref.shape[0], chunk)


def piece_at(block, at):
    apart = block ^ at
    return (apart & 1) * 2 + (apart >> 1)


def head_lanes(columns, first, lanes):
    rows = columns.shape[0]
    even = jnp.broadcast_to(columns[:, first : first + 1], (rows, 128))
    odd = jnp.broadcast_to(columns[:, first + 1 : first + 2], (rows, 128))
    return jnp.where(lanes < HEAD, even, odd)


def lane_ids(rows, cols):
    return lax.broadcasted_iota(jnp.int32, (rows, cols), 1)


def row_ids(rows, cols):
    return lax.broadcasted_iota(jnp.int32, (rows, cols), 0)


def dot_nt(left_side, right_side, **kw):
    return lax.dot_general(
        left_side, right_side, (((1,), (1,)), ((), ())), preferred_element_type=jnp.float32, **kw
    )


def dot_nn(left_side, right_side):
    return jnp.dot(left_side, right_side, preferred_element_type=jnp.float32)


def dot_tn(left_side, right_side):
    return lax.dot_general(
        left_side, right_side, (((0,), (0,)), ((), ())), preferred_element_type=jnp.float32
    )


def conv_window(window, taps, offset, keep):
    rows = window.shape[0] - 8
    summed = window[8:] * taps[CONV - 1 : CONV] + offset
    for lag in range(1, CONV):
        summed = summed + window[8 - lag : 8 - lag + rows] * keep[:, lag : lag + 1] * (
            taps[CONV - 1 - lag : CONV - lag]
        )
    return summed


def log_one_plus(values):
    ratio = values / (2.0 + values)
    square = ratio * ratio
    series = jnp.full_like(values, 1.0 / 15.0)
    for odd in (13, 11, 9, 7, 5, 3, 1):
        series = series * square + 1.0 / odd
    return 2.0 * ratio * series


def scan_lanes(values, reverse):
    length = values.shape[1]
    lanes = lane_ids(*values.shape)
    step = 1
    while step < length:
        if reverse:
            moved = jnp.where(lanes < length - step, pltpu.roll(values, length - step, 1), 0.0)
        else:
            moved = jnp.where(lanes >= step, pltpu.roll(values, step, 1), 0.0)
        values = values + moved
        step = step * 2
    return values


def pair_mask(seg_col, seg_row, at_t, at_s):
    size = seg_col.shape[0]
    rows = row_ids(size, size) + at_t * size
    cols = lane_ids(size, size) + at_s * size
    return (seg_col == seg_row) & (rows >= cols)


def swap_halves(values, lanes):
    half = HEAD // 2
    return jnp.where(
        lanes % HEAD < half, pltpu.roll(values, 128 - half, 1), pltpu.roll(values, half, 1)
    )


def ssd_forward_body(
    heads,
    at_ref,
    proj_ref,
    segc_ref,
    segr_ref,
    keep_ref,
    taps_ref,
    tapb_ref,
    rate_ref,
    scan_ref,
    mixed_ref,
    raw_ref,
    pre_ref,
    basis_ref,
    inputs_ref,
    rows_ref,
    cols_ref,
    xpad,
    bpad,
    dtr,
):
    blocks, size = proj_ref.shape[0], proj_ref.shape[1]
    channels = mixed_ref.shape[1]
    states = basis_ref.shape[1]
    tail = proj_ref.shape[2] - states - 128
    at = at_ref[0]
    xpad[0:8] = jnp.zeros((8, channels), jnp.float32)
    bpad[0:8] = jnp.zeros((8, states), jnp.float32)

    def load(a, carry):
        rows = pl.ds(pl.multiple_of(a * size + 8, 8), size)
        block = piece_at(a, at)
        xpad[rows] = proj_ref[block, :, :channels]
        bpad[rows] = proj_ref[block, :, tail : tail + states]
        here = pl.ds(pl.multiple_of(a * size, size), size)
        raw_ref[here, :channels] = proj_ref[block, :, :channels].astype(jnp.bfloat16)
        raw_ref[here, channels:] = proj_ref[block, :, tail : tail + states].astype(jnp.bfloat16)
        steps = proj_ref[block, :, tail + states :]
        dtr[:, pl.ds(pl.multiple_of(a * size, size), size)] = steps.T[0:8]
        return carry

    lax.fori_loop(0, blocks, load, 0)
    raw = dtr[...] + rate_ref[:, 0:1]
    step_size = jnp.maximum(raw, 0.0) + log_one_plus(jnp.exp(-jnp.abs(raw)))
    log_rate = -step_size * jnp.exp(rate_ref[:, 1:2])
    cum = scan_lanes(log_rate, False) * LOG2_E
    length = raw.shape[1]
    rows_ref[0:8] = step_size
    rows_ref[8:16] = cum
    rows_ref[16:24] = raw
    cols_ref[...] = jnp.concatenate(
        [step_size, cum, jnp.zeros((112, length), jnp.float32)], axis=0
    ).T
    lanes = lane_ids(size, 128)

    def prepare_block(a, carry):
        window = pl.ds(pl.multiple_of(a * size, size), size + 8)
        rows = pl.ds(pl.multiple_of(a * size, size), size)
        keep = keep_ref[rows]
        columns = cols_ref[rows]
        bpre = conv_window(bpad[window], tapb_ref[0:4], tapb_ref[4:5], keep)
        pre_ref[rows, channels:] = bpre.astype(jnp.bfloat16)
        basis_ref[rows] = (bpre * jax.nn.sigmoid(bpre)).astype(jnp.bfloat16)
        for pair in range(channels // 128):
            span = slice(pair * 128, pair * 128 + 128)
            xpre = conv_window(xpad[window, span], taps_ref[0:4, span], taps_ref[4:5, span], keep)
            pre_ref[rows, span] = xpre.astype(jnp.bfloat16)
            mixed = (xpre * jax.nn.sigmoid(xpre)).astype(jnp.bfloat16)
            mixed_ref[rows, span] = mixed
            steps = head_lanes(columns, 2 * pair, lanes)
            inputs_ref[rows, span] = (steps * mixed.astype(jnp.float32)).astype(jnp.bfloat16)
        return carry

    lax.fori_loop(0, blocks, prepare_block, 0)
    state = states // 2

    def row_block(i, carry):
        rows_t = pl.ds(pl.multiple_of(i * size, size), size)
        basis_c = basis_ref[rows_t, state:]
        seg_t = segc_ref[rows_t]
        columns = cols_ref[rows_t]

        def pair_block(j, totals):
            rows_s = pl.ds(pl.multiple_of(j * size, size), size)
            allowed = pair_mask(seg_t, segr_ref[:, rows_s], i, j)
            gram = jnp.where(allowed, dot_nt(basis_c, basis_ref[rows_s, :state]), 0.0)
            cum_s = rows_ref[8:16, rows_s]
            fresh = []
            for pair in range(heads // 2):
                values = inputs_ref[rows_s, pair * 128 : pair * 128 + 128]
                outs = []
                for h in (2 * pair, 2 * pair + 1):
                    spread = columns[:, 8 + h : 9 + h] - cum_s[h : h + 1]
                    weights = (gram * jnp.exp2(jnp.minimum(spread, 0.0))).astype(jnp.bfloat16)
                    outs.append(dot_nn(weights, values))
                fresh.append(totals[pair] + jnp.where(lanes < HEAD, outs[0], outs[1]))
            return tuple(fresh)

        zero = jnp.zeros((size, 128), jnp.float32)
        totals = lax.fori_loop(0, i + 1, pair_block, (zero,) * (heads // 2))
        for pair in range(heads // 2):
            scan_ref[rows_t, pair * 128 : pair * 128 + 128] = totals[pair]
        return carry

    lax.fori_loop(0, blocks, row_block, 0)


def attend_forward_body(
    count,
    at_ref,
    first_ref,
    proj_ref,
    scan_ref,
    mixed_ref,
    segc_ref,
    segr_ref,
    cos_ref,
    sin_ref,
    gain_ref,
    *refs,
):
    parts = refs[:count]
    cat_ref, gate_ref, combined_ref, query_ref, keyk_ref, valv_ref, logs_ref = refs[count:-2]
    weight_ref, out_weight_ref = refs[-2:]
    wide = weight_ref.shape[1]
    stack_rows([part.at[:, :wide] for part in parts], weight_ref)
    stack_rows([part.at[:, wide:] for part in parts], out_weight_ref)
    blocks, size = proj_ref.shape[0], proj_ref.shape[1]
    channels = scan_ref.shape[1]
    at = at_ref[0]
    lanes = lane_ids(size, 128)
    half_type = jnp.bfloat16

    def finish_block(a, carry):
        rows = pl.ds(pl.multiple_of(a * size, size), size)
        block = piece_at(a, at)
        mine = dot_nn(first_ref[block], weight_ref[...])
        gate, query = mine[:, :channels], mine[:, channels:]
        gate_ref[block] = gate.astype(half_type)
        combined = scan_ref[rows] + gain_ref[1:2] * mixed_ref[rows].astype(jnp.float32)
        combined_ref[rows] = combined.astype(half_type)
        gated = combined * (gate * jax.nn.sigmoid(gate))
        inverse = lax.rsqrt(jnp.mean(gated * gated, axis=-1, keepdims=True) + EPS)
        cat_ref[block, :, :channels] = (gated * inverse * gain_ref[0:1]).astype(half_type)
        cosine, sine = cos_ref[rows], sin_ref[rows]
        query_ref[rows] = (query * cosine + swap_halves(query, lanes) * sine).astype(half_type)
        keyval = proj_ref[block, :, channels : channels + 128]
        keyval = keyval * jnp.where(lanes < HEAD, cosine, 1.0) + swap_halves(
            keyval, lanes
        ) * jnp.where(lanes < HEAD, sine, 0.0)
        moved = pltpu.roll(keyval, HEAD, 1)
        keyk_ref[rows] = jnp.where(lanes < HEAD, keyval, moved).astype(half_type)
        valv_ref[rows] = jnp.where(lanes < HEAD, moved, keyval).astype(half_type)
        return carry

    lax.fori_loop(0, blocks, finish_block, 0)
    for i in range(blocks):
        width = (i + 1) * size
        rows = slice(i * size, width)
        query = query_ref[rows] * HEAD ** (-0.5)
        places = row_ids(size, width) + i * size
        allowed = (segc_ref[rows] == segr_ref[:, :width]) & (places >= lane_ids(size, width))
        outs, logs = [], []
        for h in range(2):
            mine = (lanes < HEAD) if h == 0 else (lanes >= HEAD)
            masked = jnp.where(mine, query, jnp.zeros_like(query))
            scores = dot_nt(masked, keyk_ref[:width])
            scores = jnp.where(allowed, scores, NEG_FILL)
            top = jnp.max(scores, axis=-1, keepdims=True)
            powers = jnp.exp(scores - top)
            total = jnp.sum(powers, axis=-1, keepdims=True)
            outs.append(dot_nn(powers.astype(half_type), valv_ref[:width]) / total)
            logs.append(top + jnp.log(total))
        cat_ref[piece_at(i, at), :, channels:] = jnp.where(lanes < HEAD, outs[0], outs[1]).astype(half_type)
        logs_ref[rows] = jnp.where(lanes < HEAD, logs[0], logs[1])


def gate_backward_body(
    at_ref,
    gate_ref,
    mine_ref,
    far_ref,
    near_ref,
    cross_ref,
    weight_ref,
    combined_ref,
    gain_ref,
    dgate_ref,
    dcomb_ref,
    small_ref,
    dmix_ref,
    datt_ref,
):
    blocks, size = gate_ref.shape[0], gate_ref.shape[1]
    channels = combined_ref.shape[1]
    at = at_ref[0]
    half_type = jnp.bfloat16
    for p, piece in enumerate((mine_ref, far_ref, near_ref, cross_ref)):
        dmix_ref[p] = piece[...]

    def finish_block(a, carry):
        grad_gain = carry
        rows = pl.ds(pl.multiple_of(a * size, size), size)
        block = piece_at(a, at)
        d_cat = dot_nn(dmix_ref[block], weight_ref[...])
        datt_ref[rows] = d_cat[:, channels:].astype(half_type)
        gate = gate_ref[block].astype(jnp.float32)
        sig = jax.nn.sigmoid(gate)
        act = gate * sig
        combined = combined_ref[rows].astype(jnp.float32)
        gated = combined * act
        inverse = lax.rsqrt(jnp.mean(gated * gated, axis=-1, keepdims=True) + EPS)
        normed = gated * inverse
        d_out = d_cat[:, :channels]
        grad_gain = grad_gain + jnp.sum(d_out * normed, axis=0, keepdims=True)
        scaled = d_out * gain_ref[0:1]
        d_gated = inverse * (scaled - normed * jnp.mean(scaled * normed, axis=-1, keepdims=True))
        d_comb = d_gated * act
        dcomb_ref[rows] = d_comb
        d_gate = d_gated * combined * sig * (1.0 + gate * (1.0 - sig))
        dgate_ref[block] = d_gate.astype(half_type)
        return grad_gain

    grad_gain = lax.fori_loop(0, blocks, finish_block, jnp.zeros((1, channels), jnp.float32))
    small_ref[...] = jnp.broadcast_to(grad_gain, small_ref.shape)


def attend_backward_body(
    at_ref,
    datt_ref,
    segc_ref,
    segr_ref,
    cos_ref,
    sin_ref,
    query_ref,
    keyk_ref,
    valv_ref,
    logs_ref,
    dproj_ref,
    dkey,
    dval,
):
    blocks, size = dproj_ref.shape[0], dproj_ref.shape[1]
    at = at_ref[0]
    lanes = lane_ids(size, 128)
    half_type = jnp.bfloat16
    dkey[...] = jnp.zeros_like(dkey)
    dval[...] = jnp.zeros_like(dval)
    for i in range(blocks):
        width = (i + 1) * size
        rows = slice(i * size, width)
        query = query_ref[rows] * HEAD ** (-0.5)
        d_att = datt_ref[rows]
        logs = logs_ref[rows]
        places = row_ids(size, width) + i * size
        allowed = (segc_ref[rows] == segr_ref[:, :width]) & (places >= lane_ids(size, width))
        outs = []
        for h in range(2):
            mine = (lanes < HEAD) if h == 0 else (lanes >= HEAD)
            masked = jnp.where(mine, query, jnp.zeros_like(query))
            d_masked = jnp.where(mine, d_att, jnp.zeros_like(d_att))
            scores = dot_nt(masked, keyk_ref[:width])
            scores = jnp.where(allowed, scores, NEG_FILL)
            probs = jnp.exp(scores - logs[:, h * HEAD : h * HEAD + 1])
            d_probs = dot_nt(d_masked, valv_ref[:width])
            mean = jnp.sum(probs * d_probs, axis=-1, keepdims=True)
            d_scores = (probs * (d_probs - mean)).astype(half_type)
            outs.append(dot_nn(d_scores, keyk_ref[:width]))
            dkey[:width] += dot_tn(d_scores, masked)
            dval[:width] += dot_tn(probs.astype(half_type), d_masked)
        d_query = jnp.where(lanes < HEAD, outs[0], outs[1]) * HEAD ** (-0.5)
        cosine, sine = cos_ref[rows], sin_ref[rows]
        d_query = d_query * cosine - swap_halves(d_query, lanes) * sine
        dproj_ref[piece_at(i, at), :, :128] = d_query.astype(half_type)

    def key_block(a, carry):
        rows = pl.ds(pl.multiple_of(a * size, size), size)
        d_key, d_val = dkey[rows], dval[rows]
        d_key = d_key + pltpu.roll(d_key, HEAD, 1)
        d_val = d_val + pltpu.roll(d_val, HEAD, 1)
        d_key = d_key * cos_ref[rows] - swap_halves(d_key, lanes) * sin_ref[rows]
        dproj_ref[piece_at(a, at), :, 128:] = jnp.where(lanes < HEAD, d_key, d_val).astype(
            half_type
        )
        return carry

    lax.fori_loop(0, blocks, key_block, 0)


def silu_slope(values):
    sig = jax.nn.sigmoid(values)
    return sig * (1.0 + values * (1.0 - sig))


def conv_back(d_window, keep_window, taps):
    rows = d_window.shape[0] - 8
    summed = d_window[:rows] * taps[CONV - 1 : CONV]
    for lag in range(1, CONV):
        moved = d_window * keep_window[:, lag : lag + 1]
        summed = summed + moved[lag : lag + rows] * taps[CONV - 1 - lag : CONV - lag]
    return summed


def conv_grads(d_pre, window, keep):
    rows = d_pre.shape[0]
    sums = []
    for tap in range(CONV):
        lag = CONV - 1 - tap
        moved = window[8 - lag : 8 - lag + rows]
        if lag:
            moved = moved * keep[:, lag : lag + 1]
        sums.append(jnp.sum(d_pre * moved, axis=0, keepdims=True))
    sums.append(jnp.sum(d_pre, axis=0, keepdims=True))
    sums.append(jnp.zeros((8 - len(sums), d_pre.shape[1]), jnp.float32))
    return jnp.concatenate(sums, axis=0)


def ssd_backward_body(
    heads,
    at_ref,
    dcomb_ref,
    scan_ref,
    segc_ref,
    segr_ref,
    mixed_ref,
    basis_ref,
    inputs_ref,
    rows_ref,
    cols_ref,
    dint,
    dbt,
    dcb,
    qrow,
    mixt,
    skip_ref,
    dsc,
    dst,
    cbt,
):
    length, channels = scan_ref.shape
    state = dbt.shape[0]
    size = length // 4
    blocks = 4
    half_type = jnp.bfloat16
    lanes = lane_ids(size, 128)
    dint[...] = jnp.zeros_like(dint)
    dbt[...] = jnp.zeros_like(dbt)
    head_of = jnp.where(
        lane_ids(8, channels) // HEAD == row_ids(8, channels), 1.0, 0.0
    ).astype(jnp.float32)

    def load(a, carry):
        rows = pl.ds(pl.multiple_of(a * size, size), size)
        d_comb = dcomb_ref[rows]
        d_scan = d_comb.astype(half_type)
        dsc[rows] = d_scan
        d_full = d_scan.astype(jnp.float32)
        dst[:, rows] = d_full.T.astype(half_type)
        cbt[:, rows] = basis_ref[rows, state:].astype(jnp.float32).T.astype(half_type)
        mixed = mixed_ref[rows].astype(jnp.float32)
        mixt[:, rows] = mixed.T
        qrow[:, rows] = dot_nt(head_of, d_full * scan_ref[rows], precision=lax.Precision.HIGHEST)
        return carry + jnp.sum(d_comb * mixed, axis=0, keepdims=True)

    skips = lax.fori_loop(0, blocks, load, jnp.zeros((1, channels), jnp.float32))
    skip_ref[...] = jnp.broadcast_to(skips, skip_ref.shape)

    def row_block(i, carry):
        rows_t = pl.ds(pl.multiple_of(i * size, size), size)
        basis_c = basis_ref[rows_t, state:]
        seg_t = segc_ref[rows_t]
        columns = cols_ref[rows_t]

        def pair_block(j, total):
            rows_s = pl.ds(pl.multiple_of(j * size, size), size)
            allowed = pair_mask(seg_t, segr_ref[:, rows_s], i, j)
            gram = jnp.where(allowed, dot_nt(basis_c, basis_ref[rows_s, :state]), 0.0)
            cum_s = rows_ref[8:16, rows_s]
            d_gram = jnp.zeros((size, size), jnp.float32)
            for pair in range(heads // 2):
                span = slice(pair * 128, pair * 128 + 128)
                values = inputs_ref[rows_s, span]
                d_scan = dsc[rows_t, span]
                for h in (2 * pair, 2 * pair + 1):
                    mine = (lanes < HEAD) if h % 2 == 0 else (lanes >= HEAD)
                    spread = columns[:, 8 + h : 9 + h] - cum_s[h : h + 1]
                    decay = jnp.exp2(jnp.minimum(spread, 0.0))
                    weights = (gram * decay).astype(half_type)
                    d_weights = dot_nt(jnp.where(mine, d_scan, jnp.zeros_like(d_scan)), values)
                    d_gram = d_gram + d_weights * decay
                    chans = slice(h * HEAD, h * HEAD + HEAD)
                    dint[chans, rows_s] += dot_nn(dst[chans, rows_t], weights)
            d_gram = jnp.where(allowed, d_gram, 0.0).astype(half_type)
            dbt[:, rows_s] += dot_nn(cbt[:, rows_t], d_gram)
            return total + dot_nn(d_gram, basis_ref[rows_s, :state])

        dcb[rows_t] = lax.fori_loop(0, i + 1, pair_block, jnp.zeros((size, state), jnp.float32))
        return carry

    lax.fori_loop(0, blocks, row_block, 0)


def conv_backward_body(
    heads,
    at_ref,
    raw_ref,
    dcomb_ref,
    keep_ref,
    taps_ref,
    tapb_ref,
    rate_ref,
    gain_ref,
    pre_ref,
    rows_ref,
    dint_ref,
    dbt,
    dcb,
    qrow_ref,
    mixt,
    dproj_ref,
    gradx_ref,
    gradb_ref,
    grads_ref,
    xpad,
    bpad,
    dpx,
    dpb,
    dint,
    qrow,
):
    blocks, size = dproj_ref.shape[0], dproj_ref.shape[1]
    channels = dcomb_ref.shape[1]
    states = pre_ref.shape[1] - channels
    length = blocks * size
    at = at_ref[0]
    half_type = jnp.bfloat16
    xpad[0:8] = jnp.zeros((8, channels), jnp.float32)
    bpad[0:8] = jnp.zeros((8, states), jnp.float32)
    dpx[length : length + 8] = jnp.zeros((8, channels), jnp.float32)
    dpb[length : length + 8] = jnp.zeros((8, states), jnp.float32)

    def load(a, carry):
        padded = pl.ds(pl.multiple_of(a * size + 8, 8), size)
        rows = pl.ds(pl.multiple_of(a * size, size), size)
        xpad[padded] = raw_ref[rows, :channels].astype(jnp.float32)
        bpad[padded] = raw_ref[rows, channels:].astype(jnp.float32)
        return carry

    lax.fori_loop(0, blocks, load, 0)
    step_size = rows_ref[0:8]
    raw = rows_ref[16:24]
    d_step, col_part = [], []
    for h in range(heads):
        chans = slice(h * HEAD, h * HEAD + HEAD)
        d_inputs = dint_ref[chans]
        mixed = mixt[chans]
        scaled = step_size[h : h + 1] * mixed
        d_step.append(jnp.sum(d_inputs * mixed, axis=0, keepdims=True))
        inputs = scaled.astype(half_type).astype(jnp.float32)
        col_part.append(jnp.sum(d_inputs * inputs, axis=0, keepdims=True))
        dint[chans] = d_inputs * step_size[h : h + 1]
    blank = jnp.zeros((8 - heads, length), jnp.float32)
    d_step = jnp.concatenate(d_step + [blank], axis=0)
    d_cum = qrow_ref[...] - jnp.concatenate(col_part + [blank], axis=0)
    d_log = scan_lanes(d_cum, True)
    rate = jnp.exp(rate_ref[:, 1:2])
    grad_rate = jnp.sum(d_log * (-step_size * rate), axis=1, keepdims=True)
    d_raw = (d_step - d_log * rate) * jax.nn.sigmoid(raw)
    d_raw = jnp.where(row_ids(8, length) < heads, d_raw, 0.0)
    grad_bias = jnp.sum(d_raw, axis=1, keepdims=True)
    lanes8 = lane_ids(8, 128)
    grads_ref[...] = jnp.where(lanes8 == 0, grad_bias, jnp.where(lanes8 == 1, grad_rate, 0.0))
    qrow[...] = d_raw

    def grad_block(a, carry):
        rows = pl.ds(pl.multiple_of(a * size, size), size)
        d_mixed = dint[:, rows].T + dcomb_ref[rows] * gain_ref[1:2]
        dpx[rows] = d_mixed * silu_slope(pre_ref[rows, :channels].astype(jnp.float32))
        d_basis = jnp.concatenate([dbt[:, rows].T, dcb[rows]], axis=1)
        dpb[rows] = d_basis * silu_slope(pre_ref[rows, channels:].astype(jnp.float32))
        return carry

    lax.fori_loop(0, blocks, grad_block, 0)

    def conv_block(a, carry):
        grad_x, grad_b = carry
        rows = pl.ds(pl.multiple_of(a * size, size), size)
        window = pl.ds(pl.multiple_of(a * size, size), size + 8)
        block = piece_at(a, at)
        keep_window = keep_ref[window]
        keep = keep_window[:size]
        d_wide = dpx[window]
        dproj_ref[block, :, :channels] = conv_back(d_wide, keep_window, taps_ref[...]).astype(
            half_type
        )
        grad_x = grad_x + conv_grads(d_wide[:size], xpad[window], keep)
        d_wide = dpb[window]
        dproj_ref[block, :, channels : channels + states] = conv_back(
            d_wide, keep_window, tapb_ref[...]
        ).astype(half_type)
        grad_b = grad_b + conv_grads(d_wide[:size], bpad[window], keep)
        d_steps = jnp.concatenate([qrow[:, rows], jnp.zeros((120, size), jnp.float32)], axis=0)
        dproj_ref[block, :, channels + states :] = d_steps.T.astype(half_type)
        return grad_x, grad_b

    grad_x, grad_b = lax.fori_loop(
        0,
        blocks,
        conv_block,
        (jnp.zeros((8, channels), jnp.float32), jnp.zeros((8, states), jnp.float32)),
    )
    gradx_ref[...] = grad_x
    gradb_ref[...] = grad_b


def stack_rows(pieces, out_ref):
    begin_at = 0
    for piece in pieces:
        out_ref[begin_at : begin_at + piece.shape[0]] = piece[...]
        begin_at = begin_at + piece.shape[0]


def project_body(count, order_ref, *refs):
    pieces, parts = refs[:4], refs[4 : 4 + count]
    first_ref, proj_ref, weight_ref, small_ref, taps_ref = refs[4 + count :]
    width = weight_ref.shape[0]
    rows = proj_ref.shape[1]
    states = taps_ref.shape[1]
    stack_rows(parts, weight_ref)
    small = weight_ref[:, weight_ref.shape[1] - 128 :].astype(jnp.float32).T[8:16]
    small_ref[...] = small
    gain = small[0:1]
    for p, piece in enumerate(pieces):
        first = (piece[...].astype(jnp.float32) * gain).astype(jnp.bfloat16)
        first_ref[p] = first
    whole = first_ref[...].reshape(4 * rows, width)
    proj_ref[...] = dot_nn(whole, weight_ref[...]).reshape(proj_ref.shape)
    block = width // 8
    aim = lane_ids(block, states) * CONV - row_ids(block, states)
    bits = small.astype(jnp.bfloat16)
    taps = []
    for k in range(CONV):
        picked = [
            jnp.where(aim == order_ref[b] * block - k, 1.0, 0.0).astype(jnp.bfloat16)
            for b in range(8)
        ]
        found = dot_nn(bits, jnp.concatenate(picked, axis=0))
        taps.append(found[2:3])
        if k == 0:
            offset = found[3:4]
    taps.append(offset)
    taps.append(jnp.zeros((8 - len(taps), states), jnp.float32))
    taps_ref[...] = jnp.concatenate(taps, axis=0)


def product_body(_, values_ref, weight_ref, keep_ref, give_ref):
    rows = values_ref.shape[1]
    columns = slice(weight_ref.shape[1] - values_ref.shape[2], None)
    for p in (3, 1, 2, 0):
        result = dot_nt(values_ref[p], weight_ref[:, columns])
        if p < 2:
            keep_ref[p * rows : p * rows + rows] = result
        else:
            give_ref[p * rows - 2 * rows : p * rows - rows] = result.astype(jnp.bfloat16)


def first_back_body(
    _, gate_ref, attn_ref, scan_ref, late_ref, weight_ref, keep_ref, give_ref, token_ref
):
    token_ref[...] = jnp.zeros_like(token_ref)
    rows, channels = gate_ref.shape[1], gate_ref.shape[2]
    wide = channels + 128

    def pair(ref, at):
        return ref[at : at + 2].reshape(2 * rows, ref.shape[2])

    for at, out_ref in ((2, give_ref), (0, keep_ref)):
        attn, scan = pair(attn_ref, at), pair(scan_ref, at)
        result = dot_nt(pair(gate_ref, at), late_ref[:, :channels])
        result = result + dot_nt(attn[:, :128], late_ref[:, channels:wide])
        result = result + dot_nt(attn[:, 128:], weight_ref[:, channels:wide])
        result = result + dot_nt(scan[:, :channels], weight_ref[:, :channels])
        result = result + dot_nt(scan[:, channels:], weight_ref[:, wide:])
        out_ref[...] = result.astype(out_ref.dtype)


def ffn_body(slots, fresh, _, *refs):
    pieces, cots = refs[0:2], refs[2:4]
    if fresh:
        parts, outs = refs[4:-7], refs[-7:]
        weight_ref = outs[6]
        stack_rows(parts, weight_ref)
    else:
        weight_ref, outs = refs[4], refs[-6:]
    second_ref, cot_ref, hidden_ref, dgu_ref, dkeep, dgive = outs[:6]
    hidden_local = hidden_ref.shape[2]
    rows = second_ref.shape[1]
    gate_up_weight = weight_ref.at[:, : 2 * hidden_local]
    down_weight = weight_ref.at[:, 2 * hidden_local :]
    values = jnp.concatenate([piece[...] for piece in pieces], axis=0)
    cot = jnp.concatenate([cots_ref[...] for cots_ref in cots], axis=0)
    gate_up = dot_nn(values, gate_up_weight[...])
    d_hidden = dot_nn(cot, down_weight[...])
    gate, up = gate_up[:, :hidden_local], gate_up[:, hidden_local:]
    sig = jax.nn.sigmoid(gate)
    act = gate * sig
    hidden = (act * up).astype(jnp.bfloat16)
    d_gate = (d_hidden * up * sig * (1.0 + gate * (1.0 - sig))).astype(jnp.bfloat16)
    d_up = (d_hidden * act).astype(jnp.bfloat16)
    d_gate_up = jnp.concatenate([d_gate, d_up], axis=1)
    d_second = dot_nt(d_gate_up, gate_up_weight[...])
    for k, p in enumerate(slots):
        here = slice(k * rows, k * rows + rows)
        second_ref[p] = values[here]
        cot_ref[p] = cot[here]
        hidden_ref[p] = hidden[here]
        dgu_ref[p] = d_gate_up[here]
        if p < 2:
            dkeep[...] = d_second[here]
        else:
            dgive[...] = d_second[here].astype(jnp.bfloat16)


def pick_rows(values, block, rows):
    picked = jnp.zeros((rows, values.shape[1]), values.dtype)
    for g in range(values.shape[0] // rows):
        picked = jnp.where(block == g, values[g * rows : g * rows + rows], picked)
    return picked


def shared_sums_body(conv_rows, at_ref, bc_ref, keyval_ref, *refs):
    *sums, ffn_ref, small_ref, keep_ref, give_ref = refs
    at, place = at_ref[0], at_ref[1]
    rows = keep_ref.shape[0] // 2
    states = bc_ref.shape[1]
    size = 4 * rows
    lanes = lane_ids(size, 128)
    by_row = sum(ref[...] for ref in sums)
    small = jnp.concatenate(
        [
            jnp.zeros((8, states), jnp.float32),
            small_ref[:, :states],
            jnp.zeros((112, states), jnp.float32),
        ],
        axis=0,
    ).T
    spot = row_ids(size, states)
    channel = (place * 4 + spot // rows) * conv_rows + spot % rows
    chosen = (channel == lane_ids(size, states)) & (spot % rows < conv_rows)
    small = jnp.dot(
        jnp.where(chosen, 1.0, 0.0),
        small,
        precision=lax.Precision.HIGHEST,
        preferred_element_type=jnp.float32,
    )
    gains = jnp.where(lanes == 0, by_row, jnp.where(lanes == 1, ffn_ref[...], small))
    values = jnp.concatenate([bc_ref[...], keyval_ref[...], gains], axis=1)
    for k in range(2):
        keep_ref[k * rows : k * rows + rows] = pick_rows(values, at ^ (2 * k), rows)
        give_ref[k * rows : k * rows + rows] = pick_rows(values, at ^ (2 * k + 1), rows)


def shared_total_body(at_ref, keep_ref, near_ref, far_ref, gains_ref, bc_ref, keyval_ref, out_ref):
    rows = far_ref.shape[0]
    states = bc_ref.shape[1]
    lanes = lane_ids(rows, 128)
    chip, other = keep_ref[:rows] + near_ref[:rows], far_ref[...]
    total = chip + other
    bc_ref[...] = total[:, :states]
    heads = [side[:, states : states + 128] for side in (chip, other)]
    low, high = [
        [jnp.where(at_ref[0] < 2, heads[k], heads[1 - k]) for k in range(2)][k] for k in range(2)
    ]
    keyval_ref[:, :128] = jnp.where(lanes < HEAD, low, pltpu.roll(high, HEAD, 1))
    keyval_ref[:, 128:] = jnp.where(lanes < HEAD, pltpu.roll(low, HEAD, 1), high)
    rounded = gains_ref[...].astype(jnp.bfloat16).astype(jnp.float32)
    out_ref[...] = total[:, states + 128 :] / rounded


def pack_body(turned, _, *refs):
    out_ref = refs[-1]
    begin_at = 0
    for index, ref in enumerate(refs[:-1]):
        values = ref[...]
        if index in turned:
            values = values.T
        out_ref[:, begin_at : begin_at + values.shape[1]] = values.astype(jnp.bfloat16)
        begin_at = begin_at + values.shape[1]


def shared_body(at_ref, mine_ref, near_ref, far_ref, cross_ref, step_ref, out_ref):
    at = at_ref[0]
    rows = mine_ref.shape[0]
    lanes = lane_ids(rows, 128)
    states = mine_ref.shape[1] - 384
    for j, ref in enumerate((mine_ref, near_ref, far_ref, cross_ref)):
        values = ref[...].astype(jnp.float32)
        here = pl.ds(pl.multiple_of((at ^ j) * rows, rows), rows)
        key, value = values[:, :128], values[:, 128:256]
        low = jnp.where(lanes < HEAD, key, pltpu.roll(value, HEAD, 1))
        high = jnp.where(lanes < HEAD, pltpu.roll(key, HEAD, 1), value)
        out_ref[here, :128] = jnp.where(at < 2, low, high).astype(jnp.bfloat16)
        out_ref[here, 128 : 128 + states] = values[:, 256 : 256 + states].astype(jnp.bfloat16)
        out_ref[here, 128 + states :] = (
            values[:, 256 + states :] + step_ref[here]
        ).astype(jnp.bfloat16)


def call_kernel(body, outs, scratch, *args, deps=(), micros=2, limit=8, aliases=None, distant=0, sems=0):
    shapes = [jax.ShapeDtypeStruct(shape, kind) for shape, kind in outs]
    count, extra = len(args), len(deps)
    whole = pl.BlockSpec(memory_space=pltpu.VMEM)

    def wrapped(*refs):
        body(*refs[:count], *refs[count + extra :])

    return pl.pallas_call(
        wrapped,
        out_shape=shapes,
        in_specs=[pl.BlockSpec(memory_space=pltpu.SMEM)]
        + [whole] * (count - 1 - distant)
        + [pl.BlockSpec(memory_space=pltpu.HBM)] * distant
        + [whole] * extra,
        out_specs=[whole] * len(shapes),
        scratch_shapes=[pltpu.VMEM(shape, kind) for shape, kind in scratch]
        + ([pltpu.SemaphoreType.DMA((sems,))] if sems else []),
        input_output_aliases=aliases or {},
        compiler_params=pltpu.CompilerParams(vmem_limit_bytes=limit * 2**20),
        cost_estimate=pl.CostEstimate(
            flops=int(micros * 1e9), bytes_accessed=0, transcendentals=0
        ),
    )(*args, *deps)


def sequence_tables(seg_ids):
    length = seg_ids.shape[0]
    places = jnp.arange(length, dtype=jnp.int32)
    starts = jnp.where((places == 0) | (seg_ids != jnp.roll(seg_ids, 1)), places, 0)
    position = places - lax.cummax(starts, axis=0)
    half_dim = HEAD // 2
    frequency = jnp.exp(-jnp.log(ROPE_BASE) * jnp.arange(half_dim, dtype=jnp.float32) / half_dim)
    angles = position.astype(jnp.float32)[:, None] * frequency[None, :]
    cosine, sine = jnp.cos(angles), jnp.sin(angles)
    cosine = jnp.concatenate([cosine] * 4, axis=1)
    sine = jnp.concatenate([-sine, sine] * 2, axis=1)
    masks = [jnp.ones((length,), jnp.float32)]
    for lag in range(1, CONV):
        masks.append(
            ((places >= lag) & (seg_ids == jnp.roll(seg_ids, lag))).astype(jnp.float32)
        )
    masks = jnp.stack(masks + [jnp.zeros((length,), jnp.float32)] * (8 - CONV), axis=1)
    return cosine, sine, jnp.pad(masks, ((0, 8), (0, 0)))


def tap_rows(kernel, offset):
    taps = jnp.concatenate([kernel.T, offset[None, :]], axis=0)
    return jnp.pad(taps, ((0, 8 - taps.shape[0]), (0, 0)))


def shards(
    tokens,
    segment_ids,
    cotangent,
    norm_gain,
    w_z,
    w_x,
    w_bc,
    w_dt,
    conv_x,
    conv_bias_x,
    conv_bc,
    conv_bias_bc,
    dt_bias,
    a_log,
    d_skip,
    mixer_gain,
    w_mixer_out,
    w_query,
    w_keyval,
    w_attn_out,
    ffn_gain,
    w_gate,
    w_up,
    w_down,
):
    half_type = jnp.bfloat16
    full_type = jnp.float32
    rows, width = tokens.shape
    length = segment_ids.shape[0]
    channels = w_z.shape[1]
    heads = w_dt.shape[1]
    hidden_local = w_gate.shape[1]
    states = 2 * STATE
    blocks = length // rows

    row_count = w_bc.shape[0]
    gain_rows = norm_gain.shape[0]
    conv_rows = conv_bc.shape[0]
    at = lax.axis_index("tp").astype(jnp.int32).reshape(1)
    order = feature_order()
    x_at, core_at = place_bits()
    x_core = jnp.zeros((1,), jnp.int32)

    row_half = ((rows, width), half_type)
    row_full = ((rows, width), full_type)
    small = jnp.stack([norm_gain, ffn_gain, conv_bc.reshape(-1), jnp.repeat(conv_bias_bc, CONV)], 1)
    shared_in = jnp.concatenate(
        [w_keyval, w_bc, jnp.pad(small, ((0, 0), (8, 116)))], axis=1
    ).astype(half_type)
    step_wide = jnp.pad(w_dt, ((0, 0), (0, 128 - heads)))
    if staged():
        mine, far, near, cross = gather_pieces(shared_in)
        (shared_shard,) = call_kernel(
            shared_body,
            [((4 * row_count, states + 256), half_type)],
            [],
            at,
            mine,
            near,
            far,
            cross,
            step_wide,
            micros=1,
        )
    else:
        shared_all = lax.all_gather(shared_in, "tp", axis=0, tiled=True)
        key_rows, value_rows = (
            jnp.where(x_at == 0, shared_all[:, k : k + HEAD], shared_all[:, k + HEAD : k + 2 * HEAD])
            for k in (0, 128)
        )
        shared_shard = jnp.concatenate(
            [
                key_rows,
                value_rows,
                shared_all[:, 256 : 256 + states],
                shared_all[:, 256 + states :] + step_wide.astype(half_type),
            ],
            axis=1,
        )
    normed_mine, tok_rows, cot_mine = call_kernel(
        front_body, [row_half, row_half, row_half], [], order, tokens, cotangent, deps=[shared_shard]
    )

    def pack(turned, *shards, deps=()):
        width_all = sum(shard.size for shard in shards) // w_x.shape[0]
        return call_kernel(
            functools.partial(pack_body, turned),
            [((w_x.shape[0], width_all), half_type)],
            [],
            x_core,
            *shards,
            deps=deps,
            micros=1,
        )[0]

    gather = Gather(jnp.concatenate([w_x.astype(half_type), shared_shard], axis=1))
    normed = gather_pieces(normed_mine)
    late_gather = Gather(
        pack((2, 3), w_z, w_query, w_mixer_out, w_attn_out, deps=[shared_shard, normed[2]])
    )
    seg_ids = after(segment_ids.reshape(-1, 128), shared_shard).reshape(-1)
    cosine, sine, keep_masks = sequence_tables(seg_ids)
    seg_col, seg_row = seg_ids[:, None], seg_ids[None, :]
    taps_x = tap_rows(conv_x, conv_bias_x)
    rates = jnp.pad(jnp.stack([dt_bias, a_log], axis=1), ((0, 8 - heads), (0, 126)))
    gains = jnp.stack([mixer_gain, jnp.repeat(d_skip, channels // heads)])
    gains = jnp.pad(gains, ((0, 6), (0, 0)))

    keep_masks = after(keep_masks, shared_shard)
    tables = [cosine, sine, keep_masks, taps_x, rates, gains]
    for k in range(3):
        gather.step(*(tables if k == 2 else []))
        late_step = late_gather.step()
    steps = gather.step()
    late_last = late_gather.step()
    ffn_shard = pack((2,), w_gate, w_up, w_down, deps=[*late_step[:1], *steps[1:]])
    ffn_gather = Gather(ffn_shard)

    parts = gather.parts()
    columns = channels + 128 + states + 128
    first_in, proj, weight, small_rows, taps_bc = call_kernel(
        functools.partial(project_body, len(parts)),
        [
            ((blocks, rows, width), half_type),
            ((blocks, rows, columns), full_type),
            ((width, columns), half_type),
            ((8, width), full_type),
            ((8, states), full_type),
        ],
        [],
        order,
        *normed,
        *parts,
        micros=6,
        limit=12,
    )
    gain_one, gain_two = small_rows[0:1], small_rows[1:2]

    ffn_gather.step(small_rows)
    cot = gather_pieces(after(cot_mine, small_rows))
    scan_out, mixed, raw, pre, basis, inputs, time_rows, time_cols = call_kernel(
        functools.partial(ssd_forward_body, heads),
        [
            ((length, channels), full_type),
            ((length, channels), half_type),
            ((length, channels + states), half_type),
            ((length, channels + states), half_type),
            ((length, states), half_type),
            ((length, channels), half_type),
            ((24, length), full_type),
            ((length, 128), full_type),
        ],
        [
            ((length + 8, channels), full_type),
            ((length + 8, states), full_type),
            ((8, length), full_type),
        ],
        at,
        proj,
        seg_col,
        seg_row,
        keep_masks,
        taps_x,
        taps_bc,
        rates,
        deps=[ffn_shard, late_gather.ready],
        micros=11,
        limit=12,
    )
    parts = late_gather.parts()
    head_half = ((length, 128), half_type)
    head_full = ((length, 128), full_type)
    ffn_gather.step(time_rows, *late_last[1:])
    cat, gate_in, combined, query, keyk, valv, logs, late_weight, out_weight = call_kernel(
        functools.partial(attend_forward_body, len(parts)),
        [
            ((blocks, rows, channels + 128), half_type),
            ((blocks, rows, channels), half_type),
            ((length, channels), half_type),
            head_half,
            head_half,
            head_half,
            head_full,
            ((width, channels + 128), half_type),
            ((width, channels + 128), half_type),
        ],
        [],
        at,
        first_in,
        proj,
        scan_out,
        mixed,
        seg_col,
        seg_row,
        cosine,
        sine,
        gains,
        *parts,
        deps=[ffn_gather.ready, cot[1]],
        micros=9,
        limit=12,
    )

    def row_products(values, weight, deps=()):
        return call_kernel(
            product_body,
            [((2 * rows, width), full_type), ((2 * rows, width), half_type)],
            [],
            x_core,
            values,
            weight,
            deps=deps,
        )

    keep, give = row_products(cat, out_weight, deps=ffn_gather.arrivals)
    ffn_gather.step(query)
    mix_terms = reduce_pieces(keep, give, ffn_gather.ready)
    ffn_gather.step()
    after_mix, second_mine = call_kernel(
        mixed_body,
        [row_full, row_half],
        [],
        order,
        tok_rows,
        *mix_terms[:3],
        gain_two,
        deps=[ffn_gather.ready],
    )
    second_far = flip(second_mine, "tp", 2)
    second_near = flip(second_mine, "tp", 1)

    parts = ffn_gather.parts()
    filled = [
        ((blocks, rows, width), half_type),
        ((blocks, rows, width), half_type),
        ((blocks, rows, hidden_local), half_type),
        ((blocks, rows, 2 * hidden_local), half_type),
    ]
    sums = [row_full, row_half]
    *filled_in, d_keep, d_give, ffn_weight = call_kernel(
        functools.partial(ffn_body, (0, 2), True),
        filled + sums + [((width, 3 * hidden_local), half_type)],
        [],
        x_core,
        second_mine,
        second_near,
        cot[0],
        cot[2],
        *parts,
        micros=5,
        limit=12,
    )
    *filled_in, d_keep_x, d_give_x = call_kernel(
        functools.partial(ffn_body, (1, 3), False),
        filled + sums,
        [],
        x_core,
        second_far,
        flip(after(second_far, d_give), "tp", 1),
        cot[1],
        cot[3],
        ffn_weight,
        *filled_in,
        micros=5,
        limit=12,
        aliases={6: 0, 7: 1, 8: 2, 9: 3},
    )
    second_in, cot_all, hidden, d_gate_up = (
        array.reshape(length, array.shape[2]) for array in filled_in
    )
    near = flip(d_give, "tp", 1)
    passed = d_keep_x + flip(d_give_x, "tp", 1).astype(full_type)
    d_second = d_keep, near, flip(passed.astype(half_type), "tp", 2)
    ffn_scatter = Scatter(
        [
            contract_rows(second_in, d_gate_up).astype(half_type),
            contract_rows(cot_all, hidden).astype(half_type),
        ],
    )

    d_after, d_mix = call_kernel(
        after_back_body,
        [row_full, row_half],
        [],
        order,
        after_mix,
        cot_mine,
        *d_second,
        gain_two,
        deps=ffn_scatter.arrivals,
    )
    ffn_scatter.step(3)
    d_mix_all = gather_pieces(d_mix, *ffn_scatter.arrivals)

    ffn_scatter.step(2)
    d_gate, d_comb, sums_gain, d_mix_whole, d_att = call_kernel(
        gate_backward_body,
        [
            ((blocks, rows, channels), half_type),
            ((length, channels), full_type),
            ((8, channels), full_type),
            ((blocks, rows, width), half_type),
            head_half,
        ],
        [],
        at,
        gate_in,
        *d_mix_all,
        out_weight,
        combined,
        gains,
        deps=[ffn_scatter.ready],
        micros=4,
    )
    (d_attn,) = call_kernel(
        attend_backward_body,
        [((blocks, rows, 256), half_type)],
        [((length, 128), full_type), ((length, 128), full_type)],
        at,
        d_att,
        seg_col,
        seg_row,
        cosine,
        sine,
        query,
        keyk,
        valv,
        logs,
        micros=7,
    )
    out_terms = reduce_pieces(*row_products(filled_in[2], ffn_weight, deps=[sums_gain]))
    first_rows = first_in.reshape(length, width)
    gate_scatter = Scatter(
        [
            contract_rows(first_rows, d_gate.reshape(length, channels)).astype(half_type),
            contract_rows(first_rows, d_attn.reshape(length, 256)).astype(half_type),
            contract_rows(
                d_mix_whole.reshape(length, width), cat.reshape(length, channels + 128)
            ).astype(half_type),
        ],
    )
    ffn_scatter.step(1, d_attn)
    d_inputs_t, d_basis_b, d_basis_c, q_rows, mixed_t, sums_skip = call_kernel(
        functools.partial(ssd_backward_body, heads),
        [
            ((channels, length), full_type),
            ((STATE, length), full_type),
            ((length, STATE), full_type),
            ((8, length), full_type),
            ((channels, length), full_type),
            ((8, channels), full_type),
        ],
        [
            ((length, channels), half_type),
            ((channels, length), half_type),
            ((STATE, length), half_type),
        ],
        at,
        d_comb,
        scan_out,
        seg_col,
        seg_row,
        mixed,
        basis,
        inputs,
        time_rows,
        time_cols,
        deps=[ffn_scatter.ready, gate_scatter.ready, out_terms[3]],
        micros=12,
        limit=12,
    )
    gate_scatter.step(3, sums_skip)
    d_scan, sums_x, sums_bc, sums_rate = call_kernel(
        functools.partial(conv_backward_body, heads),
        [
            ((blocks, rows, channels + states + 128), half_type),
            ((8, channels), full_type),
            ((8, states), full_type),
            ((8, 128), full_type),
        ],
        [
            ((length + 8, channels), full_type),
            ((length + 8, states), full_type),
            ((length + 8, channels), full_type),
            ((length + 8, states), full_type),
            ((channels, length), full_type),
            ((8, length), full_type),
        ],
        at,
        raw,
        d_comb,
        keep_masks,
        taps_x,
        taps_bc,
        rates,
        gains,
        pre,
        time_rows,
        d_inputs_t,
        d_basis_b,
        d_basis_c,
        q_rows,
        mixed_t,
        deps=[gate_scatter.ready, out_terms[2], *ffn_scatter.arrivals],
        micros=7,
        limit=14,
    )
    smalls = join_columns([sums_bc, sums_x, sums_gain, sums_skip, sums_rate])
    scan_scatter = Scatter(
        [
            contract_rows(
                first_rows, d_scan.reshape(length, channels + states + 128)
            ).astype(half_type)
        ],
        extra=smalls,
    )
    keep, give, token = call_kernel(
        first_back_body,
        [
            ((2 * rows, width), full_type),
            ((2 * rows, width), half_type),
            ((8, 128), full_type),
        ],
        [],
        x_core,
        d_gate,
        d_attn,
        d_scan,
        late_weight,
        weight,
        deps=[*scan_scatter.arrivals, *gate_scatter.arrivals],
        micros=4,
    )
    d_first = reduce_pieces(keep, give)
    scan_scatter.step(3, token)
    gate_scatter.step(2, d_first[3])
    scan_scatter.step(2, d_first[3])
    gate_scatter.step(1)
    scan_scatter.step(1, d_first[2])
    scan_ready = scan_scatter.ready
    sum_gate, sum_up, sum_down, ffn_rows = ffn_scatter.total(
        (
            (0, hidden_local, False),
            (hidden_local, hidden_local, False),
            (2 * hidden_local, hidden_local, True),
        ),
        ((0, 0, hidden_local), (hidden_local, 0, hidden_local)),
        w_gate,
        w_up,
        deps=[d_first[2]],
    )
    (grad_tokens,) = call_kernel(
        token_back_body,
        [row_full],
        [],
        order,
        tok_rows,
        d_after,
        *d_first[:3],
        gain_one,
        deps=[scan_ready],
    )

    sum_z, sum_mixer_out, sum_attn_out, sum_query, sum_keyval, gate_rows = gate_scatter.total(
        (
            (0, channels, False),
            (channels + 256, channels, True),
            (2 * channels + 256, 128, True),
            (channels, 128, False),
            (channels + 128, 128, False),
        ),
        ((0, 0, channels), (channels, 0, 128), (channels + 128, 0, 128)),
        w_z,
        w_query,
        shared_shard,
    )
    sum_x, sum_bc, sum_step, scan_rows, flat = scan_scatter.total(
        ((0, channels, False), (channels, states, False), (channels + states, heads, False)),
        ((0, 0, channels), (channels, 128, states), (channels + states, 0, heads)),
        w_x,
        shared_shard,
        w_dt,
    )
    keep, give = call_kernel(
        functools.partial(shared_sums_body, conv_rows),
        [((2 * row_count, states + 256), full_type)] * 2,
        [],
        jnp.concatenate([at, lax.axis_index("fsdp").astype(jnp.int32).reshape(1)]),
        sum_bc,
        sum_keyval,
        gate_rows,
        scan_rows,
        ffn_rows,
        flat,
        deps=[grad_tokens],
        micros=1,
    )
    near = flip(give, "tp", 1)
    far = flip(keep[row_count:] + near[row_count:], "tp", 2)
    grad_bc, grad_keyval, gain_sums = call_kernel(
        shared_total_body,
        [
            ((row_count, states), full_type),
            ((row_count, 256), full_type),
            ((row_count, 128), full_type),
        ],
        [],
        at,
        keep,
        near,
        far,
        jnp.pad(jnp.stack([norm_gain, ffn_gain], 1), ((0, 0), (0, 126)), constant_values=1.0),
        micros=1,
    )
    sum_gain_one, sum_gain_two = gain_sums[:, 0], gain_sums[:, 1]
    sum_conv, sum_bias = gain_sums[:conv_rows, 8:12], gain_sums[:conv_rows, 12]

    (layer_out,) = call_kernel(
        output_body,
        [row_half],
        [],
        order,
        after_mix,
        *out_terms[:3],
        deps=[d_first[3]],
    )
    x_sums = flat[:, states : states + channels]
    mixer_sums = flat[0, states + channels : states + 2 * channels]
    skip_sums = flat[0, states + 2 * channels : states + 3 * channels]
    rate_sums = flat[:, states + 3 * channels :]
    return (
        layer_out,
        grad_tokens,
        sum_gain_one,
        sum_z,
        sum_x,
        grad_bc,
        sum_step,
        x_sums[:4].T,
        x_sums[4],
        sum_conv,
        sum_bias,
        rate_sums[:heads, 0],
        rate_sums[:heads, 1],
        skip_sums.reshape(heads, channels // heads).sum(axis=1),
        mixer_sums,
        sum_mixer_out,
        sum_query,
        grad_keyval,
        sum_attn_out,
        sum_gain_two,
        sum_gate,
        sum_up,
        sum_down,
    )


def solution(mesh):
    placed = (
        P(("fsdp", "tp"), None),
        P("fsdp"),
        P(("fsdp", "tp"), None),
        P(("fsdp", "tp")),
        P("fsdp", "tp"),
        P("fsdp", "tp"),
        P(("fsdp", "tp"), None),
        P("fsdp", "tp"),
        P("tp", None),
        P("tp"),
        P(("fsdp", "tp"), None),
        P(("fsdp", "tp")),
        P("tp"),
        P("tp"),
        P("tp"),
        P("tp"),
        P("tp", "fsdp"),
        P("fsdp", "tp"),
        P(("fsdp", "tp"), None),
        P("tp", "fsdp"),
        P(("fsdp", "tp")),
        P("fsdp", "tp"),
        P("fsdp", "tp"),
        P("tp", "fsdp"),
    )
    return jax.shard_map(
        shards,
        mesh=mesh,
        in_specs=placed,
        out_specs=(
            P(("fsdp", "tp"), None),
            P(("fsdp", "tp"), None),
            P(("fsdp", "tp")),
            P("fsdp", "tp"),
            P("fsdp", "tp"),
            P(("fsdp", "tp"), None),
            P("fsdp", "tp"),
            P("tp", None),
            P("tp"),
            P(("fsdp", "tp"), None),
            P(("fsdp", "tp")),
            P("tp"),
            P("tp"),
            P("tp"),
            P("tp"),
            P("tp", "fsdp"),
            P("fsdp", "tp"),
            P(("fsdp", "tp"), None),
            P("tp", "fsdp"),
            P(("fsdp", "tp")),
            P("fsdp", "tp"),
            P("fsdp", "tp"),
            P("tp", "fsdp"),
        ),
        check_vma=False,
    )
```
